128 devices in a mesh: frame: 8 (over y, z_lo), patch: 16 (over z_hi, x, core).
Axes of the slice: x: 4, y: 4, z: 4 (z_hi: 2, z_lo: 2; z = z_hi * 2 + z_lo), core: 2. Of those that a mesh axis runs over, the one named last changes fastest.
Arguments:
- tokens: bfloat16 [32, 2048, 1152], P('frame', 'patch'), may hold values from -6 to 6
- w_qkv_s: bfloat16 [1152, 3456], replicated, may hold values from -0.70710678 to 0.70710678
- w_out_s: bfloat16 [1152, 1152], replicated, may hold values from -0.1875 to 0.1875
- mod_s: float32 [3, 1152], replicated, may hold values from -2 to 2, as said below
- w_qkv_t: bfloat16 [1152, 3456], replicated, may hold values from -0.70710678 to 0.70710678
- w_out_t: bfloat16 [1152, 1152], replicated, may hold values from -0.1875 to 0.1875
- mod_t: float32 [3, 1152], replicated, may hold values from -2 to 2, as said below
Outputs:
- blocked: bfloat16 [32, 2048, 1152], P('frame', 'patch')
The draws below stay inside these ranges and needn't reach their ends.
Inputs may be any that keep to these rules, and one draw needn't show every extreme that they name: `mod_s`: row 1 lies in -0.5 to 0.5, row 2 in 0.5 to 1.5. `mod_t`: row 1 lies in -0.5 to 0.5, row 2 in 0.5 to 1.5.
All inputs are finite; a program needn't handle non-finite values.
Results may differ from the reference program's by a relative error of at most 0.017.
Values may be sent and summed in bfloat16 or wider, within the bound.
A program may use at most 128 MiB of HBM per device.

```python
import jax
import jax.numpy as jnp
from jax import lax

HEADS = 16
HD = 72
D = 1152
FRAMES = 32
PATCHES = 2048


def qkv_columns(key, low, high):
    key_base, key_scale = jax.random.split(key)
    base = jnp.clip(jax.random.normal(key_base, (D, 3, HEADS, HD), jnp.float32), -4.0, 4.0) * D ** (-0.5)
    factor = jnp.exp(jax.random.uniform(key_scale, (HEADS,), jnp.float32, jnp.log(low), jnp.log(high)))
    query = base[:, 0] * factor[None, :, None]
    keys = base[:, 1] * factor[None, :, None]
    stacked = jnp.stack([query, keys, base[:, 2]], axis=1)
    return stacked.reshape(D, 3 * D).astype(jnp.bfloat16)


def modulation(key, spread):
    key_shift, key_scale, key_gate = jax.random.split(key, 3)
    shift = jnp.clip(jax.random.normal(key_shift, (D,), jnp.float32) * spread, -2.0, 2.0)
    scale = jax.random.uniform(key_scale, (D,), jnp.float32, -0.5, 0.5)
    gate = jax.random.uniform(key_gate, (D,), jnp.float32, 0.5, 1.5)
    return jnp.stack([shift, scale, gate], axis=0)


def draw_w_qkv_s(key, part):
    key = jax.random.fold_in(key, 11)
    return qkv_columns(key, 1.0, 3.0)


def draw_w_qkv_t(key, part):
    key = jax.random.fold_in(key, 23)
    return qkv_columns(key, 1.0, 3.0)


def draw_mod_s(key, part):
    key = jax.random.fold_in(key, 37)
    return modulation(key, 0.5)


def draw_mod_t(key, part):
    key = jax.random.fold_in(key, 41)
    return modulation(key, 0.5)


def shard_levels(stream_key, dims, cuts, smallest, largest):
    level = 1.0
    for dim, parts in cuts:
        draws = jax.random.uniform(jax.random.fold_in(jax.random.fold_in(stream_key, 6), dim), (parts,), jnp.float32, smallest / len(cuts), largest / len(cuts))
        level = level * jnp.repeat(jnp.exp(draws), dims[dim] // parts).reshape((-1,) + (1,) * (len(dims) - 1 - dim))
    return level


def normal_values(rng, extent, scale, bound, cuts=(), held_as=jnp.bfloat16):
    loudness = shard_levels(rng, extent, cuts, -0.22, 0.18) if cuts else 1.0
    array = jax.random.normal(rng, extent, jnp.float32) * scale * loudness
    return jnp.minimum(jnp.maximum(array, -bound), bound).astype(held_as)


def setup_inputs(seed: int = 0) -> dict:
    key_of = jax.random.split(jax.random.key(seed), 8)
    return {
        "tokens": normal_values(key_of[0], (FRAMES, PATCHES, D), 1.0, 6.0, ((0, 8), (1, 16))),
        "w_qkv_s": draw_w_qkv_s(jax.random.fold_in(key_of[7], 71), 0),
        "w_out_s": normal_values(key_of[2], (D, D), D ** -0.5, 0.1875),
        "mod_s": draw_mod_s(jax.random.fold_in(key_of[7], 71), 0),
        "w_qkv_t": draw_w_qkv_t(jax.random.fold_in(key_of[7], 71), 0),
        "w_out_t": normal_values(key_of[5], (D, D), D ** -0.5, 0.1875),
        "mod_t": draw_mod_t(jax.random.fold_in(key_of[7], 71), 0),
    }


def layer_norm(values):
    mean = lax.optimization_barrier(jnp.mean(values, axis=-1, keepdims=True))
    centered = values - mean
    var = lax.optimization_barrier(jnp.mean(centered * centered, axis=-1, keepdims=True))
    return centered * lax.rsqrt(var + 1e-06)

def modulate(values, mod_rows):
    return layer_norm(values.astype(jnp.float32)) * (1.0 + mod_rows[1]) + mod_rows[0]

def project_qkv(values, weight, mod_rows):
    frames, patches = (values.shape[0], values.shape[1])
    normed = modulate(values, mod_rows).astype(jnp.bfloat16).reshape(frames * patches, D)
    mixed = jnp.dot(normed, weight, preferred_element_type=jnp.float32).astype(jnp.bfloat16)
    return mixed.reshape(frames, patches, 3, HEADS, HD)

def spatial_frame(qkv_frame):
    query = qkv_frame[:, 0].astype(jnp.float32)
    keys = qkv_frame[:, 1].astype(jnp.float32)
    values = qkv_frame[:, 2].astype(jnp.float32)
    scores = jnp.einsum('qhd,khd->hqk', query, keys) * HD ** (-0.5)
    top = lax.optimization_barrier(jnp.max(scores, axis=-1, keepdims=True))
    expo = jnp.exp(scores - top)
    probs = (expo / lax.optimization_barrier(jnp.sum(expo, axis=-1, keepdims=True))).astype(jnp.bfloat16)
    return jnp.einsum('hqk,khd->qhd', probs.astype(jnp.float32), values).astype(jnp.bfloat16)

def temporal_all(qkv):
    query = qkv[:, :, 0].astype(jnp.float32)
    keys = qkv[:, :, 1].astype(jnp.float32)
    values = qkv[:, :, 2].astype(jnp.float32)
    scores = jnp.einsum('fphd,gphd->phfg', query, keys) * HD ** (-0.5)
    top = lax.optimization_barrier(jnp.max(scores, axis=-1, keepdims=True))
    expo = jnp.exp(scores - top)
    probs = (expo / lax.optimization_barrier(jnp.sum(expo, axis=-1, keepdims=True))).astype(jnp.bfloat16)
    return jnp.einsum('phfg,gphd->fphd', probs.astype(jnp.float32), values).astype(jnp.bfloat16)

def finish(values, attended, weight, mod_rows):
    frames, patches = (values.shape[0], values.shape[1])
    proj = jnp.dot(attended.reshape(frames * patches, D), weight, preferred_element_type=jnp.float32)
    proj = proj.reshape(frames, patches, D)
    return (values.astype(jnp.float32) + mod_rows[2] * proj).astype(jnp.bfloat16)

def reference(tokens, w_qkv_s, w_out_s, mod_s, w_qkv_t, w_out_t, mod_t):
    qkv = project_qkv(tokens, w_qkv_s, mod_s)
    attended = lax.map(spatial_frame, qkv)
    middle = finish(tokens, attended, w_out_s, mod_s)
    qkv_time = project_qkv(middle, w_qkv_t, mod_t)
    attended_time = temporal_all(qkv_time)
    return finish(middle, attended_time, w_out_t, mod_t)
```

```python
import functools

import jax
import jax.numpy as jnp
from jax import lax
from jax.experimental import pallas as pl
from jax.experimental.pallas import tpu as pltpu
from jax.sharding import PartitionSpec as P

HEADS = 16
HD = 72
D = 1152
WIN = 384
ROWS = 2048
QT = 256
SCALE = HD ** (-0.5) * 1.4426950408889634
MESH = pl.DeviceIdType.MESH
VMEM = pl.BlockSpec(memory_space=pltpu.VMEM)
ANY = pl.BlockSpec(memory_space=pl.ANY)
BF = jnp.bfloat16
F32 = jnp.float32


def params(collective_id=None):
    return pltpu.CompilerParams(
        collective_id=collective_id,
        has_side_effects=collective_id is not None,
        vmem_limit_bytes=56 * 2**20,
    )


def remote(src, dst, send_sem, recv_sem, device):
    return pltpu.make_async_remote_copy(
        src_ref=src, dst_ref=dst, send_sem=send_sem, recv_sem=recv_sem, device_id=device, device_id_type=MESH
    )


def meet(devices):
    barrier = pltpu.get_barrier_semaphore()
    for device in devices:
        pl.semaphore_signal(barrier, inc=1, device_id=device, device_id_type=MESH)
    pl.semaphore_wait(barrier, len(devices))


def modulate(values, mod_ref):
    mean = jnp.mean(values, axis=-1, keepdims=True)
    centered = values - mean
    var = jnp.mean(centered * centered, axis=-1, keepdims=True)
    return (centered * lax.rsqrt(var + 1e-06) * (1.0 + mod_ref[1:2, :]) + mod_ref[0:1, :]).astype(BF)


def place():
    frame, patch = lax.axis_index("frame"), lax.axis_index("patch")
    return frame, patch, patch // 8, (patch // 2) % 4, patch % 2


def rows16(index):
    return pl.ds(pl.multiple_of(index * 16, 16), 16)


def gather_kernel(tok, mod, full, tok_t, hs, zbuf, xs, xr, zs, zr, ls, ts, tr):
    frame, patch, zh, x, core = place()
    zpatch = (1 - zh) * 8 + x * 2 + core
    sibling = (frame, patch + 1 - 2 * core)
    zdev = (frame, zpatch)
    xpos = [(x + dx) % 4 for dx in (1, 3, 2)]
    xdev = [(frame, zh * 8 + p * 2 + core) for p in xpos]
    others = [((frame + d) % 8, patch) for d in range(1, 8)]
    meet([sibling, zdev] + xdev + others)

    def norm(f):
        hs[f] = modulate(tok[f].astype(F32), mod)

    copies = []
    for j in range(2):
        norm(2 * (1 - zh) + j)
        copies.append(remote(hs.at[2 * (1 - zh) + j], zbuf.at[j], zs.at[j], zr.at[j], zdev))
        copies[-1].start()
    for j in range(2):
        norm(2 * zh + j)
    for i, device in enumerate(xdev):
        copies.append(remote(hs.at[2 * zh + xpos[i] // 2], full.at[patch], xs.at[i], xr.at[patch], device))
        copies[-1].start()
    own = pltpu.make_async_copy(hs.at[2 * zh + x // 2], full.at[patch], ls.at[0])
    own.start()
    for i, device in enumerate(others):
        copies.append(remote(tok.at[:, rows16(device[0]), :], tok_t.at[frame], ts.at[i], tr.at[i], device))
        copies[-1].start()
    mine = pltpu.make_async_copy(tok.at[:, rows16(frame), :], tok_t.at[frame], ls.at[1])
    mine.start()
    own.wait()

    def relay(source, slot):
        copies.append(remote(full.at[source], full.at[source], xs.at[slot], xr.at[source], sibling))
        copies[-1].start()

    def arrived(source, device):
        remote(full.at[source], full.at[source], xs.at[0], xr.at[source], device).wait_recv()

    relay(patch, 6)
    for j in range(2):
        remote(zbuf.at[j], zbuf.at[j], zs.at[j], zr.at[j], zdev).wait_recv()
    for i, device in enumerate(xdev):
        copies.append(remote(zbuf.at[xpos[i] // 2], full.at[zpatch], xs.at[3 + i], xr.at[zpatch], device))
        copies[-1].start()
    own = pltpu.make_async_copy(zbuf.at[x // 2], full.at[zpatch], ls.at[0])
    own.start()
    own.wait()
    relay(zpatch, 7)
    for i, device in enumerate(xdev):
        arrived(device[1], device)
        relay(device[1], 8 + i)
    for i, device in enumerate(xdev):
        source = (1 - zh) * 8 + xpos[i] * 2 + core
        arrived(source, device)
        relay(source, 11 + i)
    for i in range(16):
        source = (i // 2) * 2 + 1 - core
        if i % 2 == 0:
            arrived(source, sibling)
    mine.wait()
    for i, device in enumerate(others):
        remote(tok_t.at[frame], tok_t.at[frame], ts.at[i], tr.at[6 - i], device).wait_recv()
    for copy in copies:
        copy.wait_send()


def gather(tokens, mod):
    return pl.pallas_call(
        gather_kernel,
        name="gather",
        out_shape=[jax.ShapeDtypeStruct((16, 128, D), BF), jax.ShapeDtypeStruct((8, 4, 16, D), BF)],
        in_specs=[VMEM, VMEM],
        out_specs=[VMEM, VMEM],
        scratch_shapes=[
            pltpu.VMEM((4, 128, D), BF),
            pltpu.VMEM((2, 128, D), BF),
            pltpu.SemaphoreType.DMA((14,)),
            pltpu.SemaphoreType.DMA((16,)),
            pltpu.SemaphoreType.DMA((2,)),
            pltpu.SemaphoreType.DMA((2,)),
            pltpu.SemaphoreType.DMA((2,)),
            pltpu.SemaphoreType.DMA((7,)),
            pltpu.SemaphoreType.DMA((7,)),
        ],
        compiler_params=params(1),
    )(tokens, mod)


ONE_LANE = (255, 255, 255, 0)


def head_lanes(shape, head, group):
    lane = lax.broadcasted_iota(jnp.int32, shape, 1) + (head // 2) * 128
    low = 32 * group + HD * head
    return (lane >= low) & (lane < low + HD)


def project(h, w, qkv, vals, chunk, group):
    rows = pl.ds(pl.multiple_of(chunk * QT, QT), QT)
    for part in range(3):
        cols = slice(part * WIN, (part + 1) * WIN)
        acc = jnp.dot(h, w[:, cols], preferred_element_type=F32)
        if part == 0:
            acc = acc * SCALE
        if part < 2:
            qkv[rows, cols] = acc.astype(BF)
        else:
            for head in range(4):
                base = (head // 2) * 128
                keep = head_lanes((QT, 256), head, group)
                lane = lax.broadcasted_iota(jnp.int32, (QT, 256), 1)
                one = jnp.where(lane == ONE_LANE[head], 1.0, 0.0)
                vals[head, rows, :] = jnp.where(keep, acc[:, base : base + 256], one).astype(BF)


def attend(qkv, vals, out, tile, group):
    rows = pl.ds(pl.multiple_of(tile * QT, QT), QT)
    halves = []
    for head in range(4):
        base = (head // 2) * 128
        keep = head_lanes((QT, 256), head, group)
        query = jnp.where(keep, qkv[rows, base : base + 256], jnp.zeros((), BF))
        keys = qkv[:, WIN + base : WIN + base + 256]
        scores = lax.dot_general(query, keys, (((1,), (1,)), ((), ())), preferred_element_type=F32)
        top = jnp.max(scores, axis=-1, keepdims=True)
        probs = jnp.exp2(scores - top).astype(BF)
        mixed = jnp.dot(probs, vals[head], preferred_element_type=F32)
        lane = ONE_LANE[head]
        halves.append(jnp.where(keep, mixed / mixed[:, lane : lane + 1], 0.0))
    first, second = halves[0] + halves[1], halves[2] + halves[3]
    out[rows, 0:128] = first[:, :128].astype(BF)
    out[rows, 128:256] = (first[:, 128:] + second[:, :128]).astype(BF)
    out[rows, 256:384] = second[:, 128:].astype(BF)


def load_window(w, wbuf, sems, group):
    copies = []
    for part in range(3):
        cols = pl.ds(pl.multiple_of(part * D + 256 * group, 128), WIN)
        copies.append(pltpu.make_async_copy(w.at[:, cols], wbuf.at[:, pl.ds(part * WIN, WIN)], sems.at[part]))
        copies[-1].start()
    return copies


def spatial_kernel(full, w, out, wbuf, qkv, vals, sems):
    frame, patch, zh, x, core = place()
    group = (x % 2) * 2 + core
    for copy in load_window(w, wbuf, sems, group):
        copy.wait()

    def proj(i, _):
        h = full[pl.ds(i * 2, 2)].reshape(QT, D)
        project(h, wbuf, qkv, vals, i, group)
        return 0

    lax.fori_loop(0, ROWS // QT, proj, 0)

    def att(i, _):
        attend(qkv, vals, out, i, group)
        return 0

    lax.fori_loop(0, ROWS // QT, att, 0)


def spatial(full, w):
    return pl.pallas_call(
        spatial_kernel,
        name="spatial",
        out_shape=jax.ShapeDtypeStruct((ROWS, WIN), BF),
        in_specs=[VMEM, ANY],
        out_specs=VMEM,
        scratch_shapes=[
            pltpu.VMEM((D, 3 * WIN), BF),
            pltpu.VMEM((ROWS, 2 * WIN), BF),
            pltpu.VMEM((4, ROWS, 256), BF),
            pltpu.SemaphoreType.DMA((3,)),
        ],
        compiler_params=params(),
    )(full, w)


def meet_all(frame, patch):
    barrier = pltpu.get_barrier_semaphore()

    def signal(i, _):
        device = ((frame + i // 16) % 8, (patch + i % 16) % 16)
        pl.semaphore_signal(barrier, inc=1, device_id=device, device_id_type=MESH)
        return 0

    lax.fori_loop(1, 128, signal, 0)
    pl.semaphore_wait(barrier, 127)


def spread_kernel(att, att_t, send, recv):
    frame, patch, zh, x, core = place()
    group = (x % 2) * 2 + core
    at = frame * 4 + zh * 2 + x // 2
    meet_all(frame, patch)

    def go(i, _):
        i = (i * 51) % 128
        f, p = (frame + i // 16) % 8, (patch + i % 16) % 16
        remote(att.at[rows16(p * 8 + f), :], att_t.at[group, at], send, recv, (f, p)).start()
        return 0

    lax.fori_loop(1, 128, go, 0)
    pltpu.make_async_copy(att.at[rows16(patch * 8 + frame), :], att_t.at[group, at], recv).start()
    pltpu.make_async_copy(att_t, att_t, recv).wait()
    pltpu.make_async_copy(att.at[pl.ds(0, 2032), :], att.at[pl.ds(0, 2032), :], send).wait()


def spread(att):
    return pl.pallas_call(
        spread_kernel,
        name="spread",
        out_shape=jax.ShapeDtypeStruct((4, 32, 16, WIN), BF),
        in_specs=[VMEM],
        out_specs=VMEM,
        scratch_shapes=[pltpu.SemaphoreType.DMA, pltpu.SemaphoreType.DMA],
        compiler_params=params(2),
    )(att)


def swap_rows(forward):
    row = lax.broadcasted_iota(jnp.int32, (512, 512), 0)
    col = lax.broadcasted_iota(jnp.int32, (512, 512), 1)
    if forward:
        return jnp.where(col == (row % 32) * 16 + row // 32, 1.0, 0.0).astype(BF)
    return jnp.where(col == (row % 16) * 32 + row // 16, 1.0, 0.0).astype(BF)


def temporal_kernel(
    att_t, tok, w_out_s, mod_s, w_qkv, w_out, mod, out, wo_s, wq, wo, att, mid, hp, qkv, mixed_all, sems
):
    loads = [
        pltpu.make_async_copy(src, dst, sems.at[i])
        for i, (src, dst) in enumerate([(w_out_s, wo_s), (w_qkv, wq), (w_out, wo)])
    ]
    for load in loads:
        load.start()
    for tile in range(9):
        cols = slice(tile * 128, tile * 128 + 128)
        group, rest = min(tile // 2, 3), tile - 2 * min(tile // 2, 3)
        part = att_t[group, :, :, rest * 128 : rest * 128 + 128].reshape(512, 128)
        if rest == 0 and group > 0:
            part = part + att_t[group - 1, :, :, 256:384].reshape(512, 128)
        att[:, cols] = part
    loads[0].wait()

    def finish_mid(i, _):
        rows = pl.ds(pl.multiple_of(i * 128, 128), 128)
        proj = jnp.dot(att[rows, :], wo_s[...], preferred_element_type=F32)
        values = (tok[rows, :].astype(F32) + mod_s[2:3, :] * proj).astype(BF)
        mid[rows, :] = values
        att[rows, :] = modulate(values.astype(F32), mod)
        return 0

    lax.fori_loop(0, 4, finish_mid, 0)
    hp[...] = jnp.dot(swap_rows(True), att[...], preferred_element_type=F32).astype(BF)
    loads[1].wait()
    for part in range(9):
        cols = slice(part * WIN, (part + 1) * WIN)
        acc = jnp.dot(hp[...], wq[:, cols], preferred_element_type=F32)
        if part < 3:
            acc = acc * SCALE
        qkv[:, cols] = acc.astype(BF)

    row = lax.broadcasted_iota(jnp.int32, (128, 128), 0)
    col = lax.broadcasted_iota(jnp.int32, (128, 128), 1)
    same = row // 32 == col // 32
    lane = lax.broadcasted_iota(jnp.int32, (128, 256), 1)

    def group(i, _):
        rows = pl.ds(pl.multiple_of(i * 128, 128), 128)
        for head in range(HEADS):
            base = min(head * HD // 128, 7) * 128
            low = head * HD - base
            keep = (lane >= low) & (lane < low + HD)
            query = jnp.where(keep, qkv[rows, base : base + 256], jnp.zeros((), BF))
            keys = qkv[rows, D + base : D + base + 256]
            scores = lax.dot_general(query, keys, (((1,), (1,)), ((), ())), preferred_element_type=F32)
            scores = jnp.where(same, scores, -1e30)
            top = jnp.max(scores, axis=-1, keepdims=True)
            expo = jnp.exp2(scores - top)
            probs = (expo / jnp.sum(expo, axis=-1, keepdims=True)).astype(BF)
            mixed = jnp.dot(probs, qkv[rows, 2 * D + base : 2 * D + base + 256], preferred_element_type=F32)
            mixed = mixed.astype(BF)
            if low == 0:
                mixed_all[rows, base : base + 256] = mixed
            else:
                mixed_all[rows, base : base + 256] = jnp.where(keep, mixed, mixed_all[rows, base : base + 256])
        return 0

    lax.fori_loop(0, 4, group, 0)
    att[...] = jnp.dot(swap_rows(False), mixed_all[...], preferred_element_type=F32).astype(BF)
    loads[2].wait()

    def finish(i, _):
        rows = pl.ds(pl.multiple_of(i * 128, 128), 128)
        proj = jnp.dot(att[rows, :], wo[...], preferred_element_type=F32)
        out[rows, :] = (mid[rows, :].astype(F32) + mod[2:3, :] * proj).astype(BF)
        return 0

    lax.fori_loop(0, 4, finish, 0)


def temporal(att_t, tok_t, w_out_s, mod_s, w_qkv, w_out, mod):
    return pl.pallas_call(
        temporal_kernel,
        name="temporal",
        out_shape=jax.ShapeDtypeStruct((512, D), BF),
        in_specs=[VMEM, VMEM, ANY, VMEM, ANY, ANY, VMEM],
        out_specs=VMEM,
        scratch_shapes=[
            pltpu.VMEM((D, D), BF),
            pltpu.VMEM((D, 3 * D), BF),
            pltpu.VMEM((D, D), BF),
            pltpu.VMEM((512, D), BF),
            pltpu.VMEM((512, D), BF),
            pltpu.VMEM((512, D), BF),
            pltpu.VMEM((512, 3 * D), BF),
            pltpu.VMEM((512, D), BF),
            pltpu.SemaphoreType.DMA((3,)),
        ],
        compiler_params=params(),
    )(att_t, tok_t, w_out_s, mod_s, w_qkv, w_out, mod)


def home_kernel(done, out, ss, rs, ls):
    frame, patch, zh, x, core = place()
    others = [((frame + d) % 8, patch) for d in range(1, 8)]
    meet(others)
    copies = []
    for i, device in enumerate(others):
        copies.append(remote(done.at[device[0]], out.at[:, rows16(frame), :], ss.at[i], rs.at[i], device))
        copies[-1].start()
    mine = pltpu.make_async_copy(done.at[frame], out.at[:, rows16(frame), :], ls)
    mine.start()
    mine.wait()
    for copy in copies:
        copy.wait()


def home(done):
    return pl.pallas_call(
        home_kernel,
        name="home",
        out_shape=jax.ShapeDtypeStruct((4, 128, D), BF),
        in_specs=[VMEM],
        out_specs=VMEM,
        scratch_shapes=[
            pltpu.SemaphoreType.DMA((7,)),
            pltpu.SemaphoreType.DMA((7,)),
            pltpu.SemaphoreType.DMA,
        ],
        compiler_params=params(3),
    )(done)


def shards(tokens, w_qkv_s, w_out_s, mod_s, w_qkv_t, w_out_t, mod_t):
    full, tok_t = gather(tokens, mod_s)
    att = spatial(full, w_qkv_s)
    att_t = spread(att)
    done = temporal(att_t, tok_t.reshape(512, D), w_out_s, mod_s, w_qkv_t, w_out_t, mod_t)
    return home(done.reshape(8, 4, 16, D))


def solution(mesh):
    return jax.shard_map(
        shards,
        mesh=mesh,
        in_specs=(P("frame", "patch", None), P(), P(), P(), P(), P(), P()),
        out_specs=P("frame", "patch", None),
        check_vma=False,
    )
```

```python
import functools

import jax
import jax.numpy as jnp
from jax import lax
from jax.experimental import pallas as pl
from jax.experimental.pallas import tpu as pltpu
from jax.sharding import PartitionSpec as P

HEADS = 16
HD = 72
D = 1152
WIN = 384
ROWS = 2048
QT = 256
KC = 256
SCALE = HD ** (-0.5) * 1.4426950408889634
MESH = pl.DeviceIdType.MESH
VMEM = pl.BlockSpec(memory_space=pltpu.VMEM)
ANY = pl.BlockSpec(memory_space=pl.ANY)
BF = jnp.bfloat16
F32 = jnp.float32


def params(collective_id=None):
    return pltpu.CompilerParams(
        collective_id=collective_id,
        has_side_effects=collective_id is not None,
        vmem_limit_bytes=56 * 2**20,
    )


def remote(src, dst, send_sem, recv_sem, device):
    return pltpu.make_async_remote_copy(
        src_ref=src, dst_ref=dst, send_sem=send_sem, recv_sem=recv_sem, device_id=device, device_id_type=MESH
    )


def modulate(values, mod_ref):
    mean = jnp.mean(values, axis=-1, keepdims=True)
    centered = values - mean
    var = jnp.mean(centered * centered, axis=-1, keepdims=True)
    return (centered * lax.rsqrt(var + 1e-06) * (1.0 + mod_ref[1:2, :]) + mod_ref[0:1, :]).astype(BF)


def place():
    frame, patch = lax.axis_index("frame"), lax.axis_index("patch")
    return frame, patch, patch // 8, (patch // 2) % 4, patch % 2


def rows16(index):
    return pl.ds(pl.multiple_of(index * 16, 16), 16)


def head_lanes(shape, head, group):
    lane = lax.broadcasted_iota(jnp.int32, shape, 1) + (head // 2) * 128
    low = 32 * group + HD * head
    return (lane >= low) & (lane < low + HD)


def project(h, w, qk, vt, vwide, index, group):
    rows = pl.ds(pl.multiple_of(index * QT, QT), QT)
    for part in range(3):
        cols = slice(part * WIN, (part + 1) * WIN)
        acc = jnp.dot(h, w[:, cols], preferred_element_type=F32)
        if part == 0:
            acc = acc * SCALE
        if part < 2:
            qk[rows, cols] = acc.astype(BF)
        else:
            vwide[...] = acc.T
    one = jnp.where(lax.broadcasted_iota(jnp.int32, (8, QT), 0) == 0, 1.0, 0.0)
    for head in range(4):
        part = vwide[pl.ds(pl.multiple_of(32 * group + HD * head, 8), HD), :]
        vt[head, :, rows] = jnp.concatenate([part, one], axis=0).astype(BF)


def load_window(w, wbuf, sems, group):
    copies = []
    for part in range(3):
        cols = pl.ds(pl.multiple_of(part * D + 256 * group, 128), WIN)
        copies.append(pltpu.make_async_copy(w.at[:, cols], wbuf.at[:, pl.ds(part * WIN, WIN)], sems.at[part]))
        copies[-1].start()
    return copies


def swap_rows(forward):
    row = lax.broadcasted_iota(jnp.int32, (512, 512), 0)
    col = lax.broadcasted_iota(jnp.int32, (512, 512), 1)
    if forward:
        return jnp.where(col == (row % 32) * 16 + row // 32, 1.0, 0.0).astype(BF)
    return jnp.where(col == (row % 16) * 32 + row // 16, 1.0, 0.0).astype(BF)


def fused_kernel(
    tok, mod_s, mod_t, w_qkv_s, w_out_s, w_qkv_t, w_out_t, out,
    hs, zbuf, full, wbuf, qk, vt, vwide, s0, s1, m0, m1, awide, att, att_t, tok_t, wo_s, wq, wo,
    flat, mid, hp, qkv, mixed_all, done,
    w_sem, z_sem, full_sem, gather_send, tok_send, tok_recv, att_send, att_recv, home_send, home_recv,
):
    frame, patch, zh, x, core = place()
    group = (x % 2) * 2 + core
    at = frame * 4 + zh * 2 + x // 2
    zpatch = (1 - zh) * 8 + x * 2 + core
    sibling = (frame, patch + 1 - 2 * core)
    zdev = (frame, zpatch)

    barrier = pltpu.get_barrier_semaphore()

    def signal(i, _):
        device = ((frame + i // 16) % 8, (patch + i % 16) % 16)
        pl.semaphore_signal(barrier, inc=1, device_id=device, device_id_type=MESH)
        return 0

    lax.fori_loop(1, 128, signal, 0)
    windows = load_window(w_qkv_s, wbuf, w_sem, group)
    loads = [
        pltpu.make_async_copy(src, dst, w_sem.at[3 + i])
        for i, (src, dst) in enumerate([(w_out_s, wo_s), (w_qkv_t, wq), (w_out_t, wo)])
    ]
    for load in loads:
        load.start()

    def norm(f):
        hs[f] = modulate(tok[f].astype(F32), mod_s)

    norm(2 * (1 - zh))
    norm(2 * (1 - zh) + 1)
    pl.semaphore_wait(barrier, 127)
    for j in range(2):
        remote(hs.at[2 * (1 - zh) + j], zbuf.at[j], gather_send, z_sem.at[j], zdev).start()
    norm(2 * zh)
    norm(2 * zh + 1)

    def along_x(chunk, source):
        for d in (1, 3, 2):
            xd = (x + d) % 4
            remote(chunk(xd // 2), full.at[source], gather_send, full_sem.at[source], (frame, zh * 8 + xd * 2 + core)).start()
        pltpu.make_async_copy(chunk(x // 2), full.at[source], full_sem.at[source]).start()

    along_x(lambda j: hs.at[2 * zh + j], patch)
    awide[...] = jnp.zeros_like(awide)
    for window in windows:
        window.wait()

    def arrived(source):
        pltpu.make_async_copy(full.at[source], full.at[source], full_sem.at[source]).wait()

    def chip(k, _):
        plane = (zh + k // 4) % 2
        index = plane * 4 + (x + k % 4) % 4
        source = index * 2 + core
        arrived(source)
        remote(full.at[source], full.at[source], gather_send, full_sem.at[source], sibling).start()
        arrived(index * 2 + 1 - core)
        h = full[pl.ds(index * 2, 2)].reshape(QT, D)
        project(h, wbuf, qk, vt, vwide, index, group)
        return 0

    chip(0, 0)
    for j in range(2):
        pltpu.make_async_copy(zbuf.at[j], zbuf.at[j], z_sem.at[j]).wait()
    along_x(lambda j: zbuf.at[j], zpatch)

    def tokens_out(d, _):
        f = (frame + d) % 8
        remote(tok.at[:, rows16(f), :], tok_t.at[frame], tok_send, tok_recv, (f, patch)).start()
        return 0

    lax.fori_loop(1, 8, tokens_out, 0)
    pltpu.make_async_copy(tok.at[:, rows16(frame), :], tok_t.at[frame], tok_recv).start()
    lax.fori_loop(1, 8, chip, 0)

    scores, tops = (s0, s1), (m0, m1)
    first = patch // 2

    def score(head, tile, slot):
        base = (head // 2) * 128
        rows = pl.ds(pl.multiple_of(tile * QT, QT), QT)
        keep = head_lanes((QT, 256), head, group)
        query = jnp.where(keep, qk[rows, base : base + 256], jnp.zeros((), BF))
        top = None
        for c in range(ROWS // KC):
            keys = qk[c * KC : (c + 1) * KC, WIN + base : WIN + base + 256]
            part = lax.dot_general(keys, query, (((1,), (1,)), ((), ())), preferred_element_type=F32)
            scores[slot][c * KC : (c + 1) * KC, :] = part
            part = jnp.max(part.reshape(KC // 8, 8, QT), axis=0)
            top = part if top is None else jnp.maximum(top, part)
        tops[slot][...] = jnp.broadcast_to(jnp.max(top, axis=0, keepdims=True), (8, QT))

    def mix(head, slot):
        top = tops[slot][0:1, :]
        acc = None
        for c in range(ROWS // KC):
            span = slice(c * KC, (c + 1) * KC)
            probs = jnp.exp2(scores[slot][span, :] - top).astype(BF)
            part = jnp.dot(vt[head, :, span], probs, preferred_element_type=F32)
            acc = part if acc is None else acc + part
        awide[pl.ds(pl.multiple_of(32 * group + HD * head, 8), HD), :] = acc[:HD] / acc[HD : HD + 1]

    score(0, first, 0)

    def attend(i, _):
        tile = (first + i) % 8
        for head in range(4):
            score((head + 1) % 4, tile if head < 3 else (first + i + 1) % 8, (head + 1) % 2)
            mix(head, head % 2)
        att[pl.ds(pl.multiple_of(tile * QT, QT), QT), :] = awide[...].T.astype(BF)

        def go(n, _):
            f, p = n // 2, tile * 2 + n % 2
            src, dst = att.at[rows16(p * 8 + f), :], att_t.at[group, at]
            mine = (f == frame) & (p == patch)

            @pl.when(jnp.logical_not(mine))
            def _():
                remote(src, dst, att_send, att_recv, (f, p)).start()

            @pl.when(mine)
            def _():
                pltpu.make_async_copy(src, dst, att_recv).start()

            return 0

        lax.fori_loop(0, 16, go, 0)
        return 0

    lax.fori_loop(0, 8, attend, 0)

    for load in loads:
        load.wait()
    pltpu.make_async_copy(tok_t, tok_t, tok_recv).wait()
    pltpu.make_async_copy(att_t, att_t, att_recv).wait()
    for tile in range(9):
        cols = slice(tile * 128, tile * 128 + 128)
        g, rest = min(tile // 2, 3), tile - 2 * min(tile // 2, 3)
        part = att_t[g, :, :, rest * 128 : rest * 128 + 128].reshape(512, 128)
        if rest == 0 and g > 0:
            part = part + att_t[g - 1, :, :, 256:384].reshape(512, 128)
        flat[:, cols] = part

    def finish_mid(i, _):
        rows = pl.ds(pl.multiple_of(i * 256, 256), 256)
        proj = jnp.dot(flat[rows, :], wo_s[...], preferred_element_type=F32)
        values = tok_t[pl.ds(i * 4, 4)].reshape(256, D).astype(F32)
        values = (values + mod_s[2:3, :] * proj).astype(BF)
        mid[rows, :] = values
        flat[rows, :] = modulate(values.astype(F32), mod_t)
        return 0

    lax.fori_loop(0, 2, finish_mid, 0)
    hp[...] = jnp.dot(swap_rows(True), flat[...], preferred_element_type=F32).astype(BF)
    for part in range(9):
        cols = slice(part * WIN, (part + 1) * WIN)
        acc = jnp.dot(hp[...], wq[:, cols], preferred_element_type=F32)
        if part < 3:
            acc = acc * SCALE
        qkv[:, cols] = acc.astype(BF)

    row = lax.broadcasted_iota(jnp.int32, (128, 128), 0)
    col = lax.broadcasted_iota(jnp.int32, (128, 128), 1)
    same = row // 32 == col // 32
    lane = lax.broadcasted_iota(jnp.int32, (128, 256), 1)

    def four_patches(i, _):
        rows = pl.ds(pl.multiple_of(i * 128, 128), 128)
        for head in range(HEADS):
            base = min(head * HD // 128, 7) * 128
            low = head * HD - base
            keep = (lane >= low) & (lane < low + HD)
            query = jnp.where(keep, qkv[rows, base : base + 256], jnp.zeros((), BF))
            keys = qkv[rows, D + base : D + base + 256]
            part = lax.dot_general(query, keys, (((1,), (1,)), ((), ())), preferred_element_type=F32)
            part = jnp.where(same, part, -1e30)
            expo = jnp.exp2(part - jnp.max(part, axis=-1, keepdims=True))
            probs = (expo / jnp.sum(expo, axis=-1, keepdims=True)).astype(BF)
            mixed = jnp.dot(probs, qkv[rows, 2 * D + base : 2 * D + base + 256], preferred_element_type=F32)
            mixed = mixed.astype(BF)
            if low == 0:
                mixed_all[rows, base : base + 256] = mixed
            else:
                mixed_all[rows, base : base + 256] = jnp.where(keep, mixed, mixed_all[rows, base : base + 256])
        return 0

    lax.fori_loop(0, 4, four_patches, 0)
    flat[...] = jnp.dot(swap_rows(False), mixed_all[...], preferred_element_type=F32).astype(BF)

    def finish(i, _):
        i = (frame // 2 + i) % 4
        rows = pl.ds(pl.multiple_of(i * 128, 128), 128)
        proj = jnp.dot(flat[rows, :], wo[...], preferred_element_type=F32)
        values = (mid[rows, :].astype(F32) + mod_t[2:3, :] * proj).astype(BF)
        done[pl.ds(i * 2, 2)] = values.reshape(2, 4, 16, D)
        for n in range(2):
            f = i * 2 + n
            src, dst = done.at[f], out.at[:, rows16(frame), :]

            @pl.when(f != frame)
            def _():
                remote(src, dst, home_send, home_recv, (f, patch)).start()

            @pl.when(f == frame)
            def _():
                pltpu.make_async_copy(src, dst, home_recv).start()

        return 0

    lax.fori_loop(0, 4, finish, 0)
    pltpu.make_async_copy(full, full, gather_send).wait()
    pltpu.make_async_copy(tok_t.at[pl.ds(0, 7)], tok_t.at[pl.ds(0, 7)], tok_send).wait()
    pltpu.make_async_copy(att.at[pl.ds(0, 2032), :], att.at[pl.ds(0, 2032), :], att_send).wait()
    pltpu.make_async_copy(done.at[pl.ds(0, 7)], done.at[pl.ds(0, 7)], home_send).wait()
    pltpu.make_async_copy(out, out, home_recv).wait()


def shards(tokens, w_qkv_s, w_out_s, mod_s, w_qkv_t, w_out_t, mod_t):
    dma = pltpu.SemaphoreType.DMA
    return pl.pallas_call(
        fused_kernel,
        name="blocks",
        out_shape=jax.ShapeDtypeStruct((4, 128, D), BF),
        in_specs=[VMEM, VMEM, VMEM, ANY, ANY, ANY, ANY],
        out_specs=VMEM,
        scratch_shapes=[
            pltpu.VMEM((4, 128, D), BF),
            pltpu.VMEM((2, 128, D), BF),
            pltpu.VMEM((16, 128, D), BF),
            pltpu.VMEM((D, 3 * WIN), BF),
            pltpu.VMEM((ROWS, 2 * WIN), BF),
            pltpu.VMEM((4, 80, ROWS), BF),
            pltpu.VMEM((WIN, QT), F32),
            pltpu.VMEM((ROWS, QT), F32),
            pltpu.VMEM((ROWS, QT), F32),
            pltpu.VMEM((8, QT), F32),
            pltpu.VMEM((8, QT), F32),
            pltpu.VMEM((WIN, QT), F32),
            pltpu.VMEM((ROWS, WIN), BF),
            pltpu.VMEM((4, 32, 16, WIN), BF),
            pltpu.VMEM((8, 4, 16, D), BF),
            pltpu.VMEM((D, D), BF),
            pltpu.VMEM((D, 3 * D), BF),
            pltpu.VMEM((D, D), BF),
            pltpu.VMEM((512, D), BF),
            pltpu.VMEM((512, D), BF),
            pltpu.VMEM((512, D), BF),
            pltpu.VMEM((512, 3 * D), BF),
            pltpu.VMEM((512, D), BF),
            pltpu.VMEM((8, 4, 16, D), BF),
            dma((6,)),
            dma((2,)),
            dma((16,)),
            dma,
            dma,
            dma,
            dma,
            dma,
            dma,
            dma,
        ],
        compiler_params=params(1),
    )(tokens, mod_s, mod_t, w_qkv_s, w_out_s, w_qkv_t, w_out_t)


def solution(mesh):
    return jax.shard_map(
        shards,
        mesh=mesh,
        in_specs=(P("frame", "patch", None), P(), P(), P(), P(), P(), P()),
        out_specs=P("frame", "patch", None),
        check_vma=False,
    )
```

```python
import functools

import jax
import jax.numpy as jnp
from jax import lax
from jax.experimental import pallas as pl
from jax.experimental.pallas import tpu as pltpu
from jax.sharding import PartitionSpec as P

HEADS = 16
HD = 72
D = 1152
WIN = 384
ROWS = 2048
QT = 256
KC = 256
SCALE = HD ** (-0.5) * 1.4426950408889634
MESH = pl.DeviceIdType.MESH
VMEM = pl.BlockSpec(memory_space=pltpu.VMEM)
ANY = pl.BlockSpec(memory_space=pl.ANY)
BF = jnp.bfloat16
F32 = jnp.float32


def params(collective_id=None):
    return pltpu.CompilerParams(
        collective_id=collective_id,
        has_side_effects=collective_id is not None,
        vmem_limit_bytes=56 * 2**20,
    )


def remote(src, dst, send_sem, recv_sem, device):
    return pltpu.make_async_remote_copy(
        src_ref=src, dst_ref=dst, send_sem=send_sem, recv_sem=recv_sem, device_id=device, device_id_type=MESH
    )


def modulate(values, mod_ref):
    mean = jnp.mean(values, axis=-1, keepdims=True)
    centered = values - mean
    var = jnp.mean(centered * centered, axis=-1, keepdims=True)
    return (centered * lax.rsqrt(var + 1e-06) * (1.0 + mod_ref[1:2, :]) + mod_ref[0:1, :]).astype(BF)


def place():
    frame, patch = lax.axis_index("frame"), lax.axis_index("patch")
    return frame, patch, patch // 8, (patch // 2) % 4, patch % 2


def rows16(index):
    return pl.ds(pl.multiple_of(index * 16, 16), 16)


def head_lanes(shape, head, group):
    lane = lax.broadcasted_iota(jnp.int32, shape, 1) + (head // 2) * 128
    low = 32 * group + HD * head
    return (lane >= low) & (lane < low + HD)


def project(h, w, qk, vt, vwide, index, group):
    rows = pl.ds(pl.multiple_of(index * QT, QT), QT)
    for part in range(3):
        cols = slice(part * WIN, (part + 1) * WIN)
        acc = jnp.dot(h, w[:, cols], preferred_element_type=F32)
        if part == 0:
            acc = acc * SCALE
        if part < 2:
            qk[rows, cols] = acc.astype(BF)
        else:
            vwide[...] = acc.T
    one = jnp.where(lax.broadcasted_iota(jnp.int32, (8, QT), 0) == 0, 1.0, 0.0)
    for head in range(4):
        part = vwide[pl.ds(pl.multiple_of(32 * group + HD * head, 8), HD), :]
        vt[head, :, rows] = jnp.concatenate([part, one], axis=0).astype(BF)


def load_window(w, wbuf, sems, group):
    copies = []
    for part in range(3):
        cols = pl.ds(pl.multiple_of(part * D + 256 * group, 128), WIN)
        copies.append(pltpu.make_async_copy(w.at[:, cols], wbuf.at[:, pl.ds(part * WIN, WIN)], sems.at[part]))
        copies[-1].start()
    return copies


def swap_rows(forward):
    row = lax.broadcasted_iota(jnp.int32, (512, 512), 0)
    col = lax.broadcasted_iota(jnp.int32, (512, 512), 1)
    if forward:
        return jnp.where(col == (row % 32) * 16 + row // 32, 1.0, 0.0).astype(BF)
    return jnp.where(col == (row % 16) * 32 + row // 16, 1.0, 0.0).astype(BF)


def fused_kernel(
    tok, mod_s, mod_t, w_qkv_s, w_out_s, w_qkv_t, w_out_t, out,
    hs, zbuf, full, wbuf, qk, vt, vwide, s0, s1, m0, m1, awide, att, att_t, tok_t, wo_s, wq, wo,
    flat, mid, hp, qkv, mixed_all, done,
    w_sem, z_sem, full_sem, gather_send, tok_send, tok_recv, att_send, att_recv, home_send, home_recv, group_sem,
):
    frame, patch, zh, x, core = place()
    group = (x % 2) * 2 + core
    at = frame * 4 + zh * 2 + x // 2
    zpatch = (1 - zh) * 8 + x * 2 + core
    sibling = (frame, patch + 1 - 2 * core)
    zdev = (frame, zpatch)

    barrier = pltpu.get_barrier_semaphore()

    for d in range(1, 16):
        pl.semaphore_signal(barrier, inc=1, device_id=(frame, (patch + d) % 16), device_id_type=MESH)
    for d in range(1, 8):
        pl.semaphore_signal(barrier, inc=1, device_id=((frame + d) % 8, patch), device_id_type=MESH)
    windows = load_window(w_qkv_s, wbuf, w_sem, group)
    loads = [
        pltpu.make_async_copy(src, dst, w_sem.at[3 + i])
        for i, (src, dst) in enumerate([(w_out_s, wo_s), (w_qkv_t, wq), (w_out_t, wo)])
    ]
    for load in loads:
        load.start()

    def norm(f):
        hs[f] = modulate(tok[f].astype(F32), mod_s)

    norm(2 * (1 - zh))
    norm(2 * (1 - zh) + 1)
    pl.semaphore_wait(barrier, 22)
    for j in range(2):
        remote(hs.at[2 * (1 - zh) + j], zbuf.at[j], gather_send, z_sem.at[j], zdev).start()
    for d in range(1, 8):
        pl.semaphore_signal(group_sem, inc=1, device_id=((frame + d) % 8, patch), device_id_type=MESH)
    norm(2 * zh)
    norm(2 * zh + 1)

    def along_x(chunk, source):
        for d in (1, 3, 2):
            xd = (x + d) % 4
            remote(chunk(xd // 2), full.at[source], gather_send, full_sem.at[source], (frame, zh * 8 + xd * 2 + core)).start()
        pltpu.make_async_copy(chunk(x // 2), full.at[source], full_sem.at[source]).start()

    along_x(lambda j: hs.at[2 * zh + j], patch)
    awide[...] = jnp.zeros_like(awide)
    for window in windows:
        window.wait()

    def arrived(source):
        pltpu.make_async_copy(full.at[source], full.at[source], full_sem.at[source]).wait()

    def chip(k, _):
        plane = (zh + k // 4) % 2
        index = plane * 4 + (x + k % 4) % 4
        source = index * 2 + core
        arrived(source)
        remote(full.at[source], full.at[source], gather_send, full_sem.at[source], sibling).start()
        arrived(index * 2 + 1 - core)
        h = full[pl.ds(index * 2, 2)].reshape(QT, D)
        project(h, wbuf, qk, vt, vwide, index, group)
        return 0

    chip(0, 0)
    for j in range(2):
        pltpu.make_async_copy(zbuf.at[j], zbuf.at[j], z_sem.at[j]).wait()
    along_x(lambda j: zbuf.at[j], zpatch)

    lax.fori_loop(1, 8, chip, 0)

    def tokens_out(d, _):
        f = (frame + d) % 8
        remote(tok.at[:, rows16(f), :], tok_t.at[frame], tok_send, tok_recv, (f, patch)).start()
        return 0

    lax.fori_loop(1, 8, tokens_out, 0)
    pltpu.make_async_copy(tok.at[:, rows16(frame), :], tok_t.at[frame], tok_recv).start()
    pl.semaphore_wait(group_sem, 7)

    scores, tops = (s0, s1), (m0, m1)
    first = patch // 2

    def score(head, tile, slot):
        base = (head // 2) * 128
        rows = pl.ds(pl.multiple_of(tile * QT, QT), QT)
        keep = head_lanes((QT, 256), head, group)
        query = jnp.where(keep, qk[rows, base : base + 256], jnp.zeros((), BF))
        top = None
        for c in range(ROWS // KC):
            keys = qk[c * KC : (c + 1) * KC, WIN + base : WIN + base + 256]
            part = lax.dot_general(keys, query, (((1,), (1,)), ((), ())), preferred_element_type=F32)
            scores[slot][c * KC : (c + 1) * KC, :] = part
            part = jnp.max(part.reshape(KC // 8, 8, QT), axis=0)
            top = part if top is None else jnp.maximum(top, part)
        tops[slot][...] = jnp.broadcast_to(jnp.max(top, axis=0, keepdims=True), (8, QT))

    def mix(head, slot):
        top = tops[slot][0:1, :]
        acc = None
        for c in range(ROWS // KC):
            span = slice(c * KC, (c + 1) * KC)
            probs = jnp.exp2(scores[slot][span, :] - top).astype(BF)
            part = jnp.dot(vt[head, :, span], probs, preferred_element_type=F32)
            acc = part if acc is None else acc + part
        awide[pl.ds(pl.multiple_of(32 * group + HD * head, 8), HD), :] = acc[:HD] / acc[HD : HD + 1]

    score(0, first, 0)

    def attend(i, _):
        tile = (first + i) % 8
        for head in range(4):
            score((head + 1) % 4, tile if head < 3 else (first + i + 1) % 8, (head + 1) % 2)
            mix(head, head % 2)
        att[pl.ds(pl.multiple_of(tile * QT, QT), QT), :] = awide[...].T.astype(BF)

        def go(n, _):
            f, p = n // 2, tile * 2 + n % 2
            src, dst = att.at[rows16(p * 8 + f), :], att_t.at[group, at]
            mine = (f == frame) & (p == patch)

            @pl.when(jnp.logical_not(mine))
            def _():
                remote(src, dst, att_send, att_recv, (f, p)).start()

            @pl.when(mine)
            def _():
                pltpu.make_async_copy(src, dst, att_recv).start()

            return 0

        lax.fori_loop(0, 16, go, 0)
        return 0

    lax.fori_loop(0, 8, attend, 0)

    for load in loads:
        load.wait()
    pltpu.make_async_copy(tok_t, tok_t, tok_recv).wait()
    pltpu.make_async_copy(att_t, att_t, att_recv).wait()
    for tile in range(9):
        cols = slice(tile * 128, tile * 128 + 128)
        g, rest = min(tile // 2, 3), tile - 2 * min(tile // 2, 3)
        part = att_t[g, :, :, rest * 128 : rest * 128 + 128].reshape(512, 128)
        if rest == 0 and g > 0:
            part = part + att_t[g - 1, :, :, 256:384].reshape(512, 128)
        flat[:, cols] = part

    def finish_mid(i, _):
        rows = pl.ds(pl.multiple_of(i * 256, 256), 256)
        proj = jnp.dot(flat[rows, :], wo_s[...], preferred_element_type=F32)
        values = tok_t[pl.ds(i * 4, 4)].reshape(256, D).astype(F32)
        values = (values + mod_s[2:3, :] * proj).astype(BF)
        mid[rows, :] = values
        flat[rows, :] = modulate(values.astype(F32), mod_t)
        return 0

    lax.fori_loop(0, 2, finish_mid, 0)
    hp[...] = jnp.dot(swap_rows(True), flat[...], preferred_element_type=F32).astype(BF)
    for part in range(9):
        cols = slice(part * WIN, (part + 1) * WIN)
        acc = jnp.dot(hp[...], wq[:, cols], preferred_element_type=F32)
        if part < 3:
            acc = acc * SCALE
        qkv[:, cols] = acc.astype(BF)

    row = lax.broadcasted_iota(jnp.int32, (128, 128), 0)
    col = lax.broadcasted_iota(jnp.int32, (128, 128), 1)
    same = row // 32 == col // 32
    lane = lax.broadcasted_iota(jnp.int32, (128, 256), 1)

    def four_patches(i, _):
        rows = pl.ds(pl.multiple_of(i * 128, 128), 128)
        for head in range(HEADS):
            base = min(head * HD // 128, 7) * 128
            low = head * HD - base
            keep = (lane >= low) & (lane < low + HD)
            query = jnp.where(keep, qkv[rows, base : base + 256], jnp.zeros((), BF))
            keys = qkv[rows, D + base : D + base + 256]
            part = lax.dot_general(query, keys, (((1,), (1,)), ((), ())), preferred_element_type=F32)
            part = jnp.where(same, part, -1e30)
            expo = jnp.exp2(part - jnp.max(part, axis=-1, keepdims=True))
            probs = (expo / jnp.sum(expo, axis=-1, keepdims=True)).astype(BF)
            mixed = jnp.dot(probs, qkv[rows, 2 * D + base : 2 * D + base + 256], preferred_element_type=F32)
            mixed = mixed.astype(BF)
            if low == 0:
                mixed_all[rows, base : base + 256] = mixed
            else:
                mixed_all[rows, base : base + 256] = jnp.where(keep, mixed, mixed_all[rows, base : base + 256])
        return 0

    lax.fori_loop(0, 4, four_patches, 0)
    flat[...] = jnp.dot(swap_rows(False), mixed_all[...], preferred_element_type=F32).astype(BF)

    def finish(i, _):
        i = (frame // 2 + i) % 4
        rows = pl.ds(pl.multiple_of(i * 128, 128), 128)
        proj = jnp.dot(flat[rows, :], wo[...], preferred_element_type=F32)
        values = (mid[rows, :].astype(F32) + mod_t[2:3, :] * proj).astype(BF)
        done[pl.ds(i * 2, 2)] = values.reshape(2, 4, 16, D)
        for n in range(2):
            f = i * 2 + n
            src, dst = done.at[f], out.at[:, rows16(frame), :]

            @pl.when(f != frame)
            def _():
                remote(src, dst, home_send, home_recv, (f, patch)).start()

            @pl.when(f == frame)
            def _():
                pltpu.make_async_copy(src, dst, home_recv).start()

        return 0

    lax.fori_loop(0, 4, finish, 0)
    pltpu.make_async_copy(full, full, gather_send).wait()
    pltpu.make_async_copy(tok_t.at[pl.ds(0, 7)], tok_t.at[pl.ds(0, 7)], tok_send).wait()
    pltpu.make_async_copy(att.at[pl.ds(0, 2032), :], att.at[pl.ds(0, 2032), :], att_send).wait()
    pltpu.make_async_copy(done.at[pl.ds(0, 7)], done.at[pl.ds(0, 7)], home_send).wait()
    pltpu.make_async_copy(out, out, home_recv).wait()


def shards(tokens, w_qkv_s, w_out_s, mod_s, w_qkv_t, w_out_t, mod_t):
    dma = pltpu.SemaphoreType.DMA
    return pl.pallas_call(
        fused_kernel,
        name="blocks",
        out_shape=jax.ShapeDtypeStruct((4, 128, D), BF),
        in_specs=[VMEM, VMEM, VMEM, ANY, ANY, ANY, ANY],
        out_specs=VMEM,
        scratch_shapes=[
            pltpu.VMEM((4, 128, D), BF),
            pltpu.VMEM((2, 128, D), BF),
            pltpu.VMEM((16, 128, D), BF),
            pltpu.VMEM((D, 3 * WIN), BF),
            pltpu.VMEM((ROWS, 2 * WIN), BF),
            pltpu.VMEM((4, 80, ROWS), BF),
            pltpu.VMEM((WIN, QT), F32),
            pltpu.VMEM((ROWS, QT), F32),
            pltpu.VMEM((ROWS, QT), F32),
            pltpu.VMEM((8, QT), F32),
            pltpu.VMEM((8, QT), F32),
            pltpu.VMEM((WIN, QT), F32),
            pltpu.VMEM((ROWS, WIN), BF),
            pltpu.VMEM((4, 32, 16, WIN), BF),
            pltpu.VMEM((8, 4, 16, D), BF),
            pltpu.VMEM((D, D), BF),
            pltpu.VMEM((D, 3 * D), BF),
            pltpu.VMEM((D, D), BF),
            pltpu.VMEM((512, D), BF),
            pltpu.VMEM((512, D), BF),
            pltpu.VMEM((512, D), BF),
            pltpu.VMEM((512, 3 * D), BF),
            pltpu.VMEM((512, D), BF),
            pltpu.VMEM((8, 4, 16, D), BF),
            dma((6,)),
            dma((2,)),
            dma((16,)),
            dma,
            dma,
            dma,
            dma,
            dma,
            dma,
            dma,
            pltpu.SemaphoreType.REGULAR,
        ],
        compiler_params=params(1),
    )(tokens, mod_s, mod_t, w_qkv_s, w_out_s, w_qkv_t, w_out_t)


def solution(mesh):
    return jax.shard_map(
        shards,
        mesh=mesh,
        in_specs=(P("frame", "patch", None), P(), P(), P(), P(), P(), P()),
        out_specs=P("frame", "patch", None),
        check_vma=False,
    )
```

```python
import functools

import jax
import jax.numpy as jnp
from jax import lax
from jax.experimental import pallas as pl
from jax.experimental.pallas import tpu as pltpu
from jax.sharding import PartitionSpec as P

HEADS = 16
HD = 72
D = 1152
WIN = 384
ROWS = 2048
QT = 256
KC = 256
SCALE = HD ** (-0.5) * 1.4426950408889634
MESH = pl.DeviceIdType.MESH
VMEM = pl.BlockSpec(memory_space=pltpu.VMEM)
ANY = pl.BlockSpec(memory_space=pl.ANY)
BF = jnp.bfloat16
F32 = jnp.float32


def params(collective_id=None):
    return pltpu.CompilerParams(
        collective_id=collective_id,
        has_side_effects=collective_id is not None,
        vmem_limit_bytes=56 * 2**20,
    )


def remote(src, dst, send_sem, recv_sem, device):
    return pltpu.make_async_remote_copy(
        src_ref=src, dst_ref=dst, send_sem=send_sem, recv_sem=recv_sem, device_id=device, device_id_type=MESH
    )


def modulate(values, mod_ref):
    mean = jnp.mean(values, axis=-1, keepdims=True)
    centered = values - mean
    var = jnp.mean(centered * centered, axis=-1, keepdims=True)
    return (centered * lax.rsqrt(var + 1e-06) * (1.0 + mod_ref[1:2, :]) + mod_ref[0:1, :]).astype(BF)


def place():
    frame, patch = lax.axis_index("frame"), lax.axis_index("patch")
    return frame, patch, patch // 8, (patch // 2) % 4, patch % 2


def rows16(index):
    return pl.ds(pl.multiple_of(index * 16, 16), 16)


def head_lanes(shape, head, group):
    lane = lax.broadcasted_iota(jnp.int32, shape, 1) + (head // 2) * 128
    low = 32 * group + HD * head
    return (lane >= low) & (lane < low + HD)


def project(h, w, qk, vt, vwide, index, group):
    rows = pl.ds(pl.multiple_of(index * QT, QT), QT)
    for part in range(3):
        cols = slice(part * WIN, (part + 1) * WIN)
        acc = jnp.dot(h, w[:, cols], preferred_element_type=F32)
        if part == 0:
            acc = acc * SCALE
        if part < 2:
            qk[rows, cols] = acc.astype(BF)
        else:
            vwide[...] = acc.T
    one = jnp.where(lax.broadcasted_iota(jnp.int32, (8, QT), 0) == 0, 1.0, 0.0)
    for head in range(4):
        part = vwide[pl.ds(pl.multiple_of(32 * group + HD * head, 8), HD), :]
        vt[head, :, rows] = jnp.concatenate([part, one], axis=0).astype(BF)


def load_window(w, wbuf, sems, group):
    copies = []
    for part in range(3):
        cols = pl.ds(pl.multiple_of(part * D + 256 * group, 128), WIN)
        copies.append(pltpu.make_async_copy(w.at[:, cols], wbuf.at[:, pl.ds(part * WIN, WIN)], sems.at[part]))
        copies[-1].start()
    return copies


def to_patches():
    row = lax.broadcasted_iota(jnp.int32, (512, 512), 0)
    col = lax.broadcasted_iota(jnp.int32, (512, 512), 1)
    return jnp.where(col == (row % 32) * 16 + row // 32, 1.0, 0.0).astype(BF)


def to_frames():
    row = lax.broadcasted_iota(jnp.int32, (256, 256), 0)
    col = lax.broadcasted_iota(jnp.int32, (256, 256), 1)
    return jnp.where(col == (row % 8) * 32 + row // 8, 1.0, 0.0).astype(BF)


def fused_kernel(
    tok_hbm, mod_s, mod_t, w_qkv_s, w_out_s, w_qkv_t, w_out_t, out,
    tok, hs, zbuf, full, wbuf, qk, vt, vwide, s0, s1, m0, m1, held, held_top, awide, att, att_t, tok_t, wo_s, wq, wo,
    flat, mid, hp, qkv, mixed_all, done,
    tok_sem, w_sem, z_sem, full_sem, gather_send, tok_send, tok_recv, att_send, att_recv, home_send, home_recv, group_sem,
):
    frame, patch, zh, x, core = place()
    group = (x % 2) * 2 + core
    at = frame * 4 + zh * 2 + x // 2
    zpatch = (1 - zh) * 8 + x * 2 + core
    sibling = (frame, patch + 1 - 2 * core)
    zdev = (frame, zpatch)

    barrier = pltpu.get_barrier_semaphore()

    for d in range(1, 16):
        pl.semaphore_signal(barrier, inc=1, device_id=(frame, (patch + d) % 16), device_id_type=MESH)
    for d in range(1, 8):
        pl.semaphore_signal(barrier, inc=1, device_id=((frame + d) % 8, patch), device_id_type=MESH)
    load_tok = pltpu.make_async_copy(tok_hbm, tok, tok_sem)
    load_tok.start()
    windows = load_window(w_qkv_s, wbuf, w_sem, group)
    loads = [
        pltpu.make_async_copy(src, dst, w_sem.at[3 + i])
        for i, (src, dst) in enumerate([(w_out_s, wo_s), (w_qkv_t, wq), (w_out_t, wo)])
    ]
    for load in loads:
        load.start()

    def norm(f):
        hs[f] = modulate(tok[f].astype(F32), mod_s)

    load_tok.wait()
    norm(2 * (1 - zh))
    norm(2 * (1 - zh) + 1)
    pl.semaphore_wait(barrier, 22)
    for j in range(2):
        remote(hs.at[2 * (1 - zh) + j], zbuf.at[j], gather_send, z_sem.at[j], zdev).start()
    for d in range(1, 8):
        pl.semaphore_signal(group_sem, inc=1, device_id=((frame + d) % 8, patch), device_id_type=MESH)
    norm(2 * zh)
    norm(2 * zh + 1)

    def along_x(chunk, source):
        for d in (1, 3, 2):
            xd = (x + d) % 4
            remote(chunk(xd // 2), full.at[source], gather_send, full_sem.at[source], (frame, zh * 8 + xd * 2 + core)).start()
        pltpu.make_async_copy(chunk(x // 2), full.at[source], full_sem.at[source]).start()

    along_x(lambda j: hs.at[2 * zh + j], patch)
    awide[...] = jnp.zeros_like(awide)
    for window in windows:
        window.wait()

    def arrived(source):
        pltpu.make_async_copy(full.at[source], full.at[source], full_sem.at[source]).wait()

    def chip(k, _):
        plane = (zh + k // 4) % 2
        index = plane * 4 + (x + k % 4) % 4
        source = index * 2 + core
        arrived(source)
        remote(full.at[source], full.at[source], gather_send, full_sem.at[source], sibling).start()
        arrived(index * 2 + 1 - core)
        h = full[pl.ds(index * 2, 2)].reshape(QT, D)
        project(h, wbuf, qk, vt, vwide, index, group)
        return 0

    chip(0, 0)
    for j in range(2):
        pltpu.make_async_copy(zbuf.at[j], zbuf.at[j], z_sem.at[j]).wait()
    along_x(lambda j: zbuf.at[j], zpatch)

    lax.fori_loop(1, 5, chip, 0)

    def tokens_out(d, _):
        f = (frame + d) % 8
        remote(tok.at[:, rows16(f), :], tok_t.at[frame], tok_send, tok_recv, (f, patch)).start()
        return 0

    lax.fori_loop(1, 8, tokens_out, 0)
    pltpu.make_async_copy(tok.at[:, rows16(frame), :], tok_t.at[frame], tok_recv).start()

    scores, tops = (s0, s1), (m0, m1)

    def score(head, tile, slot, start, count):
        base = (head // 2) * 128
        rows = pl.ds(pl.multiple_of(tile * QT, QT), QT)
        keep = head_lanes((QT, 256), head, group)
        query = jnp.where(keep, qk[rows, base : base + 256], jnp.zeros((), BF))
        top = None
        for c in range(count):
            keys = qk[pl.ds(pl.multiple_of(start + c * KC, KC), KC), WIN + base : WIN + base + 256]
            part = lax.dot_general(keys, query, (((1,), (1,)), ((), ())), preferred_element_type=F32)
            scores[slot][c * KC : (c + 1) * KC, :] = part
            part = jnp.max(part.reshape(KC // 8, 8, QT), axis=0)
            top = part if top is None else jnp.maximum(top, part)
        tops[slot][...] = jnp.broadcast_to(jnp.max(top, axis=0, keepdims=True), (8, QT))

    def sums(head, slot, start, count, top):
        acc = None
        for c in range(count):
            probs = jnp.exp2(scores[slot][c * KC : (c + 1) * KC, :] - top).astype(BF)
            values = vt[head, :, pl.ds(pl.multiple_of(start + c * KC, KC), KC)]
            part = jnp.dot(values, probs, preferred_element_type=F32)
            acc = part if acc is None else acc + part
        return acc

    def keep_head(head, acc):
        awide[pl.ds(pl.multiple_of(32 * group + HD * head, 8), HD), :] = acc[:HD] / acc[HD : HD + 1]

    def send_tile(tile):
        att[pl.ds(pl.multiple_of(tile * QT, QT), QT), :] = awide[...].T.astype(BF)

        def go(n, _):
            f, p = n // 2, tile * 2 + n % 2
            src, dst = att.at[rows16(p * 8 + f), :], att_t.at[group, at]
            mine = (f == frame) & (p == patch)

            @pl.when(jnp.logical_not(mine))
            def _():
                remote(src, dst, att_send, att_recv, (f, p)).start()

            @pl.when(mine)
            def _():
                pltpu.make_async_copy(src, dst, att_recv).start()

            return 0

        lax.fori_loop(0, 16, go, 0)

    half = ROWS // 2
    near, far = zh * half, (1 - zh) * half
    score(0, zh * 4 + x, 0, near, 4)

    def first_part(i, _):
        for head in range(4):
            ahead = (x + i) % 4 if head < 3 else (x + i + 1) % 4
            score((head + 1) % 4, zh * 4 + ahead, (head + 1) % 2, near, 4)
            slot = head % 2
            held[(x + i) % 4, head] = sums(head, slot, near, 4, tops[slot][0:1, :])
            held_top[(x + i) % 4, head] = tops[slot][...]
        return 0

    lax.fori_loop(0, 4, first_part, 0)
    lax.fori_loop(5, 8, chip, 0)
    pl.semaphore_wait(group_sem, 7)
    score(0, zh * 4 + x, 0, far, 4)

    def second_part(i, _):
        for head in range(4):
            ahead = (x + i) % 4 if head < 3 else (x + i + 1) % 4
            score((head + 1) % 4, zh * 4 + ahead, (head + 1) % 2, far, 4)
            slot = head % 2
            before = held_top[(x + i) % 4, head, 0:1, :]
            top = jnp.maximum(tops[slot][0:1, :], before)
            acc = held[(x + i) % 4, head] * jnp.exp2(before - top)
            keep_head(head, acc + sums(head, slot, far, 4, top))
        send_tile(zh * 4 + (x + i) % 4)
        return 0

    lax.fori_loop(0, 4, second_part, 0)
    score(0, (1 - zh) * 4 + x, 0, 0, 8)

    def other_tiles(i, _):
        for head in range(4):
            ahead = (x + i) % 4 if head < 3 else (x + i + 1) % 4
            score((head + 1) % 4, (1 - zh) * 4 + ahead, (head + 1) % 2, 0, 8)
            slot = head % 2
            keep_head(head, sums(head, slot, 0, 8, tops[slot][0:1, :]))
        send_tile((1 - zh) * 4 + (x + i) % 4)
        return 0

    lax.fori_loop(0, 4, other_tiles, 0)

    for load in loads:
        load.wait()
    pltpu.make_async_copy(tok_t, tok_t, tok_recv).wait()
    pltpu.make_async_copy(att_t, att_t, att_recv).wait()
    for tile in range(9):
        cols = slice(tile * 128, tile * 128 + 128)
        g, rest = min(tile // 2, 3), tile - 2 * min(tile // 2, 3)
        part = att_t[g, :, :, rest * 128 : rest * 128 + 128].reshape(512, 128)
        if rest == 0 and g > 0:
            part = part + att_t[g - 1, :, :, 256:384].reshape(512, 128)
        flat[:, cols] = part

    def finish_mid(i, _):
        rows = pl.ds(pl.multiple_of(i * 256, 256), 256)
        proj = jnp.dot(flat[rows, :], wo_s[...], preferred_element_type=F32)
        values = tok_t[pl.ds(i * 4, 4)].reshape(256, D).astype(F32)
        values = (values + mod_s[2:3, :] * proj).astype(BF)
        mid[pl.ds(i * 16, 16)] = values.astype(F32).reshape(16, 16, D)
        flat[rows, :] = modulate(values.astype(F32), mod_t)
        return 0

    lax.fori_loop(0, 2, finish_mid, 0)
    hp[...] = jnp.dot(to_patches(), flat[...], preferred_element_type=F32).astype(BF)

    row = lax.broadcasted_iota(jnp.int32, (128, 128), 0)
    col = lax.broadcasted_iota(jnp.int32, (128, 128), 1)
    same = row // 32 == col // 32
    lane = lax.broadcasted_iota(jnp.int32, (128, 256), 1)

    def four_patches(i, _):
        rows = pl.ds(pl.multiple_of(i * 128, 128), 128)
        tiles = [None] * 9
        for head in range(HEADS):
            tile = min(head * HD // 128, 7)
            base = tile * 128
            low = head * HD - base
            keep = (lane >= low) & (lane < low + HD)
            query = jnp.where(keep, qkv[rows, base : base + 256], jnp.zeros((), BF))
            keys = qkv[rows, D + base : D + base + 256]
            part = lax.dot_general(query, keys, (((1,), (1,)), ((), ())), preferred_element_type=F32)
            part = jnp.where(same, part, -1e30)
            expo = jnp.exp2(part - jnp.max(part, axis=-1, keepdims=True))
            probs = (expo / jnp.sum(expo, axis=-1, keepdims=True)).astype(BF)
            mixed = jnp.dot(probs, qkv[rows, 2 * D + base : 2 * D + base + 256], preferred_element_type=F32)
            for n in range(2):
                piece = mixed[:, n * 128 : n * 128 + 128]
                old = tiles[tile + n]
                tiles[tile + n] = piece if old is None else jnp.where(keep[:, n * 128 : n * 128 + 128], piece, old)
        for n in range(9):
            mixed_all[rows, n * 128 : n * 128 + 128] = tiles[n].astype(BF)
        return 0

    def eight_patches(n, _):
        rows = pl.ds(pl.multiple_of(n * 256, 256), 256)
        for part in range(9):
            cols = slice(part * WIN, (part + 1) * WIN)
            acc = jnp.dot(hp[rows, :], wq[:, cols], preferred_element_type=F32)
            if part < 3:
                acc = acc * SCALE
            qkv[:, cols] = acc.astype(BF)
        lax.fori_loop(0, 2, four_patches, 0)
        ordered = jnp.dot(to_frames(), mixed_all[...], preferred_element_type=F32).astype(BF)
        proj = jnp.dot(ordered, wo[...], preferred_element_type=F32)
        values = mid[:, pl.ds(pl.multiple_of(n * 8, 8), 8), :].reshape(256, D)
        values = (values + mod_t[2:3, :] * proj).astype(BF)
        done[n] = values.reshape(8, 32, D)

        def go(d, _):
            f = (frame + d) % 8
            remote(done.at[n, f], out.at[n, frame], home_send, home_recv, (f, patch)).start()
            return 0

        lax.fori_loop(1, 8, go, 0)
        pltpu.make_async_copy(done.at[n, frame], out.at[n, frame], home_recv).start()
        return 0

    lax.fori_loop(0, 2, eight_patches, 0)
    pltpu.make_async_copy(full, full, gather_send).wait()
    pltpu.make_async_copy(tok_t.at[pl.ds(0, 7)], tok_t.at[pl.ds(0, 7)], tok_send).wait()
    pltpu.make_async_copy(att.at[pl.ds(0, 2032), :], att.at[pl.ds(0, 2032), :], att_send).wait()
    for n in range(2):
        pltpu.make_async_copy(done.at[n, pl.ds(0, 7)], done.at[n, pl.ds(0, 7)], home_send).wait()
    pltpu.make_async_copy(out, out, home_recv).wait()


def shards(tokens, w_qkv_s, w_out_s, mod_s, w_qkv_t, w_out_t, mod_t):
    dma = pltpu.SemaphoreType.DMA
    parts = pl.pallas_call(
        fused_kernel,
        name="blocks",
        out_shape=jax.ShapeDtypeStruct((2, 8, 32, D), BF),
        in_specs=[ANY, VMEM, VMEM, ANY, ANY, ANY, ANY],
        out_specs=ANY,
        scratch_shapes=[
            pltpu.VMEM((4, 128, D), BF),
            pltpu.VMEM((4, 128, D), BF),
            pltpu.VMEM((2, 128, D), BF),
            pltpu.VMEM((16, 128, D), BF),
            pltpu.VMEM((D, 3 * WIN), BF),
            pltpu.VMEM((ROWS, 2 * WIN), BF),
            pltpu.VMEM((4, 80, ROWS), BF),
            pltpu.VMEM((WIN, QT), F32),
            pltpu.VMEM((ROWS, QT), F32),
            pltpu.VMEM((ROWS, QT), F32),
            pltpu.VMEM((8, QT), F32),
            pltpu.VMEM((8, QT), F32),
            pltpu.VMEM((4, 4, 80, QT), F32),
            pltpu.VMEM((4, 4, 8, QT), F32),
            pltpu.VMEM((WIN, QT), F32),
            pltpu.VMEM((ROWS, WIN), BF),
            pltpu.VMEM((4, 32, 16, WIN), BF),
            pltpu.VMEM((8, 4, 16, D), BF),
            pltpu.VMEM((D, D), BF),
            pltpu.VMEM((D, 3 * D), BF),
            pltpu.VMEM((D, D), BF),
            pltpu.VMEM((512, D), BF),
            pltpu.VMEM((32, 16, D), F32),
            pltpu.VMEM((512, D), BF),
            pltpu.VMEM((256, 3 * D), BF),
            pltpu.VMEM((256, D), BF),
            pltpu.VMEM((2, 8, 32, D), BF),
            dma,
            dma((6,)),
            dma((2,)),
            dma((16,)),
            dma,
            dma,
            dma,
            dma,
            dma,
            dma,
            dma,
            pltpu.SemaphoreType.REGULAR,
        ],
        compiler_params=params(1),
    )(tokens, mod_s, mod_t, w_qkv_s, w_out_s, w_qkv_t, w_out_t)
    return parts.reshape(2, 8, 4, 8, D).transpose(2, 1, 0, 3, 4).reshape(4, 128, D)


def solution(mesh):
    return jax.shard_map(
        shards,
        mesh=mesh,
        in_specs=(P("frame", "patch", None), P(), P(), P(), P(), P(), P()),
        out_specs=P("frame", "patch", None),
        check_vma=False,
    )
```

```python
import functools

import jax
import jax.numpy as jnp
from jax import lax
from jax.experimental import pallas as pl
from jax.experimental.pallas import tpu as pltpu
from jax.sharding import PartitionSpec as P

HEADS = 16
HD = 72
D = 1152
WIN = 384
ROWS = 2048
QT = 256
KC = 256
SCALE = HD ** (-0.5) * 1.4426950408889634
MESH = pl.DeviceIdType.MESH
VMEM = pl.BlockSpec(memory_space=pltpu.VMEM)
ANY = pl.BlockSpec(memory_space=pl.ANY)
BF = jnp.bfloat16
F32 = jnp.float32


def params(collective_id=None):
    return pltpu.CompilerParams(
        collective_id=collective_id,
        has_side_effects=collective_id is not None,
        vmem_limit_bytes=56 * 2**20,
    )


def remote(src, dst, send_sem, recv_sem, device):
    return pltpu.make_async_remote_copy(
        src_ref=src, dst_ref=dst, send_sem=send_sem, recv_sem=recv_sem, device_id=device, device_id_type=MESH
    )


def modulate(values, mod_ref):
    mean = jnp.mean(values, axis=-1, keepdims=True)
    centered = values - mean
    var = jnp.mean(centered * centered, axis=-1, keepdims=True)
    return (centered * lax.rsqrt(var + 1e-06) * (1.0 + mod_ref[1:2, :]) + mod_ref[0:1, :]).astype(BF)


def place():
    frame, patch = lax.axis_index("frame"), lax.axis_index("patch")
    return frame, patch, patch // 8, (patch // 2) % 4, patch % 2


def rows16(index):
    return pl.ds(pl.multiple_of(index * 16, 16), 16)


def head_lanes(shape, head):
    lane = lax.broadcasted_iota(jnp.int32, shape, 1) + (head // 2) * 128
    return (lane >= HD * head) & (lane < HD * head + HD)


def pack_weights(wbuf, packed, group):
    row = lax.broadcasted_iota(jnp.int32, (2 * WIN, 640), 0)
    col = lax.broadcasted_iota(jnp.int32, (2 * WIN, 640), 1)
    width = 4 * HD
    target = jnp.where(col < width, col, col + (WIN - width)) + 32 * group
    pick = jnp.where((row == target) & (col < 2 * width), 1.0, 0.0).astype(BF)
    row = lax.broadcasted_iota(jnp.int32, (WIN, WIN), 0)
    col = lax.broadcasted_iota(jnp.int32, (WIN, WIN), 1)
    first = jnp.where((row == col + 32 * group) & (col < width), 1.0, 0.0).astype(BF)

    def some(i, _):
        rows = pl.ds(pl.multiple_of(i * 384, 384), 384)
        packed[rows, :WIN] = jnp.dot(wbuf[rows, :WIN], first, preferred_element_type=F32).astype(BF)
        packed[rows, WIN:] = jnp.dot(wbuf[rows, WIN:], pick, preferred_element_type=F32).astype(BF)
        return 0

    lax.fori_loop(0, 3, some, 0)


def project(h, packed, qk, vt, index):
    rows = pl.ds(pl.multiple_of(index * QT, QT), QT)
    acc = jnp.dot(h, packed[...], preferred_element_type=F32)
    qk[rows, :WIN] = (acc[:, :WIN] * SCALE).astype(BF)
    qk[rows, WIN:] = acc[:, WIN : 2 * WIN].astype(BF)
    values = acc[:, 640:1024].T
    one = jnp.where(lax.broadcasted_iota(jnp.int32, (8, QT), 0) == 0, 1.0, 0.0)
    for head in range(4):
        part = values[32 + HD * head : 32 + HD * head + HD, :]
        vt[head, :, rows] = jnp.concatenate([part, one], axis=0).astype(BF)


def load_window(w, wbuf, sems, group):
    copies = []
    for part in range(3):
        cols = pl.ds(pl.multiple_of(part * D + 256 * group, 128), WIN)
        copies.append(pltpu.make_async_copy(w.at[:, cols], wbuf.at[:, pl.ds(part * WIN, WIN)], sems.at[part]))
        copies[-1].start()
    return copies


def to_patches():
    row = lax.broadcasted_iota(jnp.int32, (512, 512), 0)
    col = lax.broadcasted_iota(jnp.int32, (512, 512), 1)
    return jnp.where(col == (row % 32) * 16 + row // 32, 1.0, 0.0).astype(BF)


def to_frames():
    row = lax.broadcasted_iota(jnp.int32, (256, 256), 0)
    col = lax.broadcasted_iota(jnp.int32, (256, 256), 1)
    return jnp.where(col == (row % 8) * 32 + row // 8, 1.0, 0.0).astype(BF)


def fused_kernel(
    tok_hbm, mod_s, mod_t, w_qkv_s, w_out_s, w_qkv_t, w_out_t, out,
    tok, hs, zbuf, full, wbuf, packed, qk, vt, s0, s1, m0, m1, held, held_top, awide, att, att_t, tok_t, wo_s, wq, wo,
    flat, mid, hp, qkv, mixed_all, done,
    tok_sem, w_sem, z_sem, full_sem, gather_send, tok_send, tok_recv, att_send, att_recv, home_send, home_recv, group_sem,
):
    frame, patch, zh, x, core = place()
    group = (x % 2) * 2 + core
    at = frame * 4 + zh * 2 + x // 2
    zpatch = (1 - zh) * 8 + x * 2 + core
    sibling = (frame, patch + 1 - 2 * core)
    zdev = (frame, zpatch)

    barrier = pltpu.get_barrier_semaphore()

    for d in range(1, 16):
        pl.semaphore_signal(barrier, inc=1, device_id=(frame, (patch + d) % 16), device_id_type=MESH)
    for d in range(1, 8):
        pl.semaphore_signal(barrier, inc=1, device_id=((frame + d) % 8, patch), device_id_type=MESH)
    load_tok = pltpu.make_async_copy(tok_hbm, tok, tok_sem)
    load_tok.start()
    windows = load_window(w_qkv_s, wbuf, w_sem, group)
    loads = [
        pltpu.make_async_copy(src, dst, w_sem.at[3 + i])
        for i, (src, dst) in enumerate([(w_out_s, wo_s), (w_qkv_t, wq), (w_out_t, wo)])
    ]
    for load in loads:
        load.start()

    def norm(f):
        hs[f] = modulate(tok[f].astype(F32), mod_s)

    load_tok.wait()
    norm(2 * (1 - zh))
    norm(2 * (1 - zh) + 1)
    pl.semaphore_wait(barrier, 22)
    for j in range(2):
        remote(hs.at[2 * (1 - zh) + j], zbuf.at[j], gather_send, z_sem.at[j], zdev).start()
    for d in range(1, 8):
        pl.semaphore_signal(group_sem, inc=1, device_id=((frame + d) % 8, patch), device_id_type=MESH)
    norm(2 * zh)
    norm(2 * zh + 1)

    def along_x(chunk, source):
        for d in (2, 1, 3):
            xd = (x + d) % 4
            remote(chunk(xd // 2), full.at[source], gather_send, full_sem.at[source], (frame, zh * 8 + xd * 2 + core)).start()
        pltpu.make_async_copy(chunk(x // 2), full.at[source], full_sem.at[source]).start()

    along_x(lambda j: hs.at[2 * zh + j], patch)
    awide[...] = jnp.zeros_like(awide)
    for window in windows:
        window.wait()
    pack_weights(wbuf, packed, group)

    def arrived(source):
        pltpu.make_async_copy(full.at[source], full.at[source], full_sem.at[source]).wait()

    def chip(k, _):
        plane = (zh + k // 4) % 2
        step = 2 * (k % 4) - 3 * (k % 4 // 2)
        index = plane * 4 + (x + step) % 4
        source = index * 2 + core
        arrived(source)
        remote(full.at[source], full.at[source], gather_send, full_sem.at[source], sibling).start()
        arrived(index * 2 + 1 - core)
        h = full[pl.ds(index * 2, 2)].reshape(QT, D)
        project(h, packed, qk, vt, index)
        return 0

    chip(0, 0)
    for j in range(2):
        pltpu.make_async_copy(zbuf.at[j], zbuf.at[j], z_sem.at[j]).wait()
        for n in range(2):
            xd = 2 * j + n
            src, dst = zbuf.at[j], full.at[zpatch]

            @pl.when(xd != x)
            def _():
                remote(src, dst, gather_send, full_sem.at[zpatch], (frame, zh * 8 + xd * 2 + core)).start()

            @pl.when(xd == x)
            def _():
                pltpu.make_async_copy(src, dst, full_sem.at[zpatch]).start()

    lax.fori_loop(1, 5, chip, 0)

    def tokens_out(d, _):
        f = (frame + d) % 8
        remote(tok.at[:, rows16(f), :], tok_t.at[frame], tok_send, tok_recv, (f, patch)).start()
        return 0

    lax.fori_loop(1, 8, tokens_out, 0)
    pltpu.make_async_copy(tok.at[:, rows16(frame), :], tok_t.at[frame], tok_recv).start()

    scores, tops = (s0, s1), (m0, m1)

    def score(head, tile, slot, chunks):
        base = (head // 2) * 128
        rows = pl.ds(pl.multiple_of(tile * QT, QT), QT)
        keep = head_lanes((QT, 256), head)
        query = jnp.where(keep, qk[rows, base : base + 256], jnp.zeros((), BF))
        top = None
        for c, at_chunk in enumerate(chunks):
            keys = qk[pl.ds(pl.multiple_of(at_chunk * KC, KC), KC), WIN + base : WIN + base + 256]
            part = lax.dot_general(keys, query, (((1,), (1,)), ((), ())), preferred_element_type=F32)
            scores[slot][c * KC : (c + 1) * KC, :] = part
            part = jnp.max(part.reshape(KC // 8, 8, QT), axis=0)
            top = part if top is None else jnp.maximum(top, part)
        tops[slot][...] = jnp.broadcast_to(jnp.max(top, axis=0, keepdims=True), (8, QT))

    def sums(head, slot, chunks, top):
        acc = None
        for c, at_chunk in enumerate(chunks):
            probs = jnp.exp2(scores[slot][c * KC : (c + 1) * KC, :] - top).astype(BF)
            values = vt[head, :, pl.ds(pl.multiple_of(at_chunk * KC, KC), KC)]
            part = jnp.dot(values, probs, preferred_element_type=F32)
            acc = part if acc is None else acc + part
        return acc

    def keep_head(head, acc):
        awide[pl.ds(pl.multiple_of(32 * group + HD * head, 8), HD), :] = acc[:HD] / acc[HD : HD + 1]

    def send_tile(tile):
        att[pl.ds(pl.multiple_of(tile * QT, QT), QT), :] = awide[...].T.astype(BF)

        def go(n, _):
            f, p = n // 2, tile * 2 + n % 2
            src, dst = att.at[rows16(p * 8 + f), :], att_t.at[group, at]
            mine = (f == frame) & (p == patch)

            @pl.when(jnp.logical_not(mine))
            def _():
                remote(src, dst, att_send, att_recv, (f, p)).start()

            @pl.when(mine)
            def _():
                pltpu.make_async_copy(src, dst, att_recv).start()

            return 0

        lax.fori_loop(0, 16, go, 0)

    near = [zh * 4 + c for c in range(4)] + [(1 - zh) * 4 + x]
    far = [(1 - zh) * 4 + (x + d) % 4 for d in (2, 1, 3)]
    score(0, zh * 4 + x, 0, near)

    def first_part(i, _):
        for head in range(4):
            ahead = (x + i) % 4 if head < 3 else (x + i + 1) % 4
            score((head + 1) % 4, zh * 4 + ahead, (head + 1) % 2, near)
            slot = head % 2
            held[(x + i) % 4, head] = sums(head, slot, near, tops[slot][0:1, :])
            held_top[(x + i) % 4, head] = tops[slot][...]
        return 0

    lax.fori_loop(0, 4, first_part, 0)
    lax.fori_loop(5, 8, chip, 0)
    pl.semaphore_wait(group_sem, 7)
    score(0, zh * 4 + x, 0, far)

    def second_part(i, _):
        for head in range(4):
            ahead = (x + i) % 4 if head < 3 else (x + i + 1) % 4
            score((head + 1) % 4, zh * 4 + ahead, (head + 1) % 2, far)
            slot = head % 2
            before = held_top[(x + i) % 4, head, 0:1, :]
            top = jnp.maximum(tops[slot][0:1, :], before)
            acc = held[(x + i) % 4, head] * jnp.exp2(before - top)
            keep_head(head, acc + sums(head, slot, far, top))
        send_tile(zh * 4 + (x + i) % 4)
        return 0

    lax.fori_loop(0, 4, second_part, 0)
    score(0, (1 - zh) * 4 + x, 0, range(8))

    def other_tiles(i, _):
        for head in range(4):
            ahead = (x + i) % 4 if head < 3 else (x + i + 1) % 4
            score((head + 1) % 4, (1 - zh) * 4 + ahead, (head + 1) % 2, range(8))
            slot = head % 2
            keep_head(head, sums(head, slot, range(8), tops[slot][0:1, :]))
        send_tile((1 - zh) * 4 + (x + i) % 4)
        return 0

    lax.fori_loop(0, 4, other_tiles, 0)

    for load in loads:
        load.wait()
    pltpu.make_async_copy(tok_t, tok_t, tok_recv).wait()
    pltpu.make_async_copy(att_t, att_t, att_recv).wait()
    for tile in range(9):
        cols = slice(tile * 128, tile * 128 + 128)
        g, rest = min(tile // 2, 3), tile - 2 * min(tile // 2, 3)
        part = att_t[g, :, :, rest * 128 : rest * 128 + 128].reshape(512, 128)
        if rest == 0 and g > 0:
            part = part + att_t[g - 1, :, :, 256:384].reshape(512, 128)
        flat[:, cols] = part

    def finish_mid(i, _):
        rows = pl.ds(pl.multiple_of(i * 256, 256), 256)
        proj = jnp.dot(flat[rows, :], wo_s[...], preferred_element_type=F32)
        values = tok_t[pl.ds(i * 4, 4)].reshape(256, D).astype(F32)
        values = (values + mod_s[2:3, :] * proj).astype(BF)
        mid[pl.ds(i * 16, 16)] = values.astype(F32).reshape(16, 16, D)
        flat[rows, :] = modulate(values.astype(F32), mod_t)
        return 0

    lax.fori_loop(0, 2, finish_mid, 0)
    hp[...] = jnp.dot(to_patches(), flat[...], preferred_element_type=F32).astype(BF)

    row = lax.broadcasted_iota(jnp.int32, (128, 128), 0)
    col = lax.broadcasted_iota(jnp.int32, (128, 128), 1)
    same = row // 32 == col // 32
    lane = lax.broadcasted_iota(jnp.int32, (128, 256), 1)

    def four_patches(i, _):
        rows = pl.ds(pl.multiple_of(i * 128, 128), 128)
        tiles = [None] * 9
        for head in range(HEADS):
            tile = min(head * HD // 128, 7)
            base = tile * 128
            low = head * HD - base
            keep = (lane >= low) & (lane < low + HD)
            query = jnp.where(keep, qkv[rows, base : base + 256], jnp.zeros((), BF))
            keys = qkv[rows, D + base : D + base + 256]
            part = lax.dot_general(query, keys, (((1,), (1,)), ((), ())), preferred_element_type=F32)
            part = jnp.where(same, part, -1e30)
            expo = jnp.exp2(part - jnp.max(part, axis=-1, keepdims=True))
            probs = (expo / jnp.sum(expo, axis=-1, keepdims=True)).astype(BF)
            mixed = jnp.dot(probs, qkv[rows, 2 * D + base : 2 * D + base + 256], preferred_element_type=F32)
            for n in range(2):
                piece = mixed[:, n * 128 : n * 128 + 128]
                old = tiles[tile + n]
                tiles[tile + n] = piece if old is None else jnp.where(keep[:, n * 128 : n * 128 + 128], piece, old)
        for n in range(9):
            mixed_all[rows, n * 128 : n * 128 + 128] = tiles[n].astype(BF)
        return 0

    def eight_patches(n, _):
        rows = pl.ds(pl.multiple_of(n * 256, 256), 256)
        for cols in (slice(0, 768), slice(768, 1152), slice(1152, 1920), slice(1920, 2688), slice(2688, 3456)):
            acc = jnp.dot(hp[rows, :], wq[:, cols], preferred_element_type=F32)
            if cols.stop <= D:
                acc = acc * SCALE
            qkv[:, cols] = acc.astype(BF)
        lax.fori_loop(0, 2, four_patches, 0)
        ordered = jnp.dot(to_frames(), mixed_all[...], preferred_element_type=F32).astype(BF)
        proj = jnp.dot(ordered, wo[...], preferred_element_type=F32)
        values = mid[:, pl.ds(pl.multiple_of(n * 8, 8), 8), :].reshape(256, D)
        values = (values + mod_t[2:3, :] * proj).astype(BF)
        done[n] = values.reshape(8, 32, D)

        def go(d, _):
            f = (frame + d) % 8
            remote(done.at[n, f], out.at[n, frame], home_send, home_recv, (f, patch)).start()
            return 0

        lax.fori_loop(1, 8, go, 0)
        pltpu.make_async_copy(done.at[n, frame], out.at[n, frame], home_recv).start()
        return 0

    lax.fori_loop(0, 2, eight_patches, 0)
    pltpu.make_async_copy(full, full, gather_send).wait()
    pltpu.make_async_copy(tok_t.at[pl.ds(0, 7)], tok_t.at[pl.ds(0, 7)], tok_send).wait()
    pltpu.make_async_copy(att.at[pl.ds(0, 2032), :], att.at[pl.ds(0, 2032), :], att_send).wait()
    for n in range(2):
        pltpu.make_async_copy(done.at[n, pl.ds(0, 7)], done.at[n, pl.ds(0, 7)], home_send).wait()
    pltpu.make_async_copy(out, out, home_recv).wait()


def shards(tokens, w_qkv_s, w_out_s, mod_s, w_qkv_t, w_out_t, mod_t):
    dma = pltpu.SemaphoreType.DMA
    parts = pl.pallas_call(
        fused_kernel,
        name="blocks",
        out_shape=jax.ShapeDtypeStruct((2, 8, 32, D), BF),
        in_specs=[ANY, VMEM, VMEM, ANY, ANY, ANY, ANY],
        out_specs=ANY,
        scratch_shapes=[
            pltpu.VMEM((4, 128, D), BF),
            pltpu.VMEM((4, 128, D), BF),
            pltpu.VMEM((2, 128, D), BF),
            pltpu.VMEM((16, 128, D), BF),
            pltpu.VMEM((D, 3 * WIN), BF),
            pltpu.VMEM((D, 1024), BF),
            pltpu.VMEM((ROWS, 2 * WIN), BF),
            pltpu.VMEM((4, 80, ROWS), BF),
            pltpu.VMEM((ROWS, QT), F32),
            pltpu.VMEM((ROWS, QT), F32),
            pltpu.VMEM((8, QT), F32),
            pltpu.VMEM((8, QT), F32),
            pltpu.VMEM((4, 4, 80, QT), F32),
            pltpu.VMEM((4, 4, 8, QT), F32),
            pltpu.VMEM((WIN, QT), F32),
            pltpu.VMEM((ROWS, WIN), BF),
            pltpu.VMEM((4, 32, 16, WIN), BF),
            pltpu.VMEM((8, 4, 16, D), BF),
            pltpu.VMEM((D, D), BF),
            pltpu.VMEM((D, 3 * D), BF),
            pltpu.VMEM((D, D), BF),
            pltpu.VMEM((512, D), BF),
            pltpu.VMEM((32, 16, D), F32),
            pltpu.VMEM((512, D), BF),
            pltpu.VMEM((256, 3 * D), BF),
            pltpu.VMEM((256, D), BF),
            pltpu.VMEM((2, 8, 32, D), BF),
            dma,
            dma((6,)),
            dma((2,)),
            dma((16,)),
            dma,
            dma,
            dma,
            dma,
            dma,
            dma,
            dma,
            pltpu.SemaphoreType.REGULAR,
        ],
        compiler_params=params(1),
    )(tokens, mod_s, mod_t, w_qkv_s, w_out_s, w_qkv_t, w_out_t)
    return parts.reshape(2, 8, 4, 8, D).transpose(2, 1, 0, 3, 4).reshape(4, 128, D)


def solution(mesh):
    return jax.shard_map(
        shards,
        mesh=mesh,
        in_specs=(P("frame", "patch", None), P(), P(), P(), P(), P(), P()),
        out_specs=P("frame", "patch", None),
        check_vma=False,
    )
```

```python
import functools

import jax
import jax.numpy as jnp
from jax import lax
from jax.experimental import pallas as pl
from jax.experimental.pallas import tpu as pltpu
from jax.sharding import PartitionSpec as P

HEADS = 16
HD = 72
D = 1152
WIN = 384
ROWS = 2048
QT = 256
KC = 256
SCALE = HD ** (-0.5) * 1.4426950408889634
MESH = pl.DeviceIdType.MESH
VMEM = pl.BlockSpec(memory_space=pltpu.VMEM)
ANY = pl.BlockSpec(memory_space=pl.ANY)
BF = jnp.bfloat16
F32 = jnp.float32


def params(collective_id=None):
    return pltpu.CompilerParams(
        collective_id=collective_id,
        has_side_effects=collective_id is not None,
        vmem_limit_bytes=56 * 2**20,
    )


def remote(src, dst, send_sem, recv_sem, device):
    return pltpu.make_async_remote_copy(
        src_ref=src, dst_ref=dst, send_sem=send_sem, recv_sem=recv_sem, device_id=device, device_id_type=MESH
    )


def modulate(values, mod_ref):
    mean = jnp.mean(values, axis=-1, keepdims=True)
    centered = values - mean
    var = jnp.mean(centered * centered, axis=-1, keepdims=True)
    return (centered * lax.rsqrt(var + 1e-06) * (1.0 + mod_ref[1:2, :]) + mod_ref[0:1, :]).astype(BF)


def place():
    frame, patch = lax.axis_index("frame"), lax.axis_index("patch")
    return frame, patch, patch // 8, (patch // 2) % 4, patch % 2


def rows16(index):
    return pl.ds(pl.multiple_of(index * 16, 16), 16)


def head_lanes(shape, head):
    lane = lax.broadcasted_iota(jnp.int32, shape, 1) + (head // 2) * 128
    return (lane >= HD * head) & (lane < HD * head + HD)


def pack_weights(wbuf, packed, group):
    row = lax.broadcasted_iota(jnp.int32, (2 * WIN, 640), 0)
    col = lax.broadcasted_iota(jnp.int32, (2 * WIN, 640), 1)
    width = 4 * HD
    target = jnp.where(col < width, col, col + (WIN - width)) + 32 * group
    pick = jnp.where((row == target) & (col < 2 * width), 1.0, 0.0).astype(BF)
    row = lax.broadcasted_iota(jnp.int32, (WIN, WIN), 0)
    col = lax.broadcasted_iota(jnp.int32, (WIN, WIN), 1)
    first = jnp.where((row == col + 32 * group) & (col < width), 1.0, 0.0).astype(BF)

    def some(i, _):
        rows = pl.ds(pl.multiple_of(i * 384, 384), 384)
        packed[rows, :WIN] = jnp.dot(wbuf[rows, :WIN], first, preferred_element_type=F32).astype(BF)
        packed[rows, WIN:] = jnp.dot(wbuf[rows, WIN:], pick, preferred_element_type=F32).astype(BF)
        return 0

    lax.fori_loop(0, 3, some, 0)


def project(h, packed, qk, vt, index):
    rows = pl.ds(pl.multiple_of(index * QT, QT), QT)
    acc = jnp.dot(h, packed[...], preferred_element_type=F32)
    qk[rows, :WIN] = (acc[:, :WIN] * SCALE).astype(BF)
    qk[rows, WIN:] = acc[:, WIN : 2 * WIN].astype(BF)
    values = acc[:, 640:1024].T
    one = jnp.where(lax.broadcasted_iota(jnp.int32, (8, QT), 0) == 0, 1.0, 0.0)
    for head in range(4):
        part = values[32 + HD * head : 32 + HD * head + HD, :]
        vt[head, :, rows] = jnp.concatenate([part, one], axis=0).astype(BF)


def load_window(w, wbuf, sems, group):
    copies = []
    for part in range(3):
        cols = pl.ds(pl.multiple_of(part * D + 256 * group, 128), WIN)
        copies.append(pltpu.make_async_copy(w.at[:, cols], wbuf.at[:, pl.ds(part * WIN, WIN)], sems.at[part]))
        copies[-1].start()
    return copies


def to_patches():
    row = lax.broadcasted_iota(jnp.int32, (512, 512), 0)
    col = lax.broadcasted_iota(jnp.int32, (512, 512), 1)
    return jnp.where(col == (row % 32) * 16 + row // 32, 1.0, 0.0).astype(BF)


def to_frames():
    row = lax.broadcasted_iota(jnp.int32, (256, 256), 0)
    col = lax.broadcasted_iota(jnp.int32, (256, 256), 1)
    return jnp.where(col == (row % 8) * 32 + row // 8, 1.0, 0.0).astype(BF)


def fused_kernel(
    tok_hbm, mod_s, mod_t, w_qkv_s, w_out_s, w_qkv_t, w_out_t, out,
    tok, hs, zbuf, full, wbuf, packed, qk, vt, s0, s1, m0, m1, held, held_top, awide, att, att_t, tok_t, wo_s, wq, wo,
    flat, mid, hp, qkv, mixed_all, done,
    tok_sem, w_sem, z_sem, full_sem, gather_send, tok_send, tok_recv, att_send, att_recv, home_send, home_recv, group_sem,
):
    frame, patch, zh, x, core = place()
    group = (x % 2) * 2 + core
    at = frame * 4 + zh * 2 + x // 2
    zpatch = (1 - zh) * 8 + x * 2 + core
    sibling = (frame, patch + 1 - 2 * core)
    zdev = (frame, zpatch)

    barrier = pltpu.get_barrier_semaphore()

    for d in range(1, 16):
        pl.semaphore_signal(barrier, inc=1, device_id=(frame, (patch + d) % 16), device_id_type=MESH)
    for d in range(1, 8):
        pl.semaphore_signal(barrier, inc=1, device_id=((frame + d) % 8, patch), device_id_type=MESH)
    load_tok = pltpu.make_async_copy(tok_hbm, tok, tok_sem)
    load_tok.start()
    windows = load_window(w_qkv_s, wbuf, w_sem, group)
    loads = [
        pltpu.make_async_copy(src, dst, w_sem.at[3 + i])
        for i, (src, dst) in enumerate([(w_out_s, wo_s), (w_qkv_t, wq), (w_out_t, wo)])
    ]
    for load in loads:
        load.start()

    def norm(f):
        hs[f] = modulate(tok[f].astype(F32), mod_s)

    load_tok.wait()
    norm(2 * (1 - zh))
    norm(2 * (1 - zh) + 1)
    pl.semaphore_wait(barrier, 22)
    for j in range(2):
        remote(hs.at[2 * (1 - zh) + j], zbuf.at[j], gather_send, z_sem.at[j], zdev).start()
    for d in range(1, 8):
        pl.semaphore_signal(group_sem, inc=1, device_id=((frame + d) % 8, patch), device_id_type=MESH)
    norm(2 * zh)
    norm(2 * zh + 1)

    def along_x(chunk, source):
        for d in (2, 1, 3):
            xd = (x + d) % 4
            remote(chunk(xd // 2), full.at[source], gather_send, full_sem.at[source], (frame, zh * 8 + xd * 2 + core)).start()
        pltpu.make_async_copy(chunk(x // 2), full.at[source], full_sem.at[source]).start()

    along_x(lambda j: hs.at[2 * zh + j], patch)
    awide[...] = jnp.zeros_like(awide)
    for window in windows:
        window.wait()
    pack_weights(wbuf, packed, group)

    def arrived(source):
        pltpu.make_async_copy(full.at[source], full.at[source], full_sem.at[source]).wait()

    def chip_of(k):
        return ((zh + k // 4) % 2) * 4 + (x + 2 * (k % 4) - 3 * (k % 4 // 2)) % 4

    def relay(k, _):
        source = chip_of(k) * 2 + core
        arrived(source)
        remote(full.at[source], full.at[source], gather_send, full_sem.at[source], sibling).start()
        return 0

    def chip(k, _):
        index = chip_of(k)
        arrived(index * 2 + 1 - core)
        h = full[pl.ds(index * 2, 2)].reshape(QT, D)
        project(h, packed, qk, vt, index)
        return 0

    def token_out(f):
        remote(tok.at[:, rows16(f), :], tok_t.at[frame], tok_send, tok_recv, (f, patch)).start()

    for d in (2, 4, 6):
        token_out((frame + d) % 8)
    pltpu.make_async_copy(tok.at[:, rows16(frame), :], tok_t.at[frame], tok_recv).start()
    relay(0, 0)
    chip(0, 0)
    for j in range(2):
        pltpu.make_async_copy(zbuf.at[j], zbuf.at[j], z_sem.at[j]).wait()
        for n in range(2):
            xd = 2 * j + n
            src, dst = zbuf.at[j], full.at[zpatch]

            @pl.when(xd != x)
            def _():
                remote(src, dst, gather_send, full_sem.at[zpatch], (frame, zh * 8 + xd * 2 + core)).start()

            @pl.when(xd == x)
            def _():
                pltpu.make_async_copy(src, dst, full_sem.at[zpatch]).start()

    lax.fori_loop(1, 5, relay, 0)
    for d in (1, 3, 5, 7):
        token_out((frame + d) % 8)
    lax.fori_loop(1, 5, chip, 0)


    scores, tops = (s0, s1), (m0, m1)

    def score(head, tile, slot, chunks):
        base = (head // 2) * 128
        rows = pl.ds(pl.multiple_of(tile * QT, QT), QT)
        keep = head_lanes((QT, 256), head)
        query = jnp.where(keep, qk[rows, base : base + 256], jnp.zeros((), BF))
        top = None
        for c, at_chunk in enumerate(chunks):
            keys = qk[pl.ds(pl.multiple_of(at_chunk * KC, KC), KC), WIN + base : WIN + base + 256]
            part = lax.dot_general(keys, query, (((1,), (1,)), ((), ())), preferred_element_type=F32)
            scores[slot][c * KC : (c + 1) * KC, :] = part
            part = jnp.max(part.reshape(KC // 8, 8, QT), axis=0)
            top = part if top is None else jnp.maximum(top, part)
        tops[slot][...] = jnp.broadcast_to(jnp.max(top, axis=0, keepdims=True), (8, QT))

    def sums(head, slot, chunks, top):
        acc = None
        for c, at_chunk in enumerate(chunks):
            probs = jnp.exp2(scores[slot][c * KC : (c + 1) * KC, :] - top).astype(BF)
            values = vt[head, :, pl.ds(pl.multiple_of(at_chunk * KC, KC), KC)]
            part = jnp.dot(values, probs, preferred_element_type=F32)
            acc = part if acc is None else acc + part
        return acc

    def keep_head(head, acc):
        awide[pl.ds(pl.multiple_of(32 * group + HD * head, 8), HD), :] = acc[:HD] / acc[HD : HD + 1]

    def send_tile(tile):
        att[pl.ds(pl.multiple_of(tile * QT, QT), QT), :] = awide[...].T.astype(BF)

        def go(n, _):
            f, p = (frame + n // 2) % 8, tile * 2 + n % 2
            src, dst = att.at[rows16(p * 8 + f), :], att_t.at[group, at]
            mine = (f == frame) & (p == patch)

            @pl.when(jnp.logical_not(mine))
            def _():
                remote(src, dst, att_send, att_recv, (f, p)).start()

            @pl.when(mine)
            def _():
                pltpu.make_async_copy(src, dst, att_recv).start()

            return 0

        lax.fori_loop(0, 16, go, 0)

    near = [zh * 4 + c for c in range(4)] + [(1 - zh) * 4 + x]
    far = [(1 - zh) * 4 + (x + d) % 4 for d in (2, 1, 3)]
    score(0, zh * 4 + x, 0, near)

    def first_part(i, _):
        for head in range(4):
            ahead = (x + i) % 4 if head < 3 else (x + i + 1) % 4
            score((head + 1) % 4, zh * 4 + ahead, (head + 1) % 2, near)
            slot = head % 2
            held[(x + i) % 4, head] = sums(head, slot, near, tops[slot][0:1, :])
            held_top[(x + i) % 4, head] = tops[slot][...]
        return 0

    lax.fori_loop(0, 4, first_part, 0)
    lax.fori_loop(5, 8, relay, 0)
    lax.fori_loop(5, 8, chip, 0)
    pl.semaphore_wait(group_sem, 7)
    score(0, (1 - zh) * 4 + x, 0, range(8))

    def other_tiles(i, _):
        for head in range(4):
            ahead = (x + i) % 4 if head < 3 else (x + i + 1) % 4
            score((head + 1) % 4, (1 - zh) * 4 + ahead, (head + 1) % 2, range(8))
            slot = head % 2
            keep_head(head, sums(head, slot, range(8), tops[slot][0:1, :]))
        send_tile((1 - zh) * 4 + (x + i) % 4)
        return 0

    lax.fori_loop(0, 4, other_tiles, 0)
    score(0, zh * 4 + x, 0, far)

    def second_part(i, _):
        for head in range(4):
            ahead = (x + i) % 4 if head < 3 else (x + i + 1) % 4
            score((head + 1) % 4, zh * 4 + ahead, (head + 1) % 2, far)
            slot = head % 2
            before = held_top[(x + i) % 4, head, 0:1, :]
            top = jnp.maximum(tops[slot][0:1, :], before)
            acc = held[(x + i) % 4, head] * jnp.exp2(before - top)
            keep_head(head, acc + sums(head, slot, far, top))
        send_tile(zh * 4 + (x + i) % 4)
        return 0

    lax.fori_loop(0, 4, second_part, 0)

    for load in loads:
        load.wait()
    pltpu.make_async_copy(tok_t, tok_t, tok_recv).wait()
    pltpu.make_async_copy(att_t, att_t, att_recv).wait()
    for tile in range(9):
        cols = slice(tile * 128, tile * 128 + 128)
        g, rest = min(tile // 2, 3), tile - 2 * min(tile // 2, 3)
        part = att_t[g, :, :, rest * 128 : rest * 128 + 128].reshape(512, 128)
        if rest == 0 and g > 0:
            part = part + att_t[g - 1, :, :, 256:384].reshape(512, 128)
        flat[:, cols] = part

    def finish_mid(i, _):
        rows = pl.ds(pl.multiple_of(i * 256, 256), 256)
        proj = jnp.dot(flat[rows, :], wo_s[...], preferred_element_type=F32)
        values = tok_t[pl.ds(i * 4, 4)].reshape(256, D).astype(F32)
        values = (values + mod_s[2:3, :] * proj).astype(BF)
        mid[pl.ds(i * 16, 16)] = values.astype(F32).reshape(16, 16, D)
        flat[rows, :] = modulate(values.astype(F32), mod_t)
        return 0

    lax.fori_loop(0, 2, finish_mid, 0)
    hp[...] = jnp.dot(to_patches(), flat[...], preferred_element_type=F32).astype(BF)

    row = lax.broadcasted_iota(jnp.int32, (128, 128), 0)
    col = lax.broadcasted_iota(jnp.int32, (128, 128), 1)
    same = row // 32 == col // 32
    lane = lax.broadcasted_iota(jnp.int32, (128, 256), 1)

    def four_patches(i, _):
        rows = pl.ds(pl.multiple_of(i * 128, 128), 128)
        tiles = [None] * 9
        for head in range(HEADS):
            tile = min(head * HD // 128, 7)
            base = tile * 128
            low = head * HD - base
            keep = (lane >= low) & (lane < low + HD)
            query = jnp.where(keep, qkv[rows, base : base + 256], jnp.zeros((), BF))
            keys = qkv[rows, D + base : D + base + 256]
            part = lax.dot_general(query, keys, (((1,), (1,)), ((), ())), preferred_element_type=F32)
            part = jnp.where(same, part, -1e30)
            expo = jnp.exp2(part - jnp.max(part, axis=-1, keepdims=True))
            probs = (expo / jnp.sum(expo, axis=-1, keepdims=True)).astype(BF)
            mixed = jnp.dot(probs, qkv[rows, 2 * D + base : 2 * D + base + 256], preferred_element_type=F32)
            for n in range(2):
                piece = mixed[:, n * 128 : n * 128 + 128]
                old = tiles[tile + n]
                tiles[tile + n] = piece if old is None else jnp.where(keep[:, n * 128 : n * 128 + 128], piece, old)
        for n in range(9):
            mixed_all[rows, n * 128 : n * 128 + 128] = tiles[n].astype(BF)
        return 0

    def eight_patches(n, _):
        rows = pl.ds(pl.multiple_of(n * 256, 256), 256)
        for cols in (slice(0, 768), slice(768, 1152), slice(1152, 1920), slice(1920, 2688), slice(2688, 3456)):
            acc = jnp.dot(hp[rows, :], wq[:, cols], preferred_element_type=F32)
            if cols.stop <= D:
                acc = acc * SCALE
            qkv[:, cols] = acc.astype(BF)
        lax.fori_loop(0, 2, four_patches, 0)
        ordered = jnp.dot(to_frames(), mixed_all[...], preferred_element_type=F32).astype(BF)
        proj = jnp.dot(ordered, wo[...], preferred_element_type=F32)
        values = mid[:, pl.ds(pl.multiple_of(n * 8, 8), 8), :].reshape(256, D)
        values = (values + mod_t[2:3, :] * proj).astype(BF)
        done[n] = values.reshape(8, 32, D)

        def go(d, _):
            f = (frame + d) % 8
            remote(done.at[n, f], out.at[n, frame], home_send, home_recv, (f, patch)).start()
            return 0

        lax.fori_loop(1, 8, go, 0)
        pltpu.make_async_copy(done.at[n, frame], out.at[n, frame], home_recv).start()
        return 0

    lax.fori_loop(0, 2, eight_patches, 0)
    pltpu.make_async_copy(full, full, gather_send).wait()
    pltpu.make_async_copy(tok_t.at[pl.ds(0, 7)], tok_t.at[pl.ds(0, 7)], tok_send).wait()
    pltpu.make_async_copy(att.at[pl.ds(0, 2032), :], att.at[pl.ds(0, 2032), :], att_send).wait()
    for n in range(2):
        pltpu.make_async_copy(done.at[n, pl.ds(0, 7)], done.at[n, pl.ds(0, 7)], home_send).wait()
    pltpu.make_async_copy(out, out, home_recv).wait()


def shards(tokens, w_qkv_s, w_out_s, mod_s, w_qkv_t, w_out_t, mod_t):
    dma = pltpu.SemaphoreType.DMA
    parts = pl.pallas_call(
        fused_kernel,
        name="blocks",
        out_shape=jax.ShapeDtypeStruct((2, 8, 32, D), BF),
        in_specs=[ANY, VMEM, VMEM, ANY, ANY, ANY, ANY],
        out_specs=ANY,
        scratch_shapes=[
            pltpu.VMEM((4, 128, D), BF),
            pltpu.VMEM((4, 128, D), BF),
            pltpu.VMEM((2, 128, D), BF),
            pltpu.VMEM((16, 128, D), BF),
            pltpu.VMEM((D, 3 * WIN), BF),
            pltpu.VMEM((D, 1024), BF),
            pltpu.VMEM((ROWS, 2 * WIN), BF),
            pltpu.VMEM((4, 80, ROWS), BF),
            pltpu.VMEM((ROWS, QT), F32),
            pltpu.VMEM((ROWS, QT), F32),
            pltpu.VMEM((8, QT), F32),
            pltpu.VMEM((8, QT), F32),
            pltpu.VMEM((4, 4, 80, QT), F32),
            pltpu.VMEM((4, 4, 8, QT), F32),
            pltpu.VMEM((WIN, QT), F32),
            pltpu.VMEM((ROWS, WIN), BF),
            pltpu.VMEM((4, 32, 16, WIN), BF),
            pltpu.VMEM((8, 4, 16, D), BF),
            pltpu.VMEM((D, D), BF),
            pltpu.VMEM((D, 3 * D), BF),
            pltpu.VMEM((D, D), BF),
            pltpu.VMEM((512, D), BF),
            pltpu.VMEM((32, 16, D), F32),
            pltpu.VMEM((512, D), BF),
            pltpu.VMEM((256, 3 * D), BF),
            pltpu.VMEM((256, D), BF),
            pltpu.VMEM((2, 8, 32, D), BF),
            dma,
            dma((6,)),
            dma((2,)),
            dma((16,)),
            dma,
            dma,
            dma,
            dma,
            dma,
            dma,
            dma,
            pltpu.SemaphoreType.REGULAR,
        ],
        compiler_params=params(1),
    )(tokens, mod_s, mod_t, w_qkv_s, w_out_s, w_qkv_t, w_out_t)
    return parts.reshape(2, 8, 4, 8, D).transpose(2, 1, 0, 3, 4).reshape(4, 128, D)


def solution(mesh):
    return jax.shard_map(
        shards,
        mesh=mesh,
        in_specs=(P("frame", "patch", None), P(), P(), P(), P(), P(), P()),
        out_specs=P("frame", "patch", None),
        check_vma=False,
    )
```

```python
import functools

import jax
import jax.numpy as jnp
from jax import lax
from jax.experimental import pallas as pl
from jax.experimental.pallas import tpu as pltpu
from jax.sharding import PartitionSpec as P

HEADS = 16
HD = 72
D = 1152
WIN = 384
ROWS = 2048
QT = 256
KC = 256
SCALE = HD ** (-0.5) * 1.4426950408889634
MESH = pl.DeviceIdType.MESH
VMEM = pl.BlockSpec(memory_space=pltpu.VMEM)
ANY = pl.BlockSpec(memory_space=pl.ANY)
BF = jnp.bfloat16
F32 = jnp.float32


def params(collective_id=None):
    return pltpu.CompilerParams(
        collective_id=collective_id,
        has_side_effects=collective_id is not None,
        vmem_limit_bytes=56 * 2**20,
    )


def remote(src, dst, send_sem, recv_sem, device):
    return pltpu.make_async_remote_copy(
        src_ref=src, dst_ref=dst, send_sem=send_sem, recv_sem=recv_sem, device_id=device, device_id_type=MESH
    )


def modulate(values, mod_ref):
    mean = jnp.mean(values, axis=-1, keepdims=True)
    centered = values - mean
    var = jnp.mean(centered * centered, axis=-1, keepdims=True)
    return (centered * lax.rsqrt(var + 1e-06) * (1.0 + mod_ref[1:2, :]) + mod_ref[0:1, :]).astype(BF)


def place():
    frame, patch = lax.axis_index("frame"), lax.axis_index("patch")
    return frame, patch, patch // 8, (patch // 2) % 4, patch % 2


def rows16(index):
    return pl.ds(pl.multiple_of(index * 16, 16), 16)


def head_lanes(shape, head):
    lane = lax.broadcasted_iota(jnp.int32, shape, 1) + (head // 2) * 128
    return (lane >= HD * head) & (lane < HD * head + HD)


def pack_weights(wbuf, packed, group):
    row = lax.broadcasted_iota(jnp.int32, (2 * WIN, 640), 0)
    col = lax.broadcasted_iota(jnp.int32, (2 * WIN, 640), 1)
    width = 4 * HD
    target = jnp.where(col < width, col, col + (WIN - width)) + 32 * group
    pick = jnp.where((row == target) & (col < 2 * width), 1.0, 0.0).astype(BF)
    row = lax.broadcasted_iota(jnp.int32, (WIN, WIN), 0)
    col = lax.broadcasted_iota(jnp.int32, (WIN, WIN), 1)
    first = jnp.where((row == col + 32 * group) & (col < width), 1.0, 0.0).astype(BF)

    def some(i, _):
        rows = pl.ds(pl.multiple_of(i * 384, 384), 384)
        packed[rows, :WIN] = jnp.dot(wbuf[rows, :WIN], first, preferred_element_type=F32).astype(BF)
        packed[rows, WIN:] = jnp.dot(wbuf[rows, WIN:], pick, preferred_element_type=F32).astype(BF)
        return 0

    lax.fori_loop(0, 3, some, 0)


def project(h, packed, qk, vt, index):
    rows = pl.ds(pl.multiple_of(index * QT, QT), QT)
    acc = jnp.dot(h, packed[...], preferred_element_type=F32)
    qk[rows, :WIN] = (acc[:, :WIN] * SCALE).astype(BF)
    qk[rows, WIN:] = acc[:, WIN : 2 * WIN].astype(BF)
    values = acc[:, 640:1024].T
    one = jnp.where(lax.broadcasted_iota(jnp.int32, (8, QT), 0) == 0, 1.0, 0.0)
    for head in range(4):
        part = values[32 + HD * head : 32 + HD * head + HD, :]
        vt[head, :, rows] = jnp.concatenate([part, one], axis=0).astype(BF)


def load_window(w, wbuf, sems, group):
    copies = []
    for part in range(3):
        cols = pl.ds(pl.multiple_of(part * D + 256 * group, 128), WIN)
        copies.append(pltpu.make_async_copy(w.at[:, cols], wbuf.at[:, pl.ds(part * WIN, WIN)], sems.at[part]))
        copies[-1].start()
    return copies


def to_patches():
    row = lax.broadcasted_iota(jnp.int32, (512, 512), 0)
    col = lax.broadcasted_iota(jnp.int32, (512, 512), 1)
    return jnp.where(col == (row % 32) * 16 + row // 32, 1.0, 0.0).astype(BF)


def to_frames():
    row = lax.broadcasted_iota(jnp.int32, (256, 256), 0)
    col = lax.broadcasted_iota(jnp.int32, (256, 256), 1)
    return jnp.where(col == (row % 8) * 32 + row // 8, 1.0, 0.0).astype(BF)


def fused_kernel(
    tok_hbm, mod_s, mod_t, w_qkv_s, w_out_s, w_qkv_t, w_out_t, out,
    tok, hs, zbuf, full, wbuf, packed, qk, vt, s0, s1, m0, m1, held, held_top, awide, att, att_t, tok_t, wo_s, wq, wo,
    flat, mid, hp, qkv, mixed_all, done,
    tok_sem, w_sem, z_sem, full_sem, gather_send, tok_send, tok_recv, att_send, att_recv, home_send, home_recv, group_sem,
):
    frame, patch, zh, x, core = place()
    group = (x % 2) * 2 + core
    at = frame * 4 + zh * 2 + x // 2
    zpatch = (1 - zh) * 8 + x * 2 + core
    sibling = (frame, patch + 1 - 2 * core)
    zdev = (frame, zpatch)

    barrier = pltpu.get_barrier_semaphore()

    for d in range(1, 16):
        pl.semaphore_signal(barrier, inc=1, device_id=(frame, (patch + d) % 16), device_id_type=MESH)
    for d in range(1, 8):
        pl.semaphore_signal(barrier, inc=1, device_id=((frame + d) % 8, patch), device_id_type=MESH)
    load_tok = pltpu.make_async_copy(tok_hbm, tok, tok_sem)
    load_tok.start()
    windows = load_window(w_qkv_s, wbuf, w_sem, group)
    loads = [
        pltpu.make_async_copy(src, dst, w_sem.at[3 + i])
        for i, (src, dst) in enumerate([(w_out_s, wo_s), (w_qkv_t, wq), (w_out_t, wo)])
    ]
    for load in loads:
        load.start()

    def norm(f):
        hs[f] = modulate(tok[f].astype(F32), mod_s)

    load_tok.wait()
    norm(2 * (1 - zh))
    norm(2 * (1 - zh) + 1)
    pl.semaphore_wait(barrier, 22)
    for j in range(2):
        remote(hs.at[2 * (1 - zh) + j], zbuf.at[j], gather_send, z_sem.at[j], zdev).start()
    for d in range(1, 8):
        pl.semaphore_signal(group_sem, inc=1, device_id=((frame + d) % 8, patch), device_id_type=MESH)
    norm(2 * zh)
    norm(2 * zh + 1)

    def along_x(chunk, source):
        for d in (2, 1, 3):
            xd = (x + d) % 4
            remote(chunk(xd // 2), full.at[source], gather_send, full_sem.at[source], (frame, zh * 8 + xd * 2 + core)).start()
        pltpu.make_async_copy(chunk(x // 2), full.at[source], full_sem.at[source]).start()

    along_x(lambda j: hs.at[2 * zh + j], patch)
    awide[...] = jnp.zeros_like(awide)
    for window in windows:
        window.wait()
    pack_weights(wbuf, packed, group)

    def arrived(source):
        pltpu.make_async_copy(full.at[source], full.at[source], full_sem.at[source]).wait()

    def chip_of(k):
        return ((zh + k // 4) % 2) * 4 + (x + 2 * (k % 4) - 3 * (k % 4 // 2)) % 4

    def relay(k, _):
        source = chip_of(k) * 2 + core
        arrived(source)
        remote(full.at[source], full.at[source], gather_send, full_sem.at[source], sibling).start()
        return 0

    def chip(k, _):
        index = chip_of(k)
        arrived(index * 2 + 1 - core)
        h = full[pl.ds(index * 2, 2)].reshape(QT, D)
        project(h, packed, qk, vt, index)
        return 0

    def token_out(f):
        remote(tok.at[:, rows16(f), :], tok_t.at[frame], tok_send, tok_recv, (f, patch)).start()

    for d in (2, 4, 6):
        token_out((frame + d) % 8)
    pltpu.make_async_copy(tok.at[:, rows16(frame), :], tok_t.at[frame], tok_recv).start()
    relay(0, 0)
    chip(0, 0)
    for j in range(2):
        pltpu.make_async_copy(zbuf.at[j], zbuf.at[j], z_sem.at[j]).wait()
        for n in range(2):
            xd = 2 * j + n
            src, dst = zbuf.at[j], full.at[zpatch]

            @pl.when(xd != x)
            def _():
                remote(src, dst, gather_send, full_sem.at[zpatch], (frame, zh * 8 + xd * 2 + core)).start()

            @pl.when(xd == x)
            def _():
                pltpu.make_async_copy(src, dst, full_sem.at[zpatch]).start()

    lax.fori_loop(1, 5, relay, 0)
    for d in (1, 3, 5, 7):
        token_out((frame + d) % 8)
    lax.fori_loop(1, 5, chip, 0)


    scores, tops = (s0, s1), (m0, m1)

    def score(head, tile, slot, chunks):
        base = (head // 2) * 128
        rows = pl.ds(pl.multiple_of(tile * QT, QT), QT)
        keep = head_lanes((QT, 256), head)
        query = jnp.where(keep, qk[rows, base : base + 256], jnp.zeros((), BF))
        top = None
        for c, at_chunk in enumerate(chunks):
            keys = qk[pl.ds(pl.multiple_of(at_chunk * KC, KC), KC), WIN + base : WIN + base + 256]
            part = lax.dot_general(keys, query, (((1,), (1,)), ((), ())), preferred_element_type=F32)
            scores[slot][c * KC : (c + 1) * KC, :] = part
            part = jnp.max(part.reshape(KC // 8, 8, QT), axis=0)
            top = part if top is None else jnp.maximum(top, part)
        tops[slot][...] = jnp.broadcast_to(jnp.max(top, axis=0, keepdims=True), (8, QT))

    def sums(head, slot, chunks, top):
        acc = None
        for c, at_chunk in enumerate(chunks):
            probs = jnp.exp2(scores[slot][c * KC : (c + 1) * KC, :] - top).astype(BF)
            values = vt[head, :, pl.ds(pl.multiple_of(at_chunk * KC, KC), KC)]
            part = jnp.dot(values, probs, preferred_element_type=F32)
            acc = part if acc is None else acc + part
        return acc

    def keep_head(head, acc):
        awide[pl.ds(pl.multiple_of(32 * group + HD * head, 8), HD), :] = acc[:HD] / acc[HD : HD + 1]

    def store_tile(tile):
        att[pl.ds(pl.multiple_of(tile * QT, QT), QT), :] = awide[...].T.astype(BF)

    def send_quarter(tile, quarter, own=False):
        for n in range(4):
            d = quarter * 2 + n // 2
            f, p = (frame + d) % 8, tile * 2 + n % 2
            if own:
                p = patch if n % 2 == 0 else sibling[1]
            src, dst = att.at[rows16(p * 8 + f), :], att_t.at[group, at]
            if own and d == 0 and n % 2 == 0:
                pltpu.make_async_copy(src, dst, att_recv).start()
            else:
                remote(src, dst, att_send, att_recv, (f, p)).start()

    near = [zh * 4 + c for c in range(4)] + [(1 - zh) * 4 + x]
    far = [(1 - zh) * 4 + (x + d) % 4 for d in (2, 1, 3)]
    score(0, zh * 4 + x, 0, near)

    def first_part(i, _):
        for head in range(4):
            ahead = (x + i) % 4 if head < 3 else (x + i + 1) % 4
            score((head + 1) % 4, zh * 4 + ahead, (head + 1) % 2, near)
            slot = head % 2
            held[(x + i) % 4, head] = sums(head, slot, near, tops[slot][0:1, :])
            held_top[(x + i) % 4, head] = tops[slot][...]
        return 0

    lax.fori_loop(0, 4, first_part, 0)
    lax.fori_loop(5, 8, relay, 0)
    lax.fori_loop(5, 8, chip, 0)
    pl.semaphore_wait(group_sem, 7)

    def far_tile(i):
        return (1 - zh) * 4 + (x + i) % 4

    def own_tile(i):
        return zh * 4 + (x + 1 + i) % 4

    def other_tile(i, previous):
        for head in range(4):
            if previous is not None:
                send_quarter(previous, head)
            score((head + 1) % 4, far_tile(i if head < 3 else i + 1), (head + 1) % 2, range(8))
            slot = head % 2
            keep_head(head, sums(head, slot, range(8), tops[slot][0:1, :]))
        store_tile(far_tile(i))

    def other_tiles(i, _):
        other_tile(i, far_tile(i - 1))
        return 0

    def second_part(i, previous):
        for head in range(4):
            send_quarter(previous, head)
            score((head + 1) % 4, own_tile(i if head < 3 else i + 1), (head + 1) % 2, far)
            slot = head % 2
            place = own_tile(i) - zh * 4
            before = held_top[place, head, 0:1, :]
            top = jnp.maximum(tops[slot][0:1, :], before)
            acc = held[place, head] * jnp.exp2(before - top)
            keep_head(head, acc + sums(head, slot, far, top))
        store_tile(own_tile(i))

    def second_parts(i, _):
        second_part(i, own_tile(i - 1))
        return 0

    score(0, far_tile(0), 0, range(8))
    other_tile(0, None)
    lax.fori_loop(1, 4, other_tiles, 0)
    score(0, own_tile(0), 0, far)
    second_part(0, far_tile(3))
    lax.fori_loop(1, 4, second_parts, 0)
    for quarter in range(4):
        send_quarter(own_tile(3), quarter, own=True)

    for load in loads:
        load.wait()
    pltpu.make_async_copy(tok_t, tok_t, tok_recv).wait()
    pltpu.make_async_copy(att_t, att_t, att_recv).wait()
    for tile in range(9):
        cols = slice(tile * 128, tile * 128 + 128)
        g, rest = min(tile // 2, 3), tile - 2 * min(tile // 2, 3)
        part = att_t[g, :, :, rest * 128 : rest * 128 + 128].reshape(512, 128)
        if rest == 0 and g > 0:
            part = part + att_t[g - 1, :, :, 256:384].reshape(512, 128)
        flat[:, cols] = part

    def finish_mid(i, _):
        rows = pl.ds(pl.multiple_of(i * 256, 256), 256)
        proj = jnp.dot(flat[rows, :], wo_s[...], preferred_element_type=F32)
        values = tok_t[pl.ds(i * 4, 4)].reshape(256, D).astype(F32)
        values = (values + mod_s[2:3, :] * proj).astype(BF)
        mid[pl.ds(i * 16, 16)] = values.astype(F32).reshape(16, 16, D)
        flat[rows, :] = modulate(values.astype(F32), mod_t)
        return 0

    lax.fori_loop(0, 2, finish_mid, 0)
    hp[...] = jnp.dot(to_patches(), flat[...], preferred_element_type=F32).astype(BF)

    row = lax.broadcasted_iota(jnp.int32, (128, 128), 0)
    col = lax.broadcasted_iota(jnp.int32, (128, 128), 1)
    same = row // 32 == col // 32
    lane = lax.broadcasted_iota(jnp.int32, (128, 256), 1)

    def four_patches(i, _):
        rows = pl.ds(pl.multiple_of(i * 128, 128), 128)
        tiles = [None] * 9
        for head in range(HEADS):
            tile = min(head * HD // 128, 7)
            base = tile * 128
            low = head * HD - base
            keep = (lane >= low) & (lane < low + HD)
            query = jnp.where(keep, qkv[rows, base : base + 256], jnp.zeros((), BF))
            keys = qkv[rows, D + base : D + base + 256]
            part = lax.dot_general(query, keys, (((1,), (1,)), ((), ())), preferred_element_type=F32)
            part = jnp.where(same, part, -1e30)
            expo = jnp.exp2(part - jnp.max(part, axis=-1, keepdims=True))
            probs = (expo / jnp.sum(expo, axis=-1, keepdims=True)).astype(BF)
            mixed = jnp.dot(probs, qkv[rows, 2 * D + base : 2 * D + base + 256], preferred_element_type=F32)
            for n in range(2):
                piece = mixed[:, n * 128 : n * 128 + 128]
                old = tiles[tile + n]
                tiles[tile + n] = piece if old is None else jnp.where(keep[:, n * 128 : n * 128 + 128], piece, old)
        for n in range(9):
            mixed_all[rows, n * 128 : n * 128 + 128] = tiles[n].astype(BF)
        return 0

    def eight_patches(n, _):
        rows = pl.ds(pl.multiple_of(n * 256, 256), 256)
        for cols in (slice(0, 768), slice(768, 1152), slice(1152, 1920), slice(1920, 2688), slice(2688, 3456)):
            acc = jnp.dot(hp[rows, :], wq[:, cols], preferred_element_type=F32)
            if cols.stop <= D:
                acc = acc * SCALE
            qkv[:, cols] = acc.astype(BF)
        lax.fori_loop(0, 2, four_patches, 0)
        ordered = jnp.dot(to_frames(), mixed_all[...], preferred_element_type=F32).astype(BF)
        proj = jnp.dot(ordered, wo[...], preferred_element_type=F32)
        values = mid[:, pl.ds(pl.multiple_of(n * 8, 8), 8), :].reshape(256, D)
        values = (values + mod_t[2:3, :] * proj).astype(BF)
        done[n] = values.reshape(8, 32, D)

        def go(d, _):
            f = (frame + d) % 8
            remote(done.at[n, f], out.at[n, frame], home_send, home_recv, (f, patch)).start()
            return 0

        lax.fori_loop(1, 8, go, 0)
        pltpu.make_async_copy(done.at[n, frame], out.at[n, frame], home_recv).start()
        return 0

    lax.fori_loop(0, 2, eight_patches, 0)
    pltpu.make_async_copy(full, full, gather_send).wait()
    pltpu.make_async_copy(tok_t.at[pl.ds(0, 7)], tok_t.at[pl.ds(0, 7)], tok_send).wait()
    pltpu.make_async_copy(att.at[pl.ds(0, 2032), :], att.at[pl.ds(0, 2032), :], att_send).wait()
    for n in range(2):
        pltpu.make_async_copy(done.at[n, pl.ds(0, 7)], done.at[n, pl.ds(0, 7)], home_send).wait()
    pltpu.make_async_copy(out, out, home_recv).wait()


def shards(tokens, w_qkv_s, w_out_s, mod_s, w_qkv_t, w_out_t, mod_t):
    dma = pltpu.SemaphoreType.DMA
    parts = pl.pallas_call(
        fused_kernel,
        name="blocks",
        out_shape=jax.ShapeDtypeStruct((2, 8, 32, D), BF),
        in_specs=[ANY, VMEM, VMEM, ANY, ANY, ANY, ANY],
        out_specs=ANY,
        scratch_shapes=[
            pltpu.VMEM((4, 128, D), BF),
            pltpu.VMEM((4, 128, D), BF),
            pltpu.VMEM((2, 128, D), BF),
            pltpu.VMEM((16, 128, D), BF),
            pltpu.VMEM((D, 3 * WIN), BF),
            pltpu.VMEM((D, 1024), BF),
            pltpu.VMEM((ROWS, 2 * WIN), BF),
            pltpu.VMEM((4, 80, ROWS), BF),
            pltpu.VMEM((ROWS, QT), F32),
            pltpu.VMEM((ROWS, QT), F32),
            pltpu.VMEM((8, QT), F32),
            pltpu.VMEM((8, QT), F32),
            pltpu.VMEM((4, 4, 80, QT), F32),
            pltpu.VMEM((4, 4, 8, QT), F32),
            pltpu.VMEM((WIN, QT), F32),
            pltpu.VMEM((ROWS, WIN), BF),
            pltpu.VMEM((4, 32, 16, WIN), BF),
            pltpu.VMEM((8, 4, 16, D), BF),
            pltpu.VMEM((D, D), BF),
            pltpu.VMEM((D, 3 * D), BF),
            pltpu.VMEM((D, D), BF),
            pltpu.VMEM((512, D), BF),
            pltpu.VMEM((32, 16, D), F32),
            pltpu.VMEM((512, D), BF),
            pltpu.VMEM((256, 3 * D), BF),
            pltpu.VMEM((256, D), BF),
            pltpu.VMEM((2, 8, 32, D), BF),
            dma,
            dma((6,)),
            dma((2,)),
            dma((16,)),
            dma,
            dma,
            dma,
            dma,
            dma,
            dma,
            dma,
            pltpu.SemaphoreType.REGULAR,
        ],
        compiler_params=params(1),
    )(tokens, mod_s, mod_t, w_qkv_s, w_out_s, w_qkv_t, w_out_t)
    return parts.reshape(2, 8, 4, 8, D).transpose(2, 1, 0, 3, 4).reshape(4, 128, D)


def solution(mesh):
    return jax.shard_map(
        shards,
        mesh=mesh,
        in_specs=(P("frame", "patch", None), P(), P(), P(), P(), P(), P()),
        out_specs=P("frame", "patch", None),
        check_vma=False,
    )
```

```python
import functools

import jax
import jax.numpy as jnp
from jax import lax
from jax.experimental import pallas as pl
from jax.experimental.pallas import tpu as pltpu
from jax.sharding import PartitionSpec as P

HEADS = 16
HD = 72
D = 1152
WIN = 384
ROWS = 2048
QT = 256
KC = 256
SCALE = HD ** (-0.5) * 1.4426950408889634
MESH = pl.DeviceIdType.MESH
VMEM = pl.BlockSpec(memory_space=pltpu.VMEM)
ANY = pl.BlockSpec(memory_space=pl.ANY)
BF = jnp.bfloat16
F32 = jnp.float32


def params(collective_id=None):
    return pltpu.CompilerParams(
        collective_id=collective_id,
        has_side_effects=collective_id is not None,
        vmem_limit_bytes=56 * 2**20,
    )


def remote(src, dst, send_sem, recv_sem, device):
    return pltpu.make_async_remote_copy(
        src_ref=src, dst_ref=dst, send_sem=send_sem, recv_sem=recv_sem, device_id=device, device_id_type=MESH
    )


def modulate(values, mod_ref):
    mean = jnp.mean(values, axis=-1, keepdims=True)
    centered = values - mean
    var = jnp.mean(centered * centered, axis=-1, keepdims=True)
    return (centered * lax.rsqrt(var + 1e-06) * (1.0 + mod_ref[1:2, :]) + mod_ref[0:1, :]).astype(BF)


def place():
    frame, patch = lax.axis_index("frame"), lax.axis_index("patch")
    return frame, patch, patch // 8, (patch // 2) % 4, patch % 2


def rows16(index):
    return pl.ds(pl.multiple_of(index * 16, 16), 16)


def head_lanes(shape, head):
    lane = lax.broadcasted_iota(jnp.int32, shape, 1) + (head // 2) * 128
    return (lane >= HD * head) & (lane < HD * head + HD)


def pack_weights(wbuf, packed, group):
    row = lax.broadcasted_iota(jnp.int32, (2 * WIN, 640), 0)
    col = lax.broadcasted_iota(jnp.int32, (2 * WIN, 640), 1)
    width = 4 * HD
    target = jnp.where(col < width, col, col + (WIN - width)) + 32 * group
    pick = jnp.where((row == target) & (col < 2 * width), 1.0, 0.0).astype(BF)
    row = lax.broadcasted_iota(jnp.int32, (WIN, WIN), 0)
    col = lax.broadcasted_iota(jnp.int32, (WIN, WIN), 1)
    first = jnp.where((row == col + 32 * group) & (col < width), 1.0, 0.0).astype(BF)

    def some(i, _):
        rows = pl.ds(pl.multiple_of(i * 384, 384), 384)
        packed[rows, :WIN] = jnp.dot(wbuf[rows, :WIN], first, preferred_element_type=F32).astype(BF)
        packed[rows, WIN:] = jnp.dot(wbuf[rows, WIN:], pick, preferred_element_type=F32).astype(BF)
        return 0

    lax.fori_loop(0, 3, some, 0)


def project(h, packed, qk, vt, index):
    rows = pl.ds(pl.multiple_of(index * QT, QT), QT)
    acc = jnp.dot(h, packed[...], preferred_element_type=F32)
    qk[rows, :WIN] = (acc[:, :WIN] * SCALE).astype(BF)
    qk[rows, WIN:] = acc[:, WIN : 2 * WIN].astype(BF)
    values = acc[:, 640:1024].T
    one = jnp.where(lax.broadcasted_iota(jnp.int32, (8, QT), 0) == 0, 1.0, 0.0)
    for head in range(4):
        part = values[32 + HD * head : 32 + HD * head + HD, :]
        vt[head, :, rows] = jnp.concatenate([part, one], axis=0).astype(BF)


def load_window(w, wbuf, sems, group):
    copies = []
    for part in range(3):
        cols = pl.ds(pl.multiple_of(part * D + 256 * group, 128), WIN)
        copies.append(pltpu.make_async_copy(w.at[:, cols], wbuf.at[:, pl.ds(part * WIN, WIN)], sems.at[part]))
        copies[-1].start()
    return copies


def to_patches():
    row = lax.broadcasted_iota(jnp.int32, (512, 512), 0)
    col = lax.broadcasted_iota(jnp.int32, (512, 512), 1)
    return jnp.where(col == (row % 32) * 16 + row // 32, 1.0, 0.0).astype(BF)


def to_frames():
    row = lax.broadcasted_iota(jnp.int32, (256, 256), 0)
    col = lax.broadcasted_iota(jnp.int32, (256, 256), 1)
    return jnp.where(col == (row % 8) * 32 + row // 8, 1.0, 0.0).astype(BF)


def fused_kernel(
    tok_hbm, mod_s, mod_t, w_qkv_s, w_out_s, w_qkv_t, w_out_t, out,
    tok, hs, zbuf, full, wbuf, packed, qk, vt, s0, s1, m0, m1, held, held_top, awide, att, att_t, tok_t, wo_s, wq, wo,
    flat, mid, hp, qkv, mixed_all, done,
    tok_sem, w_sem, z_sem, full_sem, gather_send, tok_send, tok_recv, att_send, att_recv, home_send, home_recv, group_sem,
):
    frame, patch, zh, x, core = place()
    group = (x % 2) * 2 + core
    at = frame * 4 + zh * 2 + x // 2
    zpatch = (1 - zh) * 8 + x * 2 + core
    sibling = (frame, patch + 1 - 2 * core)
    zdev = (frame, zpatch)

    barrier = pltpu.get_barrier_semaphore()

    for d in range(1, 16):
        pl.semaphore_signal(barrier, inc=1, device_id=(frame, (patch + d) % 16), device_id_type=MESH)
    for d in range(1, 8):
        pl.semaphore_signal(barrier, inc=1, device_id=((frame + d) % 8, patch), device_id_type=MESH)
    load_tok = pltpu.make_async_copy(tok_hbm, tok, tok_sem)
    load_tok.start()
    windows = load_window(w_qkv_s, wbuf, w_sem, group)
    loads = [
        pltpu.make_async_copy(src, dst, w_sem.at[3 + i])
        for i, (src, dst) in enumerate([(w_out_s, wo_s), (w_qkv_t, wq), (w_out_t, wo)])
    ]
    for load in loads:
        load.start()

    def norm(f):
        hs[f] = modulate(tok[f].astype(F32), mod_s)

    load_tok.wait()
    norm(2 * (1 - zh))
    norm(2 * (1 - zh) + 1)
    pl.semaphore_wait(barrier, 22)
    parts = (pl.ds(0, 64), pl.ds(64, 64))
    for r, part in enumerate(parts):
        for j in range(2):
            remote(hs.at[2 * (1 - zh) + j, part], zbuf.at[j, part], gather_send, z_sem.at[r, j], zdev).start()
    for d in range(1, 8):
        pl.semaphore_signal(group_sem, inc=1, device_id=((frame + d) % 8, patch), device_id_type=MESH)
    norm(2 * zh)
    norm(2 * zh + 1)

    for r, part in enumerate(parts):
        for d in (2, 1, 3):
            xd = (x + d) % 4
            device = (frame, zh * 8 + xd * 2 + core)
            src, dst = hs.at[2 * zh + xd // 2, part], full.at[patch, part]
            remote(src, dst, gather_send, full_sem.at[r, patch], device).start()
        src, dst = hs.at[2 * zh + x // 2, part], full.at[patch, part]
        pltpu.make_async_copy(src, dst, full_sem.at[r, patch]).start()
    awide[...] = jnp.zeros_like(awide)
    for window in windows:
        window.wait()
    pack_weights(wbuf, packed, group)

    def arrived(source, r):
        spot = full.at[source, parts[r]]
        pltpu.make_async_copy(spot, spot, full_sem.at[r, source]).wait()

    def chip_of(k):
        return ((zh + k // 4) % 2) * 4 + (x + 2 * (k % 4) - 3 * (k % 4 // 2)) % 4

    def relay(k, _):
        source = chip_of(k) * 2 + core
        for r in range(2):
            arrived(source, r)
            spot = full.at[source, parts[r]]
            remote(spot, spot, gather_send, full_sem.at[r, source], sibling).start()
        return 0

    def chip(k, _):
        index = chip_of(k)
        for r in range(2):
            arrived(index * 2 + 1 - core, r)
        h = full[pl.ds(index * 2, 2)].reshape(QT, D)
        project(h, packed, qk, vt, index)
        return 0

    def token_out(f):
        remote(tok.at[:, rows16(f), :], tok_t.at[frame], tok_send, tok_recv, (f, patch)).start()

    for d in (2, 4, 6):
        token_out((frame + d) % 8)
    pltpu.make_async_copy(tok.at[:, rows16(frame), :], tok_t.at[frame], tok_recv).start()
    relay(0, 0)
    chip(0, 0)
    for r, part in enumerate(parts):
        for j in range(2):
            src, dst = zbuf.at[j, part], full.at[zpatch, part]
            pltpu.make_async_copy(src, src, z_sem.at[r, j]).wait()
            for n in range(2):
                xd = 2 * j + n

                @pl.when(xd != x)
                def _():
                    device = (frame, zh * 8 + xd * 2 + core)
                    remote(src, dst, gather_send, full_sem.at[r, zpatch], device).start()

                @pl.when(xd == x)
                def _():
                    pltpu.make_async_copy(src, dst, full_sem.at[r, zpatch]).start()

    lax.fori_loop(1, 5, relay, 0)
    for d in (1, 3, 5, 7):
        token_out((frame + d) % 8)
    lax.fori_loop(1, 5, chip, 0)


    scores, tops = (s0, s1), (m0, m1)

    def score(head, tile, slot, chunks):
        base = (head // 2) * 128
        rows = pl.ds(pl.multiple_of(tile * QT, QT), QT)
        keep = head_lanes((QT, 256), head)
        query = jnp.where(keep, qk[rows, base : base + 256], jnp.zeros((), BF))
        top = None
        for c, at_chunk in enumerate(chunks):
            keys = qk[pl.ds(pl.multiple_of(at_chunk * KC, KC), KC), WIN + base : WIN + base + 256]
            part = lax.dot_general(keys, query, (((1,), (1,)), ((), ())), preferred_element_type=F32)
            scores[slot][c * KC : (c + 1) * KC, :] = part
            part = jnp.max(part.reshape(KC // 8, 8, QT), axis=0)
            top = part if top is None else jnp.maximum(top, part)
        tops[slot][...] = jnp.broadcast_to(jnp.max(top, axis=0, keepdims=True), (8, QT))

    def sums(head, slot, chunks, top):
        acc = None
        for c, at_chunk in enumerate(chunks):
            probs = jnp.exp2(scores[slot][c * KC : (c + 1) * KC, :] - top).astype(BF)
            values = vt[head, :, pl.ds(pl.multiple_of(at_chunk * KC, KC), KC)]
            part = jnp.dot(values, probs, preferred_element_type=F32)
            acc = part if acc is None else acc + part
        return acc

    def keep_head(head, acc):
        awide[pl.ds(pl.multiple_of(32 * group + HD * head, 8), HD), :] = acc[:HD] / acc[HD : HD + 1]

    def send_tile(tile):
        att[pl.ds(pl.multiple_of(tile * QT, QT), QT), :] = awide[...].T.astype(BF)

        def go(n, _):
            f, p = (frame + n // 2) % 8, tile * 2 + n % 2
            src, dst = att.at[rows16(p * 8 + f), :], att_t.at[group, at]
            mine = (f == frame) & (p == patch)

            @pl.when(jnp.logical_not(mine))
            def _():
                remote(src, dst, att_send, att_recv, (f, p)).start()

            @pl.when(mine)
            def _():
                pltpu.make_async_copy(src, dst, att_recv).start()

            return 0

        lax.fori_loop(0, 16, go, 0)

    near = [zh * 4 + c for c in range(4)] + [(1 - zh) * 4 + x]
    far = [(1 - zh) * 4 + (x + d) % 4 for d in (2, 1, 3)]
    score(0, zh * 4 + x, 0, near)

    def first_part(i, _):
        for head in range(4):
            ahead = (x + i) % 4 if head < 3 else (x + i + 1) % 4
            score((head + 1) % 4, zh * 4 + ahead, (head + 1) % 2, near)
            slot = head % 2
            held[(x + i) % 4, head] = sums(head, slot, near, tops[slot][0:1, :])
            held_top[(x + i) % 4, head] = tops[slot][...]
        return 0

    lax.fori_loop(0, 4, first_part, 0)
    lax.fori_loop(5, 8, relay, 0)
    lax.fori_loop(5, 8, chip, 0)
    pl.semaphore_wait(group_sem, 7)

    def far_tile(i):
        return (1 - zh) * 4 + (x + 2 * (i % 4) - 3 * (i % 4 // 2)) % 4

    def own_tile(i):
        return zh * 4 + (x + 1 + 2 * (i % 4) - 3 * (i % 4 // 2)) % 4

    score(0, far_tile(0), 0, range(8))

    def two_tiles(i, _):
        for head in range(4):
            if head < 3:
                score(head + 1, far_tile(i), (head + 1) % 2, range(8))
            else:
                score(0, own_tile(i), 0, far)
            slot = head % 2
            keep_head(head, sums(head, slot, range(8), tops[slot][0:1, :]))
        send_tile(far_tile(i))
        for head in range(4):
            if head < 3:
                score(head + 1, own_tile(i), (head + 1) % 2, far)
            else:
                score(0, far_tile(i + 1), 0, range(8))
            slot = head % 2
            place = own_tile(i) - zh * 4
            before = held_top[place, head, 0:1, :]
            top = jnp.maximum(tops[slot][0:1, :], before)
            acc = held[place, head] * jnp.exp2(before - top)
            keep_head(head, acc + sums(head, slot, far, top))
        send_tile(own_tile(i))
        return 0

    lax.fori_loop(0, 4, two_tiles, 0)

    for load in loads:
        load.wait()
    pltpu.make_async_copy(tok_t, tok_t, tok_recv).wait()
    pltpu.make_async_copy(att_t, att_t, att_recv).wait()
    for tile in range(9):
        cols = slice(tile * 128, tile * 128 + 128)
        g, rest = min(tile // 2, 3), tile - 2 * min(tile // 2, 3)
        part = att_t[g, :, :, rest * 128 : rest * 128 + 128].reshape(512, 128)
        if rest == 0 and g > 0:
            part = part + att_t[g - 1, :, :, 256:384].reshape(512, 128)
        flat[:, cols] = part

    def finish_mid(i, _):
        rows = pl.ds(pl.multiple_of(i * 256, 256), 256)
        proj = jnp.dot(flat[rows, :], wo_s[...], preferred_element_type=F32)
        values = tok_t[pl.ds(i * 4, 4)].reshape(256, D).astype(F32)
        values = (values + mod_s[2:3, :] * proj).astype(BF)
        mid[pl.ds(i * 16, 16)] = values.astype(F32).reshape(16, 16, D)
        flat[rows, :] = modulate(values.astype(F32), mod_t)
        return 0

    lax.fori_loop(0, 2, finish_mid, 0)
    hp[...] = jnp.dot(to_patches(), flat[...], preferred_element_type=F32).astype(BF)

    row = lax.broadcasted_iota(jnp.int32, (128, 128), 0)
    col = lax.broadcasted_iota(jnp.int32, (128, 128), 1)
    same = row // 32 == col // 32
    lane = lax.broadcasted_iota(jnp.int32, (128, 256), 1)

    def four_patches(i, _):
        rows = pl.ds(pl.multiple_of(i * 128, 128), 128)
        tiles = [None] * 9
        for head in range(HEADS):
            tile = min(head * HD // 128, 7)
            base = tile * 128
            low = head * HD - base
            keep = (lane >= low) & (lane < low + HD)
            query = jnp.where(keep, qkv[rows, base : base + 256], jnp.zeros((), BF))
            keys = qkv[rows, D + base : D + base + 256]
            part = lax.dot_general(query, keys, (((1,), (1,)), ((), ())), preferred_element_type=F32)
            part = jnp.where(same, part, -1e30)
            expo = jnp.exp2(part - jnp.max(part, axis=-1, keepdims=True))
            probs = (expo / jnp.sum(expo, axis=-1, keepdims=True)).astype(BF)
            mixed = jnp.dot(probs, qkv[rows, 2 * D + base : 2 * D + base + 256], preferred_element_type=F32)
            for n in range(2):
                piece = mixed[:, n * 128 : n * 128 + 128]
                old = tiles[tile + n]
                tiles[tile + n] = piece if old is None else jnp.where(keep[:, n * 128 : n * 128 + 128], piece, old)
        for n in range(9):
            mixed_all[rows, n * 128 : n * 128 + 128] = tiles[n].astype(BF)
        return 0

    def eight_patches(n, _):
        rows = pl.ds(pl.multiple_of(n * 256, 256), 256)
        for cols in (slice(0, 768), slice(768, 1152), slice(1152, 1920), slice(1920, 2688), slice(2688, 3456)):
            acc = jnp.dot(hp[rows, :], wq[:, cols], preferred_element_type=F32)
            if cols.stop <= D:
                acc = acc * SCALE
            qkv[:, cols] = acc.astype(BF)
        lax.fori_loop(0, 2, four_patches, 0)
        ordered = jnp.dot(to_frames(), mixed_all[...], preferred_element_type=F32).astype(BF)
        proj = jnp.dot(ordered, wo[...], preferred_element_type=F32)
        values = mid[:, pl.ds(pl.multiple_of(n * 8, 8), 8), :].reshape(256, D)
        values = (values + mod_t[2:3, :] * proj).astype(BF)
        done[n] = values.reshape(8, 32, D)

        def go(d, _):
            f = (frame + d) % 8
            remote(done.at[n, f], out.at[n, frame], home_send, home_recv, (f, patch)).start()
            return 0

        lax.fori_loop(1, 8, go, 0)
        pltpu.make_async_copy(done.at[n, frame], out.at[n, frame], home_recv).start()
        return 0

    lax.fori_loop(0, 2, eight_patches, 0)
    pltpu.make_async_copy(full, full, gather_send).wait()
    pltpu.make_async_copy(tok_t.at[pl.ds(0, 7)], tok_t.at[pl.ds(0, 7)], tok_send).wait()
    pltpu.make_async_copy(att.at[pl.ds(0, 2032), :], att.at[pl.ds(0, 2032), :], att_send).wait()
    for n in range(2):
        pltpu.make_async_copy(done.at[n, pl.ds(0, 7)], done.at[n, pl.ds(0, 7)], home_send).wait()
    pltpu.make_async_copy(out, out, home_recv).wait()


def shards(tokens, w_qkv_s, w_out_s, mod_s, w_qkv_t, w_out_t, mod_t):
    dma = pltpu.SemaphoreType.DMA
    parts = pl.pallas_call(
        fused_kernel,
        name="blocks",
        out_shape=jax.ShapeDtypeStruct((2, 8, 32, D), BF),
        in_specs=[ANY, VMEM, VMEM, ANY, ANY, ANY, ANY],
        out_specs=ANY,
        scratch_shapes=[
            pltpu.VMEM((4, 128, D), BF),
            pltpu.VMEM((4, 128, D), BF),
            pltpu.VMEM((2, 128, D), BF),
            pltpu.VMEM((16, 128, D), BF),
            pltpu.VMEM((D, 3 * WIN), BF),
            pltpu.VMEM((D, 1024), BF),
            pltpu.VMEM((ROWS, 2 * WIN), BF),
            pltpu.VMEM((4, 80, ROWS), BF),
            pltpu.VMEM((ROWS, QT), F32),
            pltpu.VMEM((ROWS, QT), F32),
            pltpu.VMEM((8, QT), F32),
            pltpu.VMEM((8, QT), F32),
            pltpu.VMEM((4, 4, 80, QT), F32),
            pltpu.VMEM((4, 4, 8, QT), F32),
            pltpu.VMEM((WIN, QT), F32),
            pltpu.VMEM((ROWS, WIN), BF),
            pltpu.VMEM((4, 32, 16, WIN), BF),
            pltpu.VMEM((8, 4, 16, D), BF),
            pltpu.VMEM((D, D), BF),
            pltpu.VMEM((D, 3 * D), BF),
            pltpu.VMEM((D, D), BF),
            pltpu.VMEM((512, D), BF),
            pltpu.VMEM((32, 16, D), F32),
            pltpu.VMEM((512, D), BF),
            pltpu.VMEM((256, 3 * D), BF),
            pltpu.VMEM((256, D), BF),
            pltpu.VMEM((2, 8, 32, D), BF),
            dma,
            dma((6,)),
            dma((2, 2)),
            dma((2, 16)),
            dma,
            dma,
            dma,
            dma,
            dma,
            dma,
            dma,
            pltpu.SemaphoreType.REGULAR,
        ],
        compiler_params=params(1),
    )(tokens, mod_s, mod_t, w_qkv_s, w_out_s, w_qkv_t, w_out_t)
    return parts.reshape(2, 8, 4, 8, D).transpose(2, 1, 0, 3, 4).reshape(4, 128, D)


def solution(mesh):
    return jax.shard_map(
        shards,
        mesh=mesh,
        in_specs=(P("frame", "patch", None), P(), P(), P(), P(), P(), P()),
        out_specs=P("frame", "patch", None),
        check_vma=False,
    )
```

```python
import functools

import jax
import jax.numpy as jnp
from jax import lax
from jax.experimental import pallas as pl
from jax.experimental.pallas import tpu as pltpu
from jax.sharding import PartitionSpec as P

HEADS = 16
HD = 72
D = 1152
WIN = 384
ROWS = 2048
QT = 256
KC = 256
SCALE = HD ** (-0.5) * 1.4426950408889634
MESH = pl.DeviceIdType.MESH
VMEM = pl.BlockSpec(memory_space=pltpu.VMEM)
ANY = pl.BlockSpec(memory_space=pl.ANY)
BF = jnp.bfloat16
F32 = jnp.float32


def params(collective_id=None):
    return pltpu.CompilerParams(
        collective_id=collective_id,
        has_side_effects=collective_id is not None,
        vmem_limit_bytes=56 * 2**20,
    )


def remote(src, dst, send_sem, recv_sem, device):
    return pltpu.make_async_remote_copy(
        src_ref=src, dst_ref=dst, send_sem=send_sem, recv_sem=recv_sem, device_id=device, device_id_type=MESH
    )


def modulate(values, mod_ref):
    mean = jnp.mean(values, axis=-1, keepdims=True)
    centered = values - mean
    var = jnp.mean(centered * centered, axis=-1, keepdims=True)
    return (centered * lax.rsqrt(var + 1e-06) * (1.0 + mod_ref[1:2, :]) + mod_ref[0:1, :]).astype(BF)


def place():
    frame, patch = lax.axis_index("frame"), lax.axis_index("patch")
    return frame, patch, patch // 8, (patch // 2) % 4, patch % 2


def rows16(index):
    return pl.ds(pl.multiple_of(index * 16, 16), 16)


def head_lanes(shape, head):
    lane = lax.broadcasted_iota(jnp.int32, shape, 1) + (head // 2) * 128
    return (lane >= HD * head) & (lane < HD * head + HD)


def pack_weights(wbuf, packed, group):
    row = lax.broadcasted_iota(jnp.int32, (2 * WIN, 640), 0)
    col = lax.broadcasted_iota(jnp.int32, (2 * WIN, 640), 1)
    width = 4 * HD
    target = jnp.where(col < width, col, col + (WIN - width)) + 32 * group
    pick = jnp.where((row == target) & (col < 2 * width), 1.0, 0.0).astype(BF)
    row = lax.broadcasted_iota(jnp.int32, (WIN, WIN), 0)
    col = lax.broadcasted_iota(jnp.int32, (WIN, WIN), 1)
    first = jnp.where((row == col + 32 * group) & (col < width), 1.0, 0.0).astype(BF)

    def some(i, _):
        rows = pl.ds(pl.multiple_of(i * 384, 384), 384)
        packed[rows, :WIN] = jnp.dot(wbuf[rows, :WIN], first, preferred_element_type=F32).astype(BF)
        packed[rows, WIN:] = jnp.dot(wbuf[rows, WIN:], pick, preferred_element_type=F32).astype(BF)
        return 0

    lax.fori_loop(0, 3, some, 0)


def project(h, packed, qk, vt, index):
    rows = pl.ds(pl.multiple_of(index * QT, QT), QT)
    acc = jnp.dot(h, packed[...], preferred_element_type=F32)
    qk[rows, :WIN] = (acc[:, :WIN] * SCALE).astype(BF)
    qk[rows, WIN:] = acc[:, WIN : 2 * WIN].astype(BF)
    values = acc[:, 640:1024].T
    one = jnp.where(lax.broadcasted_iota(jnp.int32, (8, QT), 0) == 0, 1.0, 0.0)
    for head in range(4):
        part = values[32 + HD * head : 32 + HD * head + HD, :]
        vt[head, :, rows] = jnp.concatenate([part, one], axis=0).astype(BF)


def load_window(w, wbuf, sems, group):
    copies = []
    for part in range(3):
        cols = pl.ds(pl.multiple_of(part * D + 256 * group, 128), WIN)
        copies.append(pltpu.make_async_copy(w.at[:, cols], wbuf.at[:, pl.ds(part * WIN, WIN)], sems.at[part]))
        copies[-1].start()
    return copies


def to_patches():
    row = lax.broadcasted_iota(jnp.int32, (512, 512), 0)
    col = lax.broadcasted_iota(jnp.int32, (512, 512), 1)
    return jnp.where(col == (row % 32) * 16 + row // 32, 1.0, 0.0).astype(BF)


def to_frames():
    row = lax.broadcasted_iota(jnp.int32, (256, 256), 0)
    col = lax.broadcasted_iota(jnp.int32, (256, 256), 1)
    return jnp.where(col == (row % 8) * 32 + row // 8, 1.0, 0.0).astype(BF)


def fused_kernel(
    tok_hbm, mod_s, mod_t, w_qkv_s, w_out_s, w_qkv_t, w_out_t, out,
    tok, hs, zbuf, full, wbuf, packed, qk, vt, s0, s1, m0, m1, held, held_top, awide, att, att_t, tok_t, wo_s, wq, wo,
    flat, mid, hp, qkv, mixed_all, done,
    tok_sem, w_sem, z_sem, full_sem, gather_send, tok_send, tok_recv, att_send, att_recv, side_send, side_recv, home_send, home_recv, group_sem,
):
    frame, patch, zh, x, core = place()
    group = (x % 2) * 2 + core
    zpatch = (1 - zh) * 8 + x * 2 + core
    sibling = (frame, patch + 1 - 2 * core)
    zdev = (frame, zpatch)

    barrier = pltpu.get_barrier_semaphore()

    for d in range(1, 16):
        pl.semaphore_signal(barrier, inc=1, device_id=(frame, (patch + d) % 16), device_id_type=MESH)
    for d in range(1, 8):
        pl.semaphore_signal(barrier, inc=1, device_id=((frame + d) % 8, patch), device_id_type=MESH)
    load_tok = pltpu.make_async_copy(tok_hbm, tok, tok_sem)
    load_tok.start()
    windows = load_window(w_qkv_s, wbuf, w_sem, group)
    loads = [
        pltpu.make_async_copy(src, dst, w_sem.at[3 + i])
        for i, (src, dst) in enumerate([(w_out_s, wo_s), (w_qkv_t, wq), (w_out_t, wo)])
    ]
    for load in loads:
        load.start()

    def norm(f):
        hs[f] = modulate(tok[f].astype(F32), mod_s)

    load_tok.wait()
    norm(2 * (1 - zh))
    norm(2 * (1 - zh) + 1)
    pl.semaphore_wait(barrier, 22)
    parts = (pl.ds(0, 64), pl.ds(64, 64))
    for r, part in enumerate(parts):
        for j in range(2):
            remote(hs.at[2 * (1 - zh) + j, part], zbuf.at[j, part], gather_send, z_sem.at[r, j], zdev).start()
    for d in range(1, 8):
        pl.semaphore_signal(group_sem, inc=1, device_id=((frame + d) % 8, patch), device_id_type=MESH)
    norm(2 * zh)
    norm(2 * zh + 1)

    for r, part in enumerate(parts):
        for d in (2, 1, 3):
            xd = (x + d) % 4
            device = (frame, zh * 8 + xd * 2 + core)
            src, dst = hs.at[2 * zh + xd // 2, part], full.at[patch, part]
            remote(src, dst, gather_send, full_sem.at[r, patch], device).start()
        src, dst = hs.at[2 * zh + x // 2, part], full.at[patch, part]
        pltpu.make_async_copy(src, dst, full_sem.at[r, patch]).start()
    awide[...] = jnp.zeros_like(awide)
    for window in windows:
        window.wait()
    pack_weights(wbuf, packed, group)

    def arrived(source, r):
        spot = full.at[source, parts[r]]
        pltpu.make_async_copy(spot, spot, full_sem.at[r, source]).wait()

    def chip_of(k):
        return ((zh + k // 4) % 2) * 4 + (x + 2 * (k % 4) - 3 * (k % 4 // 2)) % 4

    def relay(k, _):
        source = chip_of(k) * 2 + core
        for r in range(2):
            arrived(source, r)
            spot = full.at[source, parts[r]]
            remote(spot, spot, gather_send, full_sem.at[r, source], sibling).start()
        return 0

    def chip(k, _):
        index = chip_of(k)
        for r in range(2):
            arrived(index * 2 + 1 - core, r)
        h = full[pl.ds(index * 2, 2)].reshape(QT, D)
        project(h, packed, qk, vt, index)
        return 0

    def token_out(f):
        remote(tok.at[:, rows16(f), :], tok_t.at[frame], tok_send, tok_recv, (f, patch)).start()

    for d in (2, 4, 6):
        token_out((frame + d) % 8)
    pltpu.make_async_copy(tok.at[:, rows16(frame), :], tok_t.at[frame], tok_recv).start()
    relay(0, 0)
    chip(0, 0)
    for r, part in enumerate(parts):
        for j in range(2):
            src, dst = zbuf.at[j, part], full.at[zpatch, part]
            pltpu.make_async_copy(src, src, z_sem.at[r, j]).wait()
            for n in range(2):
                xd = 2 * j + n

                @pl.when(xd != x)
                def _():
                    device = (frame, zh * 8 + xd * 2 + core)
                    remote(src, dst, gather_send, full_sem.at[r, zpatch], device).start()

                @pl.when(xd == x)
                def _():
                    pltpu.make_async_copy(src, dst, full_sem.at[r, zpatch]).start()

    lax.fori_loop(1, 5, relay, 0)
    for d in (1, 3, 5, 7):
        token_out((frame + d) % 8)
    lax.fori_loop(1, 5, chip, 0)


    scores, tops = (s0, s1), (m0, m1)

    def score(head, tile, slot, chunks):
        base = (head // 2) * 128
        rows = pl.ds(pl.multiple_of(tile * QT, QT), QT)
        keep = head_lanes((QT, 256), head)
        query = jnp.where(keep, qk[rows, base : base + 256], jnp.zeros((), BF))
        top = None
        for c, at_chunk in enumerate(chunks):
            keys = qk[pl.ds(pl.multiple_of(at_chunk * KC, KC), KC), WIN + base : WIN + base + 256]
            part = lax.dot_general(keys, query, (((1,), (1,)), ((), ())), preferred_element_type=F32)
            scores[slot][c * KC : (c + 1) * KC, :] = part
            part = jnp.max(part.reshape(KC // 8, 8, QT), axis=0)
            top = part if top is None else jnp.maximum(top, part)
        tops[slot][...] = jnp.broadcast_to(jnp.max(top, axis=0, keepdims=True), (8, QT))

    def sums(head, slot, chunks, top):
        acc = None
        for c, at_chunk in enumerate(chunks):
            probs = jnp.exp2(scores[slot][c * KC : (c + 1) * KC, :] - top).astype(BF)
            values = vt[head, :, pl.ds(pl.multiple_of(at_chunk * KC, KC), KC)]
            part = jnp.dot(values, probs, preferred_element_type=F32)
            acc = part if acc is None else acc + part
        return acc

    def keep_head(head, acc):
        awide[pl.ds(pl.multiple_of(32 * group + HD * head, 8), HD), :] = acc[:HD] / acc[HD : HD + 1]

    def send_tile(tile):
        att[tile] = awide[...].T.astype(BF).reshape(2, 8, 16, WIN)

        def go(n, _):
            f = (frame + n) % 8
            src, dst = att.at[tile, :, f], att_t.at[:, core, x % 2, frame, zh, x // 2]
            mine = (f == frame) & (tile == zh * 4 + x)

            @pl.when(jnp.logical_not(mine))
            def _():
                remote(src, dst, att_send, att_recv.at[zh], (f, tile * 2 + core)).start()

            @pl.when(mine)
            def _():
                pltpu.make_async_copy(src, dst, att_recv.at[zh]).start()

            return 0

        lax.fori_loop(0, 8, go, 0)

    near = [zh * 4 + c for c in range(4)] + [(1 - zh) * 4 + x]
    far = [(1 - zh) * 4 + (x + d) % 4 for d in (2, 1, 3)]
    score(0, zh * 4 + x, 0, near)

    def first_part(i, _):
        for head in range(4):
            ahead = (x + i) % 4 if head < 3 else (x + i + 1) % 4
            score((head + 1) % 4, zh * 4 + ahead, (head + 1) % 2, near)
            slot = head % 2
            held[(x + i) % 4, head] = sums(head, slot, near, tops[slot][0:1, :])
            held_top[(x + i) % 4, head] = tops[slot][...]
        return 0

    lax.fori_loop(0, 4, first_part, 0)
    lax.fori_loop(5, 8, relay, 0)
    lax.fori_loop(5, 8, chip, 0)
    pl.semaphore_wait(group_sem, 7)

    def far_tile(i):
        return (1 - zh) * 4 + (x + 2 * (i % 4) - 3 * (i % 4 // 2)) % 4

    def own_tile(i):
        return zh * 4 + (x + 1 + 2 * (i % 4) - 3 * (i % 4 // 2)) % 4

    score(0, far_tile(0), 0, range(8))

    def two_tiles(i, _):
        for head in range(4):
            if head < 3:
                score(head + 1, far_tile(i), (head + 1) % 2, range(8))
            else:
                score(0, own_tile(i), 0, far)
            slot = head % 2
            keep_head(head, sums(head, slot, range(8), tops[slot][0:1, :]))
        send_tile(far_tile(i))
        for head in range(4):
            if head < 3:
                score(head + 1, own_tile(i), (head + 1) % 2, far)
            else:
                score(0, far_tile(i + 1), 0, range(8))
            slot = head % 2
            place = own_tile(i) - zh * 4
            before = held_top[place, head, 0:1, :]
            top = jnp.maximum(tops[slot][0:1, :], before)
            acc = held[place, head] * jnp.exp2(before - top)
            keep_head(head, acc + sums(head, slot, far, top))
        send_tile(own_tile(i))
        return 0

    lax.fori_loop(0, 4, two_tiles, 0)

    for n in range(2):
        z = (zh + 1 + n) % 2
        came = att_t.at[:, core, :, :, z]
        pltpu.make_async_copy(came, came, att_recv.at[z]).wait()
        part = att_t.at[1 - core, core, :, :, z]
        remote(part, part, side_send, side_recv.at[n], sibling).start()

    for load in loads:
        load.wait()
    pltpu.make_async_copy(tok_t, tok_t, tok_recv).wait()
    for n in range(2):
        came = att_t.at[core, 1 - core, :, :, (zh + 1 + n) % 2]
        pltpu.make_async_copy(came, came, side_recv.at[n]).wait()
    for tile in range(9):
        cols = slice(tile * 128, tile * 128 + 128)
        g, rest = min(tile // 2, 3), tile - 2 * min(tile // 2, 3)
        part = att_t[core, g % 2, g // 2, :, :, :, :, rest * 128 : rest * 128 + 128].reshape(512, 128)
        if rest == 0 and g > 0:
            part = part + att_t[core, (g - 1) % 2, (g - 1) // 2, :, :, :, :, 256:384].reshape(512, 128)
        flat[:, cols] = part

    def finish_mid(i, _):
        rows = pl.ds(pl.multiple_of(i * 256, 256), 256)
        proj = jnp.dot(flat[rows, :], wo_s[...], preferred_element_type=F32)
        values = tok_t[pl.ds(i * 4, 4)].reshape(256, D).astype(F32)
        values = (values + mod_s[2:3, :] * proj).astype(BF)
        mid[pl.ds(i * 16, 16)] = values.astype(F32).reshape(16, 16, D)
        flat[rows, :] = modulate(values.astype(F32), mod_t)
        return 0

    lax.fori_loop(0, 2, finish_mid, 0)
    hp[...] = jnp.dot(to_patches(), flat[...], preferred_element_type=F32).astype(BF)

    row = lax.broadcasted_iota(jnp.int32, (128, 128), 0)
    col = lax.broadcasted_iota(jnp.int32, (128, 128), 1)
    same = row // 32 == col // 32
    lane = lax.broadcasted_iota(jnp.int32, (128, 256), 1)

    def four_patches(i, _):
        rows = pl.ds(pl.multiple_of(i * 128, 128), 128)
        tiles = [None] * 9
        for head in range(HEADS):
            tile = min(head * HD // 128, 7)
            base = tile * 128
            low = head * HD - base
            keep = (lane >= low) & (lane < low + HD)
            query = jnp.where(keep, qkv[rows, base : base + 256], jnp.zeros((), BF))
            keys = qkv[rows, D + base : D + base + 256]
            part = lax.dot_general(query, keys, (((1,), (1,)), ((), ())), preferred_element_type=F32)
            part = jnp.where(same, part, -1e30)
            expo = jnp.exp2(part - jnp.max(part, axis=-1, keepdims=True))
            probs = (expo / jnp.sum(expo, axis=-1, keepdims=True)).astype(BF)
            mixed = jnp.dot(probs, qkv[rows, 2 * D + base : 2 * D + base + 256], preferred_element_type=F32)
            for n in range(2):
                piece = mixed[:, n * 128 : n * 128 + 128]
                old = tiles[tile + n]
                tiles[tile + n] = piece if old is None else jnp.where(keep[:, n * 128 : n * 128 + 128], piece, old)
        for n in range(9):
            mixed_all[rows, n * 128 : n * 128 + 128] = tiles[n].astype(BF)
        return 0

    def eight_patches(n, _):
        rows = pl.ds(pl.multiple_of(n * 256, 256), 256)
        for cols in (slice(0, 768), slice(768, 1152), slice(1152, 1920), slice(1920, 2688), slice(2688, 3456)):
            acc = jnp.dot(hp[rows, :], wq[:, cols], preferred_element_type=F32)
            if cols.stop <= D:
                acc = acc * SCALE
            qkv[:, cols] = acc.astype(BF)
        lax.fori_loop(0, 2, four_patches, 0)
        ordered = jnp.dot(to_frames(), mixed_all[...], preferred_element_type=F32).astype(BF)
        proj = jnp.dot(ordered, wo[...], preferred_element_type=F32)
        values = mid[:, pl.ds(pl.multiple_of(n * 8, 8), 8), :].reshape(256, D)
        values = (values + mod_t[2:3, :] * proj).astype(BF)
        done[n] = values.reshape(8, 32, D)

        def go(d, _):
            f = (frame + d) % 8
            remote(done.at[n, f], out.at[n, frame], home_send, home_recv, (f, patch)).start()
            return 0

        lax.fori_loop(1, 8, go, 0)
        pltpu.make_async_copy(done.at[n, frame], out.at[n, frame], home_recv).start()
        return 0

    lax.fori_loop(0, 2, eight_patches, 0)
    pltpu.make_async_copy(full, full, gather_send).wait()
    pltpu.make_async_copy(tok_t.at[pl.ds(0, 7)], tok_t.at[pl.ds(0, 7)], tok_send).wait()
    pltpu.make_async_copy(att.at[pl.ds(0, 7)], att.at[pl.ds(0, 7)], att_send).wait()
    last = att.at[7, :, pl.ds(0, 7)]
    pltpu.make_async_copy(last, last, att_send).wait()
    part = att_t.at[1 - core, core]
    pltpu.make_async_copy(part, part, side_send).wait()
    for n in range(2):
        pltpu.make_async_copy(done.at[n, pl.ds(0, 7)], done.at[n, pl.ds(0, 7)], home_send).wait()
    pltpu.make_async_copy(out, out, home_recv).wait()


def shards(tokens, w_qkv_s, w_out_s, mod_s, w_qkv_t, w_out_t, mod_t):
    dma = pltpu.SemaphoreType.DMA
    parts = pl.pallas_call(
        fused_kernel,
        name="blocks",
        out_shape=jax.ShapeDtypeStruct((2, 8, 32, D), BF),
        in_specs=[ANY, VMEM, VMEM, ANY, ANY, ANY, ANY],
        out_specs=ANY,
        scratch_shapes=[
            pltpu.VMEM((4, 128, D), BF),
            pltpu.VMEM((4, 128, D), BF),
            pltpu.VMEM((2, 128, D), BF),
            pltpu.VMEM((16, 128, D), BF),
            pltpu.VMEM((D, 3 * WIN), BF),
            pltpu.VMEM((D, 1024), BF),
            pltpu.VMEM((ROWS, 2 * WIN), BF),
            pltpu.VMEM((4, 80, ROWS), BF),
            pltpu.VMEM((ROWS, QT), F32),
            pltpu.VMEM((ROWS, QT), F32),
            pltpu.VMEM((8, QT), F32),
            pltpu.VMEM((8, QT), F32),
            pltpu.VMEM((4, 4, 80, QT), F32),
            pltpu.VMEM((4, 4, 8, QT), F32),
            pltpu.VMEM((WIN, QT), F32),
            pltpu.VMEM((8, 2, 8, 16, WIN), BF),
            pltpu.VMEM((2, 2, 2, 8, 2, 2, 16, WIN), BF),
            pltpu.VMEM((8, 4, 16, D), BF),
            pltpu.VMEM((D, D), BF),
            pltpu.VMEM((D, 3 * D), BF),
            pltpu.VMEM((D, D), BF),
            pltpu.VMEM((512, D), BF),
            pltpu.VMEM((32, 16, D), F32),
            pltpu.VMEM((512, D), BF),
            pltpu.VMEM((256, 3 * D), BF),
            pltpu.VMEM((256, D), BF),
            pltpu.VMEM((2, 8, 32, D), BF),
            dma,
            dma((6,)),
            dma((2, 2)),
            dma((2, 16)),
            dma,
            dma,
            dma,
            dma,
            dma((2,)),
            dma,
            dma((2,)),
            dma,
            dma,
            pltpu.SemaphoreType.REGULAR,
        ],
        compiler_params=params(1),
    )(tokens, mod_s, mod_t, w_qkv_s, w_out_s, w_qkv_t, w_out_t)
    return parts.reshape(2, 8, 4, 8, D).transpose(2, 1, 0, 3, 4).reshape(4, 128, D)


def solution(mesh):
    return jax.shard_map(
        shards,
        mesh=mesh,
        in_specs=(P("frame", "patch", None), P(), P(), P(), P(), P(), P()),
        out_specs=P("frame", "patch", None),
        check_vma=False,
    )
```

```python
import functools

import jax
import jax.numpy as jnp
from jax import lax
from jax.experimental import pallas as pl
from jax.experimental.pallas import tpu as pltpu
from jax.sharding import PartitionSpec as P

HEADS = 16
HD = 72
D = 1152
WIN = 384
ROWS = 2048
QT = 256
KC = 256
SCALE = HD ** (-0.5) * 1.4426950408889634
MESH = pl.DeviceIdType.MESH
VMEM = pl.BlockSpec(memory_space=pltpu.VMEM)
ANY = pl.BlockSpec(memory_space=pl.ANY)
BF = jnp.bfloat16
F32 = jnp.float32


def params(collective_id=None):
    return pltpu.CompilerParams(
        collective_id=collective_id,
        has_side_effects=collective_id is not None,
        vmem_limit_bytes=56 * 2**20,
    )


def remote(src, dst, send_sem, recv_sem, device):
    return pltpu.make_async_remote_copy(
        src_ref=src, dst_ref=dst, send_sem=send_sem, recv_sem=recv_sem, device_id=device, device_id_type=MESH
    )


def modulate(values, mod_ref):
    mean = jnp.mean(values, axis=-1, keepdims=True)
    centered = values - mean
    var = jnp.mean(centered * centered, axis=-1, keepdims=True)
    return (centered * lax.rsqrt(var + 1e-06) * (1.0 + mod_ref[1:2, :]) + mod_ref[0:1, :]).astype(BF)


def place():
    frame, patch = lax.axis_index("frame"), lax.axis_index("patch")
    return frame, patch, patch // 8, (patch // 2) % 4, patch % 2


def rows16(index):
    return pl.ds(pl.multiple_of(index * 16, 16), 16)


def head_lanes(shape, head):
    lane = lax.broadcasted_iota(jnp.int32, shape, 1) + (head // 2) * 128
    return (lane >= HD * head) & (lane < HD * head + HD)


def pack_weights(wbuf, packed, group):
    row = lax.broadcasted_iota(jnp.int32, (2 * WIN, 640), 0)
    col = lax.broadcasted_iota(jnp.int32, (2 * WIN, 640), 1)
    width = 4 * HD
    target = jnp.where(col < width, col, col + (WIN - width)) + 32 * group
    pick = jnp.where((row == target) & (col < 2 * width), 1.0, 0.0).astype(BF)
    row = lax.broadcasted_iota(jnp.int32, (WIN, WIN), 0)
    col = lax.broadcasted_iota(jnp.int32, (WIN, WIN), 1)
    first = jnp.where((row == col + 32 * group) & (col < width), 1.0, 0.0).astype(BF)

    def some(i, _):
        rows = pl.ds(pl.multiple_of(i * 384, 384), 384)
        packed[rows, :WIN] = jnp.dot(wbuf[rows, :WIN], first, preferred_element_type=F32).astype(BF)
        packed[rows, WIN:] = jnp.dot(wbuf[rows, WIN:], pick, preferred_element_type=F32).astype(BF)
        return 0

    lax.fori_loop(0, 3, some, 0)


def project(h, packed, qk, vt, index):
    rows = pl.ds(pl.multiple_of(index * QT, QT), QT)
    acc = jnp.dot(h, packed[...], preferred_element_type=F32)
    qk[rows, :WIN] = (acc[:, :WIN] * SCALE).astype(BF)
    qk[rows, WIN:] = acc[:, WIN : 2 * WIN].astype(BF)
    values = acc[:, 640:1024].T
    one = jnp.where(lax.broadcasted_iota(jnp.int32, (8, QT), 0) == 0, 1.0, 0.0)
    for head in range(4):
        part = values[32 + HD * head : 32 + HD * head + HD, :]
        vt[head, :, rows] = jnp.concatenate([part, one], axis=0).astype(BF)


def load_window(w, wbuf, sems, group):
    copies = []
    for part in range(3):
        cols = pl.ds(pl.multiple_of(part * D + 256 * group, 128), WIN)
        copies.append(pltpu.make_async_copy(w.at[:, cols], wbuf.at[:, pl.ds(part * WIN, WIN)], sems.at[part]))
        copies[-1].start()
    return copies


def to_patches():
    row = lax.broadcasted_iota(jnp.int32, (512, 512), 0)
    col = lax.broadcasted_iota(jnp.int32, (512, 512), 1)
    return jnp.where(col == (row % 32) * 16 + row // 32, 1.0, 0.0).astype(BF)


def to_frames():
    row = lax.broadcasted_iota(jnp.int32, (256, 256), 0)
    col = lax.broadcasted_iota(jnp.int32, (256, 256), 1)
    return jnp.where(col == (row % 8) * 32 + row // 8, 1.0, 0.0).astype(BF)


def fused_kernel(
    tok_hbm, mod_s, mod_t, w_qkv_s, w_out_s, w_qkv_t, w_out_t, out,
    tok, hs, zbuf, full, wbuf, packed, qk, vt, s0, s1, m0, m1, held, held_top, awide, att, att_t, tok_t, wo_s, wq, wo,
    flat, mid, hp, qkv, mixed_all, done,
    tok_sem, w_sem, z_sem, full_sem, gather_send, tok_send, tok_recv, att_send, att_recv, home_send, home_recv, group_sem,
):
    frame, patch, zh, x, core = place()
    group = (x % 2) * 2 + core
    at = zh * 2 + x // 2
    zpatch = (1 - zh) * 8 + x * 2 + core
    sibling = (frame, patch + 1 - 2 * core)
    zdev = (frame, zpatch)

    barrier = pltpu.get_barrier_semaphore()

    for d in range(1, 16):
        pl.semaphore_signal(barrier, inc=1, device_id=(frame, (patch + d) % 16), device_id_type=MESH)
    for d in range(1, 8):
        pl.semaphore_signal(barrier, inc=1, device_id=((frame + d) % 8, patch), device_id_type=MESH)
    load_tok = pltpu.make_async_copy(tok_hbm, tok, tok_sem)
    load_tok.start()
    windows = load_window(w_qkv_s, wbuf, w_sem, group)
    loads = [
        pltpu.make_async_copy(src, dst, w_sem.at[3 + i])
        for i, (src, dst) in enumerate([(w_out_s, wo_s), (w_qkv_t, wq), (w_out_t, wo)])
    ]
    for load in loads:
        load.start()

    def norm(f):
        hs[f] = modulate(tok[f].astype(F32), mod_s)

    load_tok.wait()
    norm(2 * (1 - zh))
    norm(2 * (1 - zh) + 1)
    pl.semaphore_wait(barrier, 22)
    parts = (pl.ds(0, 64), pl.ds(64, 64))
    for r, part in enumerate(parts):
        for j in range(2):
            remote(hs.at[2 * (1 - zh) + j, part], zbuf.at[j, part], gather_send, z_sem.at[r, j], zdev).start()
    for d in range(1, 8):
        pl.semaphore_signal(group_sem, inc=1, device_id=((frame + d) % 8, patch), device_id_type=MESH)
    norm(2 * zh)
    norm(2 * zh + 1)

    for r, part in enumerate(parts):
        for d in (2, 1, 3):
            xd = (x + d) % 4
            device = (frame, zh * 8 + xd * 2 + core)
            src, dst = hs.at[2 * zh + xd // 2, part], full.at[patch, part]
            remote(src, dst, gather_send, full_sem.at[r, patch], device).start()
        src, dst = hs.at[2 * zh + x // 2, part], full.at[patch, part]
        pltpu.make_async_copy(src, dst, full_sem.at[r, patch]).start()
    awide[...] = jnp.zeros_like(awide)
    for window in windows:
        window.wait()
    pack_weights(wbuf, packed, group)

    def arrived(source, r):
        spot = full.at[source, parts[r]]
        pltpu.make_async_copy(spot, spot, full_sem.at[r, source]).wait()

    def chip_of(k):
        return ((zh + k // 4) % 2) * 4 + (x + 2 * (k % 4) - 3 * (k % 4 // 2)) % 4

    def relay(k, _):
        source = chip_of(k) * 2 + core
        for r in range(2):
            arrived(source, r)
            spot = full.at[source, parts[r]]
            remote(spot, spot, gather_send, full_sem.at[r, source], sibling).start()
        return 0

    def chip(k, _):
        index = chip_of(k)
        for r in range(2):
            arrived(index * 2 + 1 - core, r)
        h = full[pl.ds(index * 2, 2)].reshape(QT, D)
        project(h, packed, qk, vt, index)
        return 0

    def token_out(f):
        remote(tok.at[:, rows16(f), :], tok_t.at[frame], tok_send, tok_recv, (f, patch)).start()

    for d in (2, 4, 6):
        token_out((frame + d) % 8)
    pltpu.make_async_copy(tok.at[:, rows16(frame), :], tok_t.at[frame], tok_recv).start()
    relay(0, 0)
    chip(0, 0)
    for r, part in enumerate(parts):
        for j in range(2):
            src, dst = zbuf.at[j, part], full.at[zpatch, part]
            pltpu.make_async_copy(src, src, z_sem.at[r, j]).wait()
            for n in range(2):
                xd = 2 * j + n

                @pl.when(xd != x)
                def _():
                    device = (frame, zh * 8 + xd * 2 + core)
                    remote(src, dst, gather_send, full_sem.at[r, zpatch], device).start()

                @pl.when(xd == x)
                def _():
                    pltpu.make_async_copy(src, dst, full_sem.at[r, zpatch]).start()

    lax.fori_loop(1, 5, relay, 0)
    for d in (1, 3, 5, 7):
        token_out((frame + d) % 8)
    lax.fori_loop(1, 5, chip, 0)


    scores, tops = (s0, s1), (m0, m1)

    def score(head, tile, slot, chunks):
        base = (head // 2) * 128
        rows = pl.ds(pl.multiple_of(tile * QT, QT), QT)
        keep = head_lanes((QT, 256), head)
        query = jnp.where(keep, qk[rows, base : base + 256], jnp.zeros((), BF))
        top = None
        for c, at_chunk in enumerate(chunks):
            keys = qk[pl.ds(pl.multiple_of(at_chunk * KC, KC), KC), WIN + base : WIN + base + 256]
            part = lax.dot_general(keys, query, (((1,), (1,)), ((), ())), preferred_element_type=F32)
            scores[slot][c * KC : (c + 1) * KC, :] = part
            part = jnp.max(part.reshape(KC // 8, 8, QT), axis=0)
            top = part if top is None else jnp.maximum(top, part)
        tops[slot][...] = jnp.broadcast_to(jnp.max(top, axis=0, keepdims=True), (8, QT))

    def sums(head, slot, chunks, top):
        acc = None
        for c, at_chunk in enumerate(chunks):
            probs = jnp.exp2(scores[slot][c * KC : (c + 1) * KC, :] - top).astype(BF)
            values = vt[head, :, pl.ds(pl.multiple_of(at_chunk * KC, KC), KC)]
            part = jnp.dot(values, probs, preferred_element_type=F32)
            acc = part if acc is None else acc + part
        return acc

    def keep_head(head, acc):
        awide[pl.ds(pl.multiple_of(32 * group + HD * head, 8), HD), :] = acc[:HD] / acc[HD : HD + 1]

    def send_tile(tile):
        att[pl.ds(pl.multiple_of(tile * QT, QT), QT), :] = awide[...].T.astype(BF)

        def go(n, _):
            f, p = (frame + n // 2) % 8, tile * 2 + n % 2
            src, dst = att.at[rows16(p * 8 + f), :], att_t.at[group, frame, at]
            mine = (f == frame) & (p == patch)

            @pl.when(jnp.logical_not(mine))
            def _():
                remote(src, dst, att_send, att_recv.at[zh], (f, p)).start()

            @pl.when(mine)
            def _():
                pltpu.make_async_copy(src, dst, att_recv.at[zh]).start()

            return 0

        lax.fori_loop(0, 16, go, 0)

    near = [zh * 4 + c for c in range(4)] + [(1 - zh) * 4 + x]
    far = [(1 - zh) * 4 + (x + d) % 4 for d in (2, 1, 3)]
    score(0, zh * 4 + x, 0, near)

    def first_part(i, _):
        for head in range(4):
            ahead = (x + i) % 4 if head < 3 else (x + i + 1) % 4
            score((head + 1) % 4, zh * 4 + ahead, (head + 1) % 2, near)
            slot = head % 2
            held[(x + i) % 4, head] = sums(head, slot, near, tops[slot][0:1, :])
            held_top[(x + i) % 4, head] = tops[slot][...]
        return 0

    lax.fori_loop(0, 4, first_part, 0)
    lax.fori_loop(5, 8, relay, 0)
    lax.fori_loop(5, 8, chip, 0)
    pl.semaphore_wait(group_sem, 7)

    def far_tile(i):
        return (1 - zh) * 4 + (x + 2 * (i % 4) - 3 * (i % 4 // 2)) % 4

    def own_tile(i):
        return zh * 4 + (x + 1 + 2 * (i % 4) - 3 * (i % 4 // 2)) % 4

    score(0, own_tile(0), 0, far)

    def two_tiles(i, _):
        for head in range(4):
            if head < 3:
                score(head + 1, own_tile(i), (head + 1) % 2, far)
            else:
                score(0, far_tile(i), 0, range(8))
            slot = head % 2
            spot = own_tile(i) - zh * 4
            before = held_top[spot, head, 0:1, :]
            top = jnp.maximum(tops[slot][0:1, :], before)
            acc = held[spot, head] * jnp.exp2(before - top)
            keep_head(head, acc + sums(head, slot, far, top))
        send_tile(own_tile(i))
        for head in range(4):
            if head < 3:
                score(head + 1, far_tile(i), (head + 1) % 2, range(8))
            else:
                score(0, own_tile(i + 1), 0, far)
            slot = head % 2
            keep_head(head, sums(head, slot, range(8), tops[slot][0:1, :]))
        send_tile(far_tile(i))
        return 0

    lax.fori_loop(0, 4, two_tiles, 0)

    for load in loads:
        load.wait()
    pltpu.make_async_copy(tok_t, tok_t, tok_recv).wait()

    def finish_mid(n, _):
        z = (zh + n) % 2
        came = att_t.at[:, :, pl.ds(2 * z, 2)]
        pltpu.make_async_copy(came, came, att_recv.at[z]).wait()
        frames = pl.ds(2 * z, 2)
        tiles = []
        for tile in range(9):
            g, rest = min(tile // 2, 3), tile - 2 * min(tile // 2, 3)
            part = att_t[g, :, frames, :, rest * 128 : rest * 128 + 128].reshape(256, 128)
            if rest == 0 and g > 0:
                part = part + att_t[g - 1, :, frames, :, 256:384].reshape(256, 128)
            tiles.append(part)
        proj = jnp.dot(jnp.concatenate(tiles, axis=1), wo_s[...], preferred_element_type=F32)
        values = tok_t[:, frames].reshape(256, D).astype(F32)
        values = (values + mod_s[2:3, :] * proj).astype(BF).astype(F32)
        mid[:, frames] = values.reshape(8, 2, 16, D)
        flat[:, frames] = modulate(values, mod_t).reshape(8, 2, 16, D)
        return 0

    lax.fori_loop(0, 2, finish_mid, 0)
    hp[...] = jnp.dot(to_patches(), flat[...].reshape(512, D), preferred_element_type=F32).astype(BF)

    row = lax.broadcasted_iota(jnp.int32, (128, 128), 0)
    col = lax.broadcasted_iota(jnp.int32, (128, 128), 1)
    same = row // 32 == col // 32
    lane = lax.broadcasted_iota(jnp.int32, (128, 256), 1)

    def four_patches(i, _):
        rows = pl.ds(pl.multiple_of(i * 128, 128), 128)
        tiles = [None] * 9
        for head in range(HEADS):
            tile = min(head * HD // 128, 7)
            base = tile * 128
            low = head * HD - base
            keep = (lane >= low) & (lane < low + HD)
            query = jnp.where(keep, qkv[rows, base : base + 256], jnp.zeros((), BF))
            keys = qkv[rows, D + base : D + base + 256]
            part = lax.dot_general(query, keys, (((1,), (1,)), ((), ())), preferred_element_type=F32)
            part = jnp.where(same, part, -1e30)
            expo = jnp.exp2(part - jnp.max(part, axis=-1, keepdims=True))
            probs = (expo / jnp.sum(expo, axis=-1, keepdims=True)).astype(BF)
            mixed = jnp.dot(probs, qkv[rows, 2 * D + base : 2 * D + base + 256], preferred_element_type=F32)
            for n in range(2):
                piece = mixed[:, n * 128 : n * 128 + 128]
                old = tiles[tile + n]
                tiles[tile + n] = piece if old is None else jnp.where(keep[:, n * 128 : n * 128 + 128], piece, old)
        for n in range(9):
            mixed_all[rows, n * 128 : n * 128 + 128] = tiles[n].astype(BF)
        return 0

    def eight_patches(n, _):
        rows = pl.ds(pl.multiple_of(n * 256, 256), 256)
        for cols in (slice(0, 768), slice(768, 1152), slice(1152, 1920), slice(1920, 2688), slice(2688, 3456)):
            acc = jnp.dot(hp[rows, :], wq[:, cols], preferred_element_type=F32)
            if cols.stop <= D:
                acc = acc * SCALE
            qkv[:, cols] = acc.astype(BF)
        lax.fori_loop(0, 2, four_patches, 0)
        ordered = jnp.dot(to_frames(), mixed_all[...], preferred_element_type=F32).astype(BF)
        proj = jnp.dot(ordered, wo[...], preferred_element_type=F32)
        values = mid[:, :, pl.ds(pl.multiple_of(n * 8, 8), 8), :].reshape(256, D)
        values = (values + mod_t[2:3, :] * proj).astype(BF)
        done[n] = values.reshape(8, 32, D)

        def go(d, _):
            f = (frame + d) % 8
            remote(done.at[n, f], out.at[n, frame], home_send, home_recv, (f, patch)).start()
            return 0

        lax.fori_loop(1, 8, go, 0)
        pltpu.make_async_copy(done.at[n, frame], out.at[n, frame], home_recv).start()
        return 0

    lax.fori_loop(0, 2, eight_patches, 0)
    pltpu.make_async_copy(full, full, gather_send).wait()
    pltpu.make_async_copy(tok_t.at[pl.ds(0, 7)], tok_t.at[pl.ds(0, 7)], tok_send).wait()
    pltpu.make_async_copy(att.at[pl.ds(0, 2032), :], att.at[pl.ds(0, 2032), :], att_send).wait()
    for n in range(2):
        pltpu.make_async_copy(done.at[n, pl.ds(0, 7)], done.at[n, pl.ds(0, 7)], home_send).wait()
    pltpu.make_async_copy(out, out, home_recv).wait()


def shards(tokens, w_qkv_s, w_out_s, mod_s, w_qkv_t, w_out_t, mod_t):
    dma = pltpu.SemaphoreType.DMA
    parts = pl.pallas_call(
        fused_kernel,
        name="blocks",
        out_shape=jax.ShapeDtypeStruct((2, 8, 32, D), BF),
        in_specs=[ANY, VMEM, VMEM, ANY, ANY, ANY, ANY],
        out_specs=ANY,
        scratch_shapes=[
            pltpu.VMEM((4, 128, D), BF),
            pltpu.VMEM((4, 128, D), BF),
            pltpu.VMEM((2, 128, D), BF),
            pltpu.VMEM((16, 128, D), BF),
            pltpu.VMEM((D, 3 * WIN), BF),
            pltpu.VMEM((D, 1024), BF),
            pltpu.VMEM((ROWS, 2 * WIN), BF),
            pltpu.VMEM((4, 80, ROWS), BF),
            pltpu.VMEM((ROWS, QT), F32),
            pltpu.VMEM((ROWS, QT), F32),
            pltpu.VMEM((8, QT), F32),
            pltpu.VMEM((8, QT), F32),
            pltpu.VMEM((4, 4, 80, QT), F32),
            pltpu.VMEM((4, 4, 8, QT), F32),
            pltpu.VMEM((WIN, QT), F32),
            pltpu.VMEM((ROWS, WIN), BF),
            pltpu.VMEM((4, 8, 4, 16, WIN), BF),
            pltpu.VMEM((8, 4, 16, D), BF),
            pltpu.VMEM((D, D), BF),
            pltpu.VMEM((D, 3 * D), BF),
            pltpu.VMEM((D, D), BF),
            pltpu.VMEM((8, 4, 16, D), BF),
            pltpu.VMEM((8, 4, 16, D), F32),
            pltpu.VMEM((512, D), BF),
            pltpu.VMEM((256, 3 * D), BF),
            pltpu.VMEM((256, D), BF),
            pltpu.VMEM((2, 8, 32, D), BF),
            dma,
            dma((6,)),
            dma((2, 2)),
            dma((2, 16)),
            dma,
            dma,
            dma,
            dma,
            dma((2,)),
            dma,
            dma,
            pltpu.SemaphoreType.REGULAR,
        ],
        compiler_params=params(1),
    )(tokens, mod_s, mod_t, w_qkv_s, w_out_s, w_qkv_t, w_out_t)
    return parts.reshape(2, 8, 4, 8, D).transpose(2, 1, 0, 3, 4).reshape(4, 128, D)


def solution(mesh):
    return jax.shard_map(
        shards,
        mesh=mesh,
        in_specs=(P("frame", "patch", None), P(), P(), P(), P(), P(), P()),
        out_specs=P("frame", "patch", None),
        check_vma=False,
    )
```

```python
import functools

import jax
import jax.numpy as jnp
from jax import lax
from jax.experimental import pallas as pl
from jax.experimental.pallas import tpu as pltpu
from jax.sharding import PartitionSpec as P

HEADS = 16
HD = 72
D = 1152
WIN = 384
ROWS = 2048
QT = 256
KC = 256
SCALE = HD ** (-0.5) * 1.4426950408889634
MESH = pl.DeviceIdType.MESH
VMEM = pl.BlockSpec(memory_space=pltpu.VMEM)
ANY = pl.BlockSpec(memory_space=pl.ANY)
BF = jnp.bfloat16
F32 = jnp.float32


def params(collective_id=None):
    return pltpu.CompilerParams(
        collective_id=collective_id,
        has_side_effects=collective_id is not None,
        vmem_limit_bytes=56 * 2**20,
    )


def remote(src, dst, send_sem, recv_sem, device):
    return pltpu.make_async_remote_copy(
        src_ref=src, dst_ref=dst, send_sem=send_sem, recv_sem=recv_sem, device_id=device, device_id_type=MESH
    )


def modulate(values, mod_ref):
    mean = jnp.mean(values, axis=-1, keepdims=True)
    centered = values - mean
    var = jnp.mean(centered * centered, axis=-1, keepdims=True)
    return (centered * lax.rsqrt(var + 1e-06) * (1.0 + mod_ref[1:2, :]) + mod_ref[0:1, :]).astype(BF)


def place():
    frame, patch = lax.axis_index("frame"), lax.axis_index("patch")
    return frame, patch, patch // 8, (patch // 2) % 4, patch % 2


def rows16(index):
    return pl.ds(pl.multiple_of(index * 16, 16), 16)


def head_lanes(shape, head):
    lane = lax.broadcasted_iota(jnp.int32, shape, 1) + (head // 2) * 128
    return (lane >= HD * head) & (lane < HD * head + HD)


def pack_weights(wbuf, packed, group):
    row = lax.broadcasted_iota(jnp.int32, (2 * WIN, 640), 0)
    col = lax.broadcasted_iota(jnp.int32, (2 * WIN, 640), 1)
    width = 4 * HD
    target = jnp.where(col < width, col, col + (WIN - width)) + 32 * group
    pick = jnp.where((row == target) & (col < 2 * width), 1.0, 0.0).astype(BF)
    row = lax.broadcasted_iota(jnp.int32, (WIN, WIN), 0)
    col = lax.broadcasted_iota(jnp.int32, (WIN, WIN), 1)
    first = jnp.where((row == col + 32 * group) & (col < width), 1.0, 0.0).astype(BF)

    def some(i, _):
        rows = pl.ds(pl.multiple_of(i * 384, 384), 384)
        packed[rows, :WIN] = jnp.dot(wbuf[rows, :WIN], first, preferred_element_type=F32).astype(BF)
        packed[rows, WIN:] = jnp.dot(wbuf[rows, WIN:], pick, preferred_element_type=F32).astype(BF)
        return 0

    lax.fori_loop(0, 3, some, 0)


def project(h, packed, qk, vt, index):
    rows = pl.ds(pl.multiple_of(index * QT, QT), QT)
    acc = jnp.dot(h, packed[...], preferred_element_type=F32)
    qk[rows, :WIN] = (acc[:, :WIN] * SCALE).astype(BF)
    qk[rows, WIN:] = acc[:, WIN : 2 * WIN].astype(BF)
    values = acc[:, 640:1024].T
    one = jnp.where(lax.broadcasted_iota(jnp.int32, (8, QT), 0) == 0, 1.0, 0.0)
    for head in range(4):
        part = values[32 + HD * head : 32 + HD * head + HD, :]
        vt[head, :, rows] = jnp.concatenate([part, one], axis=0).astype(BF)


def load_window(w, wbuf, sems, group):
    copies = []
    for part in range(3):
        cols = pl.ds(pl.multiple_of(part * D + 256 * group, 128), WIN)
        copies.append(pltpu.make_async_copy(w.at[:, cols], wbuf.at[:, pl.ds(part * WIN, WIN)], sems.at[part]))
        copies[-1].start()
    return copies


def to_patches():
    row = lax.broadcasted_iota(jnp.int32, (512, 512), 0)
    col = lax.broadcasted_iota(jnp.int32, (512, 512), 1)
    return jnp.where(col == (row % 32) * 16 + row // 32, 1.0, 0.0).astype(BF)


def to_frames():
    row = lax.broadcasted_iota(jnp.int32, (256, 256), 0)
    col = lax.broadcasted_iota(jnp.int32, (256, 256), 1)
    return jnp.where(col == (row % 8) * 32 + row // 8, 1.0, 0.0).astype(BF)


def fused_kernel(
    tok_hbm, mod_s, mod_t, w_qkv_s, w_out_s, w_qkv_t, w_out_t, out,
    tok, hs, zbuf, full, wbuf, packed, qk, vt, s0, s1, m0, m1, held, held_top, awide, att, att_t, tok_t, wo_s, wq, wo,
    flat, mid, hp, qkv, mixed_all, done,
    tok_sem, w_sem, z_sem, full_sem, gather_send, tok_send, tok_recv, att_send, att_recv, home_send, home_recv, group_sem,
):
    frame, patch, zh, x, core = place()
    group = (x % 2) * 2 + core
    at = zh * 2 + x // 2
    zpatch = (1 - zh) * 8 + x * 2 + core
    sibling = (frame, patch + 1 - 2 * core)
    zdev = (frame, zpatch)

    barrier = pltpu.get_barrier_semaphore()

    for d in range(1, 16):
        pl.semaphore_signal(barrier, inc=1, device_id=(frame, (patch + d) % 16), device_id_type=MESH)
    for d in range(1, 8):
        pl.semaphore_signal(barrier, inc=1, device_id=((frame + d) % 8, patch), device_id_type=MESH)
    load_tok = pltpu.make_async_copy(tok_hbm, tok, tok_sem)
    load_tok.start()
    windows = load_window(w_qkv_s, wbuf, w_sem, group)
    loads = [
        pltpu.make_async_copy(src, dst, w_sem.at[3 + i])
        for i, (src, dst) in enumerate([(w_out_s, wo_s), (w_qkv_t, wq), (w_out_t, wo)])
    ]
    for load in loads:
        load.start()

    def norm(f):
        hs[f] = modulate(tok[f].astype(F32), mod_s)

    load_tok.wait()
    norm(2 * (1 - zh))
    norm(2 * (1 - zh) + 1)
    norm(2 * zh)
    norm(2 * zh + 1)
    pl.semaphore_wait(barrier, 22)
    parts = (pl.ds(0, 64), pl.ds(64, 64))
    for r, part in enumerate(parts):
        for j in range(2):
            remote(hs.at[2 * (1 - zh) + j, part], zbuf.at[j, part], gather_send, z_sem.at[r, j], zdev).start()
    for d in range(1, 8):
        pl.semaphore_signal(group_sem, inc=1, device_id=((frame + d) % 8, patch), device_id_type=MESH)

    for r, part in enumerate(parts):
        for d in (2, 1, 3):
            xd = (x + d) % 4
            device = (frame, zh * 8 + xd * 2 + core)
            src, dst = hs.at[2 * zh + xd // 2, part], full.at[patch, part]
            remote(src, dst, gather_send, full_sem.at[r, patch], device).start()
        src, dst = hs.at[2 * zh + x // 2, part], full.at[patch, part]
        pltpu.make_async_copy(src, dst, full_sem.at[r, patch]).start()
    awide[...] = jnp.zeros_like(awide)
    for window in windows:
        window.wait()
    pack_weights(wbuf, packed, group)

    def arrived(source, r):
        spot = full.at[source, parts[r]]
        pltpu.make_async_copy(spot, spot, full_sem.at[r, source]).wait()

    def chip_of(k):
        return ((zh + k // 4) % 2) * 4 + (x + 2 * (k % 4) - 3 * (k % 4 // 2)) % 4

    def relay(k, _):
        source = chip_of(k) * 2 + core
        for r in range(2):
            arrived(source, r)
            spot = full.at[source, parts[r]]
            remote(spot, spot, gather_send, full_sem.at[r, source], sibling).start()
        return 0

    def chip(k, _):
        index = chip_of(k)
        for r in range(2):
            arrived(index * 2 + 1 - core, r)
        h = full[pl.ds(index * 2, 2)].reshape(QT, D)
        project(h, packed, qk, vt, index)
        return 0

    def token_out(f):
        remote(tok.at[:, rows16(f), :], tok_t.at[frame], tok_send, tok_recv, (f, patch)).start()

    for d in (2, 4, 6):
        token_out((frame + d) % 8)
    pltpu.make_async_copy(tok.at[:, rows16(frame), :], tok_t.at[frame], tok_recv).start()
    relay(0, 0)
    chip(0, 0)
    for r, part in enumerate(parts):
        for j in range(2):
            src, dst = zbuf.at[j, part], full.at[zpatch, part]
            pltpu.make_async_copy(src, src, z_sem.at[r, j]).wait()
            for n in range(2):
                xd = 2 * j + n

                @pl.when(xd != x)
                def _():
                    device = (frame, zh * 8 + xd * 2 + core)
                    remote(src, dst, gather_send, full_sem.at[r, zpatch], device).start()

                @pl.when(xd == x)
                def _():
                    pltpu.make_async_copy(src, dst, full_sem.at[r, zpatch]).start()

    lax.fori_loop(1, 5, relay, 0)
    for d in (1, 3, 5, 7):
        token_out((frame + d) % 8)
    lax.fori_loop(1, 5, chip, 0)


    scores, tops = (s0, s1), (m0, m1)

    def score(head, tile, slot, chunks):
        base = (head // 2) * 128
        rows = pl.ds(pl.multiple_of(tile * QT, QT), QT)
        keep = head_lanes((QT, 256), head)
        query = jnp.where(keep, qk[rows, base : base + 256], jnp.zeros((), BF))
        top = None
        for c, at_chunk in enumerate(chunks):
            keys = qk[pl.ds(pl.multiple_of(at_chunk * KC, KC), KC), WIN + base : WIN + base + 256]
            part = lax.dot_general(keys, query, (((1,), (1,)), ((), ())), preferred_element_type=F32)
            scores[slot][c * KC : (c + 1) * KC, :] = part
            part = jnp.max(part.reshape(KC // 8, 8, QT), axis=0)
            top = part if top is None else jnp.maximum(top, part)
        tops[slot][...] = jnp.broadcast_to(jnp.max(top, axis=0, keepdims=True), (8, QT))

    def sums(head, slot, chunks, top):
        acc = None
        for c, at_chunk in enumerate(chunks):
            probs = jnp.exp2(scores[slot][c * KC : (c + 1) * KC, :] - top).astype(BF)
            values = vt[head, :, pl.ds(pl.multiple_of(at_chunk * KC, KC), KC)]
            part = jnp.dot(values, probs, preferred_element_type=F32)
            acc = part if acc is None else acc + part
        return acc

    def keep_head(head, acc):
        awide[pl.ds(pl.multiple_of(32 * group + HD * head, 8), HD), :] = acc[:HD] / acc[HD : HD + 1]

    def send_tile(tile):
        att[pl.ds(pl.multiple_of(tile * QT, QT), QT), :] = awide[...].T.astype(BF)

        def go(n, _):
            f, p = (frame + n // 2) % 8, tile * 2 + n % 2
            src, dst = att.at[rows16(p * 8 + f), :], att_t.at[group, frame, at]
            mine = (f == frame) & (p == patch)

            @pl.when(jnp.logical_not(mine))
            def _():
                remote(src, dst, att_send, att_recv.at[zh], (f, p)).start()

            @pl.when(mine)
            def _():
                pltpu.make_async_copy(src, dst, att_recv.at[zh]).start()

            return 0

        lax.fori_loop(0, 16, go, 0)

    near = [zh * 4 + c for c in range(4)] + [(1 - zh) * 4 + x]
    far = [(1 - zh) * 4 + (x + d) % 4 for d in (2, 1, 3)]
    score(0, zh * 4 + x, 0, near)

    def first_part(i, _):
        for head in range(4):
            ahead = (x + i) % 4 if head < 3 else (x + i + 1) % 4
            score((head + 1) % 4, zh * 4 + ahead, (head + 1) % 2, near)
            slot = head % 2
            held[(x + i) % 4, head] = sums(head, slot, near, tops[slot][0:1, :])
            held_top[(x + i) % 4, head] = tops[slot][...]
        return 0

    lax.fori_loop(0, 4, first_part, 0)
    lax.fori_loop(5, 8, relay, 0)
    lax.fori_loop(5, 8, chip, 0)
    pl.semaphore_wait(group_sem, 7)

    def far_tile(i):
        return (1 - zh) * 4 + (x + 2 * (i % 4) - 3 * (i % 4 // 2)) % 4

    def own_tile(i):
        return zh * 4 + (x + 1 + 2 * (i % 4) - 3 * (i % 4 // 2)) % 4

    score(0, own_tile(0), 0, far)

    def two_tiles(i, _):
        for head in range(4):
            if head < 3:
                score(head + 1, own_tile(i), (head + 1) % 2, far)
            else:
                score(0, far_tile(i), 0, range(8))
            slot = head % 2
            spot = own_tile(i) - zh * 4
            before = held_top[spot, head, 0:1, :]
            top = jnp.maximum(tops[slot][0:1, :], before)
            acc = held[spot, head] * jnp.exp2(before - top)
            keep_head(head, acc + sums(head, slot, far, top))
        send_tile(own_tile(i))
        for head in range(4):
            if head < 3:
                score(head + 1, far_tile(i), (head + 1) % 2, range(8))
            else:
                score(0, own_tile(i + 1), 0, far)
            slot = head % 2
            keep_head(head, sums(head, slot, range(8), tops[slot][0:1, :]))
        send_tile(far_tile(i))
        return 0

    lax.fori_loop(0, 4, two_tiles, 0)

    for load in loads:
        load.wait()
    pltpu.make_async_copy(tok_t, tok_t, tok_recv).wait()

    def finish_mid(n, _):
        z = (zh + n) % 2
        came = att_t.at[:, :, pl.ds(2 * z, 2)]
        pltpu.make_async_copy(came, came, att_recv.at[z]).wait()
        frames = pl.ds(2 * z, 2)
        tiles = []
        for tile in range(9):
            g, rest = min(tile // 2, 3), tile - 2 * min(tile // 2, 3)
            part = att_t[g, :, frames, :, rest * 128 : rest * 128 + 128].reshape(256, 128)
            if rest == 0 and g > 0:
                part = part + att_t[g - 1, :, frames, :, 256:384].reshape(256, 128)
            tiles.append(part)
        proj = jnp.dot(jnp.concatenate(tiles, axis=1), wo_s[...], preferred_element_type=F32)
        values = tok_t[:, frames].reshape(256, D).astype(F32)
        values = (values + mod_s[2:3, :] * proj).astype(BF).astype(F32)
        mid[:, frames] = values.reshape(8, 2, 16, D)
        flat[:, frames] = modulate(values, mod_t).reshape(8, 2, 16, D)
        return 0

    lax.fori_loop(0, 2, finish_mid, 0)
    hp[...] = jnp.dot(to_patches(), flat[...].reshape(512, D), preferred_element_type=F32).astype(BF)

    row = lax.broadcasted_iota(jnp.int32, (128, 128), 0)
    col = lax.broadcasted_iota(jnp.int32, (128, 128), 1)
    same = row // 32 == col // 32
    lane = lax.broadcasted_iota(jnp.int32, (128, 256), 1)

    def four_patches(i, _):
        rows = pl.ds(pl.multiple_of(i * 128, 128), 128)
        tiles = [None] * 9
        for head in range(HEADS):
            tile = min(head * HD // 128, 7)
            base = tile * 128
            low = head * HD - base
            keep = (lane >= low) & (lane < low + HD)
            query = jnp.where(keep, qkv[rows, base : base + 256], jnp.zeros((), BF))
            keys = qkv[rows, D + base : D + base + 256]
            part = lax.dot_general(query, keys, (((1,), (1,)), ((), ())), preferred_element_type=F32)
            part = jnp.where(same, part, -1e30)
            expo = jnp.exp2(part - jnp.max(part, axis=-1, keepdims=True))
            probs = (expo / jnp.sum(expo, axis=-1, keepdims=True)).astype(BF)
            mixed = jnp.dot(probs, qkv[rows, 2 * D + base : 2 * D + base + 256], preferred_element_type=F32)
            for n in range(2):
                piece = mixed[:, n * 128 : n * 128 + 128]
                old = tiles[tile + n]
                tiles[tile + n] = piece if old is None else jnp.where(keep[:, n * 128 : n * 128 + 128], piece, old)
        for n in range(9):
            mixed_all[rows, n * 128 : n * 128 + 128] = tiles[n].astype(BF)
        return 0

    def eight_patches(n, _):
        rows = pl.ds(pl.multiple_of(n * 256, 256), 256)
        for cols in (slice(0, 768), slice(768, 1152), slice(1152, 1920), slice(1920, 2688), slice(2688, 3456)):
            acc = jnp.dot(hp[rows, :], wq[:, cols], preferred_element_type=F32)
            if cols.stop <= D:
                acc = acc * SCALE
            qkv[:, cols] = acc.astype(BF)
        lax.fori_loop(0, 2, four_patches, 0)
        ordered = jnp.dot(to_frames(), mixed_all[...], preferred_element_type=F32).astype(BF)
        values = mid[:, :, pl.ds(pl.multiple_of(n * 8, 8), 8), :].reshape(256, D)
        for cols in (slice(0, 512), slice(512, 1152)):
            proj = jnp.dot(ordered, wo[:, cols], preferred_element_type=F32)
            block = (values[:, cols] + mod_t[2:3, cols] * proj).astype(BF)
            done[n, :, :, cols] = block.reshape(8, 32, cols.stop - cols.start)

            def go(d, _):
                f = (frame + d) % 8
                src, dst = done.at[n, f, :, cols], out.at[n, frame, :, cols]
                remote(src, dst, home_send, home_recv, (f, patch)).start()
                return 0

            lax.fori_loop(1, 8, go, 0)
            src, dst = done.at[n, frame, :, cols], out.at[n, frame, :, cols]
            pltpu.make_async_copy(src, dst, home_recv).start()
        return 0

    lax.fori_loop(0, 2, eight_patches, 0)
    pltpu.make_async_copy(full, full, gather_send).wait()
    pltpu.make_async_copy(tok_t.at[pl.ds(0, 7)], tok_t.at[pl.ds(0, 7)], tok_send).wait()
    pltpu.make_async_copy(att.at[pl.ds(0, 2032), :], att.at[pl.ds(0, 2032), :], att_send).wait()
    for n in range(2):
        pltpu.make_async_copy(done.at[n, pl.ds(0, 7)], done.at[n, pl.ds(0, 7)], home_send).wait()
    pltpu.make_async_copy(out, out, home_recv).wait()


def order_kernel(parts, out):
    for f in range(parts.shape[1]):
        first, second = (parts[n, f].astype(F32).reshape(4, 8, D) for n in range(2))
        out[:, f * 16 : f * 16 + 16, :] = jnp.concatenate([first, second], axis=1).astype(BF)


def shards(tokens, w_qkv_s, w_out_s, mod_s, w_qkv_t, w_out_t, mod_t):
    dma = pltpu.SemaphoreType.DMA
    parts = pl.pallas_call(
        fused_kernel,
        name="blocks",
        out_shape=jax.ShapeDtypeStruct((2, 8, 32, D), BF),
        in_specs=[ANY, VMEM, VMEM, ANY, ANY, ANY, ANY],
        out_specs=ANY,
        scratch_shapes=[
            pltpu.VMEM((4, 128, D), BF),
            pltpu.VMEM((4, 128, D), BF),
            pltpu.VMEM((2, 128, D), BF),
            pltpu.VMEM((16, 128, D), BF),
            pltpu.VMEM((D, 3 * WIN), BF),
            pltpu.VMEM((D, 1024), BF),
            pltpu.VMEM((ROWS, 2 * WIN), BF),
            pltpu.VMEM((4, 80, ROWS), BF),
            pltpu.VMEM((ROWS, QT), F32),
            pltpu.VMEM((ROWS, QT), F32),
            pltpu.VMEM((8, QT), F32),
            pltpu.VMEM((8, QT), F32),
            pltpu.VMEM((4, 4, 80, QT), F32),
            pltpu.VMEM((4, 4, 8, QT), F32),
            pltpu.VMEM((WIN, QT), F32),
            pltpu.VMEM((ROWS, WIN), BF),
            pltpu.VMEM((4, 8, 4, 16, WIN), BF),
            pltpu.VMEM((8, 4, 16, D), BF),
            pltpu.VMEM((D, D), BF),
            pltpu.VMEM((D, 3 * D), BF),
            pltpu.VMEM((D, D), BF),
            pltpu.VMEM((8, 4, 16, D), BF),
            pltpu.VMEM((8, 4, 16, D), F32),
            pltpu.VMEM((512, D), BF),
            pltpu.VMEM((256, 3 * D), BF),
            pltpu.VMEM((256, D), BF),
            pltpu.VMEM((2, 8, 32, D), BF),
            dma,
            dma((6,)),
            dma((2, 2)),
            dma((2, 16)),
            dma,
            dma,
            dma,
            dma,
            dma((2,)),
            dma,
            dma,
            pltpu.SemaphoreType.REGULAR,
        ],
        compiler_params=params(1),
    )(tokens, mod_s, mod_t, w_qkv_s, w_out_s, w_qkv_t, w_out_t)
    steps = 2
    return pl.pallas_call(
        order_kernel,
        name="order",
        grid=(steps,),
        out_shape=jax.ShapeDtypeStruct((4, 128, D), BF),
        in_specs=[pl.BlockSpec((2, 8 // steps, 32, D), lambda i: (0, i, 0, 0))],
        out_specs=pl.BlockSpec((4, 128 // steps, D), lambda i: (0, i, 0)),
        compiler_params=params(),
    )(parts)


def solution(mesh):
    return jax.shard_map(
        shards,
        mesh=mesh,
        in_specs=(P("frame", "patch", None), P(), P(), P(), P(), P(), P()),
        out_specs=P("frame", "patch", None),
        check_vma=False,
    )
```
